32 devices in a mesh: dp: 8 (over y, x, core), fsdp: 4 (over z).
Axes of the slice: x: 2, y: 2, z: 4, core: 2. Of those that a mesh axis runs over, the one named last changes fastest.
Arguments:
- latents: bfloat16 [32, 256, 16], P(('dp', 'fsdp')), may hold values from -6 to 6
- orders: int32 [32, 256], P(('dp', 'fsdp')), may hold values from 0 to 255, each once within a row
- mask_counts: int32 [32], P(('dp', 'fsdp')), may hold values from 1 to 256, 6144 in all
- noise: bfloat16 [6144, 64], P(('dp', 'fsdp')), may hold values from -6 to 6
- timesteps: int32 [6144, 4], P(('dp', 'fsdp')), may hold values from 0 to 999
- loss_weights: float32 [6144, 4], P(('dp', 'fsdp')), may hold values from 0.5 to 7.5
- block_weights: float32 [2, 768, 9216], P(None, ('dp', 'fsdp')), may hold values from -0.21875 to 0.21875
- block_gains: float32 [2, 2, 768], P(None, None, ('dp', 'fsdp')), may hold values from 0.5 to 1.5
- entry_table: float32 [656, 768], P(None, ('dp', 'fsdp')), may hold values from -1.5 to 1.5
- head_weights: float32 [2, 1024, 5120], P(None, ('dp', 'fsdp')), may hold values from -0.1875 to 0.1875
- head_biases: float32 [3, 5120], P(None, ('dp', 'fsdp')), may hold values from -1.5 to 1.5
- head_edges: float32 [4128, 1024], P(None, ('dp', 'fsdp')), may hold values from -1 to 1
- first_blocks: float32 [2, 768, 9216], P(None, ('dp', 'fsdp')), may hold values from -5.722046e-06 to 5.722046e-06
- first_gains: float32 [2, 2, 768], P(None, None, ('dp', 'fsdp')), may hold values from -1.5258789e-05 to 1.5258789e-05
- first_entry: float32 [656, 768], P(None, ('dp', 'fsdp')), may hold values from -5.722046e-06 to 5.722046e-06
- first_head: float32 [2, 1024, 5120], P(None, ('dp', 'fsdp')), may hold values from -5.722046e-06 to 5.722046e-06
- first_biases: float32 [3, 5120], P(None, ('dp', 'fsdp')), may hold values from -1.5258789e-05 to 1.5258789e-05
- first_edges: float32 [4128, 1024], P(None, ('dp', 'fsdp')), may hold values from -5.722046e-06 to 5.722046e-06
- second_blocks: float32 [2, 768, 9216], P(None, ('dp', 'fsdp')), may hold values from 1.3609678e-13 to 5.443871e-13
- second_gains: float32 [2, 2, 768], P(None, None, ('dp', 'fsdp')), may hold values from 1.2248711e-12 to 4.8994845e-12
- second_entry: float32 [656, 768], P(None, ('dp', 'fsdp')), may hold values from 1.3609678e-13 to 5.443871e-13
- second_head: float32 [2, 1024, 5120], P(None, ('dp', 'fsdp')), may hold values from 1.3609678e-13 to 5.443871e-13
- second_biases: float32 [3, 5120], P(None, ('dp', 'fsdp')), may hold values from 1.2248711e-12 to 4.8994845e-12
- second_edges: float32 [4128, 1024], P(None, ('dp', 'fsdp')), may hold values from 1.3609678e-13 to 5.443871e-13
Outputs:
- updated_blocks: float32 [2, 768, 9216], P(None, ('dp', 'fsdp'))
- updated_gains: float32 [2, 2, 768], P(None, None, ('dp', 'fsdp'))
- updated_entry: float32 [656, 768], P(None, ('dp', 'fsdp'))
- updated_head: float32 [2, 1024, 5120], P(None, ('dp', 'fsdp'))
- updated_biases: float32 [3, 5120], P(None, ('dp', 'fsdp'))
- updated_edges: float32 [4128, 1024], P(None, ('dp', 'fsdp'))
- momentum_blocks: float32 [2, 768, 9216], P(None, ('dp', 'fsdp'))
- momentum_gains: float32 [2, 2, 768], P(None, None, ('dp', 'fsdp'))
- momentum_entry: float32 [656, 768], P(None, ('dp', 'fsdp'))
- momentum_head: float32 [2, 1024, 5120], P(None, ('dp', 'fsdp'))
- momentum_biases: float32 [3, 5120], P(None, ('dp', 'fsdp'))
- momentum_edges: float32 [4128, 1024], P(None, ('dp', 'fsdp'))
- variance_blocks: float32 [2, 768, 9216], P(None, ('dp', 'fsdp'))
- variance_gains: float32 [2, 2, 768], P(None, None, ('dp', 'fsdp'))
- variance_entry: float32 [656, 768], P(None, ('dp', 'fsdp'))
- variance_head: float32 [2, 1024, 5120], P(None, ('dp', 'fsdp'))
- variance_biases: float32 [3, 5120], P(None, ('dp', 'fsdp'))
- variance_edges: float32 [4128, 1024], P(None, ('dp', 'fsdp'))
- loss_sum: float32 [], replicated
- weight_sum: float32 [], replicated
- grad_norm: float32 [], replicated
The draws below stay inside these ranges and needn't reach their ends.
Inputs may be any that keep to these rules, and one draw needn't show every extreme that they name: `orders`: each row is a permutation of 0 to 255. `mask_counts`: the counts of all images sum to 6144; the largest is 256.
All inputs are finite; a program needn't handle non-finite values. No bound on the sum of `mask_counts` on one device may be relied on, other than what follows from the above.
Results may differ from the reference program's by a relative error of at most 0.0088.
Values may be sent and summed in bfloat16 or wider, within the bound.
A program may use at most 512 MiB of HBM per device.

```python
import math
import jax
import jax.numpy as jnp
import numpy as np
from jax import lax

D = 768
HEADS = 12
HD = 64
FF = 3072
HW = 1024
CH = 16
FREQ = 256
LAT = 256
BUF = 64
LAYERS = 2
HB = 2
COPIES = 4
MASKED = 192
TSTEPS = 1000
ADAM_STEP = 5
SEQ = 320
IMAGES = 32
HEAD_DEV = 192
TOTAL_MASKED = 6144
PARAMS = 29390848
N_DP = 8
N_FSDP = 4


def draw_loss_weights(key, part):
    key = jax.random.fold_in(key, 11)
    rows = MASKED * IMAGES
    ramp = jnp.arange(rows, dtype=jnp.float32)[:, None] / rows
    base = jax.random.uniform(key, (rows, COPIES), jnp.float32, 0.5, 1.5)
    return base * (1.0 + 2.0 * ramp)


def draw_head_edges(key, part):
    key = jax.random.fold_in(key, 23)
    total_rows = D + 2 * CH + FREQ + 3 * HW
    row_ids = jnp.arange(total_rows)[:, None]
    row_scale = jnp.where(row_ids < D, D ** (-0.5), jnp.where(row_ids < D + CH, CH ** (-0.5), jnp.where(row_ids < D + 2 * CH, HW ** (-0.5), jnp.where(row_ids < D + 2 * CH + FREQ, FREQ ** (-0.5), HW ** (-0.5))))).astype(jnp.float32)
    values = jnp.clip(jax.random.normal(key, (total_rows, HW), jnp.float32), -4.0, 4.0)
    return values * row_scale


def place_ends(values, own_key, low, largest):
    longest = values.shape.index(max(values.shape))
    spots = []
    for shift in (0, 1):
        where = [jax.random.randint(jax.random.fold_in(own_key, axis), (), 0, length) for axis, length in enumerate(values.shape)]
        where[longest] = (where[longest] + shift) % values.shape[longest]
        spots.append(tuple(where))
    return values.at[spots[0]].set(low).at[spots[1]].set(largest)


def block_scale(stream_key, dims, shards, least, high):
    loudness, own = 1.0, jax.random.fold_in(stream_key, 6)
    for axis_at, shards_of in shards:
        draws = jnp.exp(jax.random.uniform(jax.random.fold_in(own, axis_at), (shards_of,), jnp.float32, least / len(shards), high / len(shards)))
        loudness = loudness * jnp.repeat(draws, dims[axis_at] // shards_of).reshape([-1 if axis == axis_at else 1 for axis in range(len(dims))])
    return loudness


def length_profile(count, total, reach, lean):
    weights = [(1 << 20) // math.isqrt(rank ** lean) + 1 for rank in range(2, count + 1)]
    rest, given = total - reach - (count - 1), [1] * (count - 1)
    while rest > 0:
        candidates = [i for i in range(count - 1) if given[i] < reach]
        mass, budget = sum([weights[i] for i in candidates]), rest
        for i in candidates:
            more = min(reach - given[i], max(1, budget * weights[i] // mass), rest)
            given[i] = given[i] + more
            rest = rest - more
    return np.array([reach] + given)


def ragged_sizes(rng, amount, total, bound, skew):
    if amount == 2:
        one = jax.random.randint(rng, (), max(1, total - bound), min(bound, total - 1) + 1)
        return jnp.stack([one, total - one])
    lengths = jnp.asarray(length_profile(amount, total, bound, skew), jnp.int32)
    couples = (amount - 1) // 2
    donor, sink = lengths[1:1 + 2 * couples:2], lengths[2:2 + 2 * couples:2]
    room = jnp.minimum(donor - 1, bound - sink)
    passed = jax.random.randint(jax.random.fold_in(rng, 1), (couples,), 0, 1 << 20) % (room + 1)
    lengths = lengths.at[1:1 + 2 * couples:2].set(donor - passed).at[2:2 + 2 * couples:2].set(sink + passed)
    return lengths[jax.random.permutation(jax.random.fold_in(rng, 2), amount)]


def gaussian(rng, dims, width, limit, cuts=(), kind=jnp.bfloat16):
    drawn = width * jax.random.normal(rng, dims, jnp.float32)
    if cuts:
        drawn = drawn * block_scale(rng, dims, cuts, -0.22, 0.18)
    return jnp.clip(drawn, -limit, limit).astype(kind)


def setup_inputs(seed: int = 0) -> dict:
    key_list = jax.random.split(jax.random.key(seed), 25)
    latents = gaussian(key_list[0], (IMAGES, LAT, CH), 1.0, 6.0, ((0, 32),))
    orders = jax.vmap(lambda own: jax.random.permutation(own, LAT))(jax.random.split(key_list[1], IMAGES)).reshape((IMAGES, LAT)).astype(jnp.int32)
    mask_counts = ragged_sizes(key_list[2], IMAGES, TOTAL_MASKED, LAT, 2).astype(jnp.int32)
    noise = gaussian(key_list[3], (TOTAL_MASKED, COPIES * CH), 1.0, 6.0, ((0, 32),))
    timesteps = place_ends(jax.random.randint(key_list[4], (TOTAL_MASKED, COPIES), 0, TSTEPS), jax.random.fold_in(key_list[4], 1), 0, TSTEPS - 1).astype(jnp.int32)
    loss_weights = draw_loss_weights(jax.random.fold_in(key_list[24], 71), 0)
    block_weights = gaussian(key_list[6], (LAYERS, D, 4 * D + 2 * FF), D ** -0.5, 0.21875, ((1, 32),), jnp.float32)
    block_gains = jnp.clip(1.0 + 0.1 * jax.random.normal(key_list[7], (LAYERS, 2, D), jnp.float32), 0.5, 1.5)
    entry_table = gaussian(key_list[8], (2 * SEQ + CH, D), 0.25, 1.5, ((1, 32),), jnp.float32)
    head_weights = gaussian(key_list[9], (HB, HW, 5 * HW), HW ** -0.5, 0.1875, ((1, 32),), jnp.float32)
    head_biases = gaussian(key_list[10], (HB + 1, 5 * HW), 0.3, 1.5, ((1, 32),), jnp.float32)
    head_edges = draw_head_edges(jax.random.fold_in(key_list[24], 71), 0)
    first_blocks = gaussian(key_list[12], (LAYERS, D, 4 * D + 2 * FF), (0.002 / PARAMS ** 0.5), 5.7220458984375e-06, ((1, 32),), jnp.float32)
    first_gains = gaussian(key_list[13], (LAYERS, 2, D), (0.006 / PARAMS ** 0.5), 1.52587890625e-05, ((2, 32),), jnp.float32)
    first_entry = gaussian(key_list[14], (2 * SEQ + CH, D), (0.002 / PARAMS ** 0.5), 5.7220458984375e-06, ((1, 32),), jnp.float32)
    first_head = gaussian(key_list[15], (HB, HW, 5 * HW), (0.002 / PARAMS ** 0.5), 5.7220458984375e-06, ((1, 32),), jnp.float32)
    first_biases = gaussian(key_list[16], (HB + 1, 5 * HW), (0.006 / PARAMS ** 0.5), 1.52587890625e-05, ((1, 32),), jnp.float32)
    first_edges = gaussian(key_list[17], (D + 2 * CH + FREQ + 3 * HW, HW), (0.002 / PARAMS ** 0.5), 5.7220458984375e-06, ((1, 32),), jnp.float32)
    second_blocks = jnp.clip(jnp.exp(math.log(5.443871265234379e-13) - 1.3862944 * jax.random.uniform(key_list[18], (LAYERS, D, 4 * D + 2 * FF), jnp.float32) ** block_scale(key_list[18], (LAYERS, D, 4 * D + 2 * FF), ((1, 32),), -0.2, 0.2)), 1.3609678163085948e-13, 5.443871265234379e-13)
    second_gains = jnp.clip(jnp.exp(math.log(4.899484463971593e-12) - 1.3862944 * jax.random.uniform(key_list[19], (LAYERS, 2, D), jnp.float32) ** block_scale(key_list[19], (LAYERS, 2, D), ((2, 32),), -0.2, 0.2)), 1.2248711159928982e-12, 4.899484463971593e-12)
    second_entry = jnp.clip(jnp.exp(math.log(5.443871265234379e-13) - 1.3862944 * jax.random.uniform(key_list[20], (2 * SEQ + CH, D), jnp.float32) ** block_scale(key_list[20], (2 * SEQ + CH, D), ((1, 32),), -0.2, 0.2)), 1.3609678163085948e-13, 5.443871265234379e-13)
    second_head = jnp.clip(jnp.exp(math.log(5.443871265234379e-13) - 1.3862944 * jax.random.uniform(key_list[21], (HB, HW, 5 * HW), jnp.float32) ** block_scale(key_list[21], (HB, HW, 5 * HW), ((1, 32),), -0.2, 0.2)), 1.3609678163085948e-13, 5.443871265234379e-13)
    second_biases = jnp.clip(jnp.exp(math.log(4.899484463971593e-12) - 1.3862944 * jax.random.uniform(key_list[22], (HB + 1, 5 * HW), jnp.float32) ** block_scale(key_list[22], (HB + 1, 5 * HW), ((1, 32),), -0.2, 0.2)), 1.2248711159928982e-12, 4.899484463971593e-12)
    second_edges = jnp.clip(jnp.exp(math.log(5.443871265234379e-13) - 1.3862944 * jax.random.uniform(key_list[23], (D + 2 * CH + FREQ + 3 * HW, HW), jnp.float32) ** block_scale(key_list[23], (D + 2 * CH + FREQ + 3 * HW, HW), ((1, 32),), -0.2, 0.2)), 1.3609678163085948e-13, 5.443871265234379e-13)
    return {"latents": latents, "orders": orders, "mask_counts": mask_counts, "noise": noise, "timesteps": timesteps, "loss_weights": loss_weights, "block_weights": block_weights, "block_gains": block_gains, "entry_table": entry_table, "head_weights": head_weights, "head_biases": head_biases, "head_edges": head_edges, "first_blocks": first_blocks, "first_gains": first_gains, "first_entry": first_entry, "first_head": first_head, "first_biases": first_biases, "first_edges": first_edges, "second_blocks": second_blocks, "second_gains": second_gains, "second_entry": second_entry, "second_head": second_head, "second_biases": second_biases, "second_edges": second_edges}


@jax.custom_vjp
def low(v):
    return lax.optimization_barrier(v.astype(jnp.bfloat16)).astype(jnp.float32)

@jax.custom_vjp
def low_back(v):
    return v

def low_keep(v):
    return (low(v), None)

def low_pass(kept, grad):
    return (grad,)

def back_keep(v):
    return (v, None)

def back_low(kept, grad):
    return (low(grad),)
low.defvjp(low_keep, low_pass)
low_back.defvjp(back_keep, back_low)
BETA_ONE = 0.5
BETA_TWO = 0.5
LEARN_RATE = 0.03
GAIN_RATE = 0.3
DECAY_RATE = 0.02
ADAM_EPS = 1e-08
CLIP_NORM = 0.002
NORM_EPS = 1e-06
HIGHEST = lax.Precision.HIGHEST

def matmul(left, right):
    return jnp.dot(left, right, precision=HIGHEST)

def normalize(values):
    centred = values - lax.optimization_barrier(jnp.mean(values, -1, keepdims=True))
    return centred * lax.rsqrt(lax.optimization_barrier(jnp.mean(centred * centred, -1, keepdims=True)) + NORM_EPS)

def block(hidden, weights, gain_rows, key_keep):
    normed = low(normalize(hidden) * gain_rows[0])
    packed = low_back(low(matmul(normed, weights[:, :3 * D])))
    query_rows = packed[:, :D].reshape(SEQ, HEADS, HD)
    key_rows = packed[:, D:2 * D].reshape(SEQ, HEADS, HD)
    value_rows = packed[:, 2 * D:].reshape(SEQ, HEADS, HD)
    scores = low_back(jnp.einsum('qhd,khd->hqk', query_rows, key_rows, precision=HIGHEST) * HD ** (-0.5))
    scores = jnp.where(key_keep[None, None, :] > 0, scores, -1e+30)
    attention = jax.nn.softmax(scores, -1)
    mixed_heads = jnp.einsum('hqk,khd->qhd', low(attention), value_rows, precision=HIGHEST).reshape(SEQ, D)
    mixed_heads = low_back(low(mixed_heads))
    hidden = hidden + low_back(matmul(mixed_heads, weights[:, 3 * D:4 * D]))
    second = low(normalize(hidden) * gain_rows[1])
    inner_rows = low_back(matmul(second, weights[:, 4 * D:4 * D + FF]))
    upper_rows = low(jax.nn.gelu(inner_rows))
    return hidden + low_back(matmul(upper_rows, weights[:, 4 * D + FF:].T))

def trunk(blocks, gain_sets, entry_rows, latent_rows, masked_rows):
    projected = low_back(matmul(latent_rows, entry_rows[2 * SEQ:]))
    hidden = entry_rows[:SEQ] + jnp.concatenate([jnp.zeros((BUF, D), jnp.float32), projected], 0)
    key_keep = jnp.concatenate([jnp.ones((BUF,), jnp.float32), 1.0 - masked_rows.astype(jnp.float32)])
    hidden = block(hidden, blocks[0], gain_sets[0], key_keep)
    hidden = hidden * key_keep[:, None] + entry_rows[SEQ:2 * SEQ]
    return block(hidden, blocks[1], gain_sets[1], jnp.ones((SEQ,), jnp.float32))

def head(blocks, biases, edge_rows, cond_rows, clean_rows, noise_rows, step_rows, weight_rows):
    base = D + 2 * CH
    extra = biases[HB]
    half_freq = FREQ // 2
    frequencies = jnp.exp(-math.log(10000.0) * jnp.arange(half_freq, dtype=jnp.float32) / half_freq)
    step_times = step_rows.astype(jnp.float32)
    angles = step_times.reshape(-1)[:, None] * frequencies
    time_embed = low(jnp.concatenate([jnp.cos(angles), jnp.sin(angles)], -1))
    time_inner = low_back(matmul(time_embed, edge_rows[base:base + FREQ]) + extra[:HW])
    time_vector = low_back(matmul(low(jax.nn.silu(time_inner)), edge_rows[base + FREQ:base + FREQ + HW]) + extra[HW:2 * HW])
    projected = low_back(matmul(cond_rows, edge_rows[:D]))
    conditioning = (projected[:, None, :] + time_vector.reshape(-1, COPIES, HW)).reshape(-1, HW)
    silu_cond = low(jax.nn.silu(conditioning))
    phase_angle = (step_times / TSTEPS + 0.008) / 1.008 * (math.pi / 2)
    keep_part = jnp.cos(phase_angle)[..., None]
    noise_part = jnp.sin(phase_angle)[..., None]
    fresh_noise = noise_rows.reshape(-1, COPIES, CH)
    clean_copies = clean_rows[:, None, :]
    noisy_rows = low((keep_part * clean_copies + noise_part * fresh_noise).reshape(-1, CH))
    target = (keep_part * fresh_noise - noise_part * clean_copies).reshape(-1, CH)
    stream = low_back(matmul(noisy_rows, edge_rows[D:D + CH]) + extra[4 * HW:])
    for block_number in range(HB):
        modulation = low_back(matmul(silu_cond, blocks[block_number, :, :3 * HW]) + biases[block_number, :3 * HW])
        shaped = low(normalize(stream) * (1.0 + modulation[:, HW:2 * HW]) + modulation[:, :HW])
        inner_rows = low_back(matmul(shaped, blocks[block_number, :, 3 * HW:4 * HW]) + biases[block_number, 3 * HW:4 * HW])
        branch = low_back(matmul(low(jax.nn.silu(inner_rows)), blocks[block_number, :, 4 * HW:].T) + biases[block_number, 4 * HW:])
        stream = stream + modulation[:, 2 * HW:] * branch
    final_weights = jnp.concatenate([edge_rows[base + FREQ + HW:base + FREQ + 2 * HW], edge_rows[base + FREQ + 2 * HW:]], 1)
    final_mod = low_back(matmul(silu_cond, final_weights) + extra[2 * HW:4 * HW])
    final_in = low(normalize(stream) * (1.0 + final_mod[:, HW:]) + final_mod[:, :HW])
    predicted = low_back(matmul(final_in, edge_rows[D + CH:D + 2 * CH].T))
    errors = lax.optimization_barrier(jnp.mean((predicted - target) ** 2, -1))
    return jnp.sum(weight_rows.reshape(-1) * errors)

def invert(order_row):
    return jnp.zeros(order_row.shape, jnp.int32).at[order_row].set(jnp.arange(order_row.shape[0], dtype=jnp.int32))

def grouped(array):
    return array.reshape((N_DP * N_FSDP, HEAD_DEV) + array.shape[1:])

def adamw(master, first, second, gradient, factor, step_rate):
    clipped = gradient * factor
    first_new = BETA_ONE * first + (1.0 - BETA_ONE) * clipped
    second_new = BETA_TWO * second + (1.0 - BETA_TWO) * clipped * clipped
    mean_hat = first_new / (1.0 - BETA_ONE ** ADAM_STEP)
    var_hat = second_new / (1.0 - BETA_TWO ** ADAM_STEP)
    updated = master - step_rate * (mean_hat / (jnp.sqrt(var_hat) + ADAM_EPS) + DECAY_RATE * master)
    return (updated, first_new, second_new)

def reference(latents, orders, mask_counts, noise, timesteps, loss_weights, block_weights, block_gains, entry_table, head_weights, head_biases, head_edges, first_blocks, first_gains, first_entry, first_head, first_biases, first_edges, second_blocks, second_gains, second_entry, second_head, second_biases, second_edges):
    masters = (block_weights, block_gains, entry_table, head_weights, head_biases, head_edges)
    firsts = (first_blocks, first_gains, first_entry, first_head, first_biases, first_edges)
    seconds = (second_blocks, second_gains, second_entry, second_head, second_biases, second_edges)
    step_rates = (LEARN_RATE, GAIN_RATE, LEARN_RATE, LEARN_RATE, LEARN_RATE, LEARN_RATE)
    clean_all = latents.astype(jnp.float32)
    noise_all = noise.astype(jnp.float32)
    ranks = jax.vmap(invert)(orders)
    masked = ranks < mask_counts[:, None]
    count_ends = jnp.cumsum(mask_counts).astype(jnp.int32)
    starts = count_ends - mask_counts
    row_ids = jnp.arange(TOTAL_MASKED, dtype=jnp.int32)
    global_ids = row_ids % HEAD_DEV * (N_DP * N_FSDP) + row_ids // HEAD_DEV
    image_of = lax.optimization_barrier(jnp.sum((global_ids[:, None] >= count_ends[None, :]).astype(jnp.int32), 1))
    position = orders[image_of, global_ids - starts[image_of]]
    weight_sum = jnp.sum(loss_weights)

    def objective(params):
        used = [low(param_array) for param_array in params]

        def one_image(image_pair):
            return trunk(used[0], used[1], used[2], image_pair[0], image_pair[1])
        top_rows = lax.map(jax.checkpoint(one_image), (clean_all, masked))
        cond_rows = low_back(low(top_rows[image_of, BUF + position]))

        def one_group(group_items):
            return head(used[3], used[4], used[5], group_items[0], group_items[1], group_items[2], group_items[3], group_items[4])
        sums = lax.map(jax.checkpoint(one_group), (grouped(cond_rows), grouped(clean_all[image_of, position]), grouped(noise_all), grouped(timesteps), grouped(loss_weights)))
        loss_total = jnp.sum(sums)
        return (loss_total / weight_sum, loss_total)
    objective_value, pullback, loss_sum = jax.vjp(objective, masters, has_aux=True)
    gradients = pullback(jnp.ones((), jnp.float32))[0]
    squares = sum((jnp.sum(gradient * gradient) for gradient in gradients))
    grad_norm = jnp.sqrt(squares)
    factor = CLIP_NORM / jnp.maximum(grad_norm, CLIP_NORM)
    results = [adamw(masters[number], firsts[number], seconds[number], gradients[number], factor, step_rates[number]) for number in range(6)]
    return (results[0][0], results[1][0], results[2][0], results[3][0], results[4][0], results[5][0], results[0][1], results[1][1], results[2][1], results[3][1], results[4][1], results[5][1], results[0][2], results[1][2], results[2][2], results[3][2], results[4][2], results[5][2], loss_sum, weight_sum, grad_norm)
```

```python
import functools
import math

import jax
import jax.numpy as jnp
from jax import lax
from jax.experimental import pallas as pl
from jax.experimental.pallas import tpu as pltpu
from jax.sharding import PartitionSpec as P

D = 768
HEADS = 12
HD = 64
FF = 3072
HW = 1024
CH = 16
FREQ = 256
LAT = 256
BUF = 64
HB = 2
COPIES = 4
TSTEPS = 1000
ADAM_STEP = 5
SEQ = 320

BETA_ONE = 0.5
BETA_TWO = 0.5
LEARN_RATE = 0.03
GAIN_RATE = 0.3
DECAY_RATE = 0.02
ADAM_EPS = 1e-08
CLIP_NORM = 0.002
NORM_EPS = 1e-06
AXES = ("dp", "fsdp")
HEAD_DIRECT = False
MESH_IDS = pl.DeviceIdType.MESH


def rs_kernel(nz, row_count, width, jobs, extra_count, *refs):
    job_count = len(jobs)
    x_refs, y_refs = refs[:job_count], refs[job_count : 2 * job_count]
    position = 2 * job_count
    extra_ref = None
    if extra_count:
        extra_ref = refs[position]
        position += 1
    out_ref = refs[position]
    (
        x_buf, y_buf, whole, land_core, first, land_first, second, land_second,
        last, last_low, land_last,
        load_sem, core_send, core_recv, first_send, first_recv, second_send, second_recv,
        last_send, last_recv, credit,
    ) = refs[position + 1 :]
    dp, z = lax.axis_index("dp"), lax.axis_index("fsdp")
    core, xb, yb = lax.rem(dp, 2), lax.rem(dp // 2, 2), dp // 4
    group = row_count // 8
    part = group // nz
    starts, total = [], 0
    for _, columns in jobs:
        starts.append(total)
        total += columns // width
    computed = total
    total += extra_count

    core_peer = (dp + 1 - 2 * core, z)
    x_step, y_step = 2 - 4 * xb, 4 - 8 * yb
    z_peers = [(dp, lax.rem(z + s, nz)) for s in range(1, nz)]
    barrier = pltpu.get_barrier_semaphore()
    for peer in [core_peer, (dp + x_step, z), (dp + y_step, z)] + z_peers:
        pl.semaphore_signal(barrier, inc=1, device_id=peer, device_id_type=MESH_IDS)
    pl.semaphore_wait(barrier, 2 + nz)

    def loads(x_ref, y_ref, column, slot):
        return (
            pltpu.make_async_copy(x_ref, x_buf.at[slot], load_sem.at[0, slot]),
            pltpu.make_async_copy(
                y_ref.at[:, pl.ds(pl.multiple_of(column, 128), width)], y_buf.at[slot], load_sem.at[1, slot]
            ),
        )

    def prefetch(g):
        for number, (_, columns) in enumerate(jobs):
            start, stop = starts[number], starts[number] + columns // width

            @pl.when((g >= start) & (g < stop))
            def _():
                for copy in loads(x_refs[number], y_refs[number], (g - start) * width, lax.rem(g, 2)):
                    copy.start()

    def core_copy(g):
        return pltpu.make_async_remote_copy(
            src_ref=whole.at[lax.rem(g, 2), 1 - core],
            dst_ref=land_core.at[lax.rem(g, 4)],
            send_sem=core_send.at[lax.rem(g, 2)],
            recv_sem=core_recv.at[lax.rem(g, 4)],
            device_id=core_peer,
            device_id_type=MESH_IDS,
        )

    def first_copy(g):
        p = lax.rem(g, 2)
        mine = (1 - p) * xb + p * yb
        return pltpu.make_async_remote_copy(
            src_ref=first.at[lax.rem(g, 3), 1 - mine],
            dst_ref=land_first.at[g],
            send_sem=first_send.at[lax.rem(g, 3)],
            recv_sem=first_recv.at[g],
            device_id=(dp + (1 - p) * x_step + p * y_step, z),
            device_id_type=MESH_IDS,
        )

    def second_copy(g):
        p = lax.rem(g, 2)
        mine = (1 - p) * yb + p * xb
        return pltpu.make_async_remote_copy(
            src_ref=second.at[lax.rem(g, 3), 1 - mine],
            dst_ref=land_second.at[g],
            send_sem=second_send.at[lax.rem(g, 3)],
            recv_sem=second_recv.at[g],
            device_id=(dp + (1 - p) * y_step + p * x_step, z),
            device_id_type=MESH_IDS,
        )

    def last_copies(g):
        return [
            pltpu.make_async_remote_copy(
                src_ref=last_low.at[lax.rem(g, 3), lax.rem(z + s, nz)],
                dst_ref=land_last.at[g, s - 1],
                send_sem=last_send.at[lax.rem(g, 3), s - 1],
                recv_sem=last_recv.at[g, s - 1],
                device_id=z_peers[s - 1],
                device_id_type=MESH_IDS,
            )
            for s in range(1, nz)
        ]

    low_rows, low_width = last_low.shape[2:]
    folds = width // low_width

    def fold(block):
        return jnp.concatenate([block[:, k * low_width : (k + 1) * low_width] for k in range(folds)], 0)

    def stage_core(g):
        slot = lax.rem(g, 2)

        @pl.when(g >= 2)
        def _():
            core_copy(g - 2).wait_send()

        def put(number, value):
            yx, c = number // 2, number % 2
            whole[slot, c, yx] = value

        @pl.when(g < computed)
        def _():
            for copy in loads(x_refs[0], y_refs[0], 0, slot):
                copy.wait()
            for number in range(8):
                put(number, lax.dot_general(
                    x_buf[slot, :, pl.ds(number * group, group)], y_buf[slot],
                    (((0,), (0,)), ((), ())), preferred_element_type=jnp.float32,
                ).astype(jnp.bfloat16))

        if extra_count:
            @pl.when(g >= computed)
            def _():
                for number in range(8):
                    put(number, extra_ref[g - computed, pl.ds(number * group, group), :])

        @pl.when(g >= 4)
        def _():
            pl.semaphore_wait(credit, 1)
        core_copy(g).start()

    def stage_first(g):
        p = lax.rem(g, 2)

        @pl.when(g >= 3)
        def _():
            first_copy(g - 3).wait_send()
        core_copy(g).wait_recv()
        for f in range(2):
            for s in range(2):
                yx = (1 - p) * (2 * s + f) + p * (2 * f + s)
                first[lax.rem(g, 3), f, s] = (
                    whole[lax.rem(g, 2), core, yx].astype(jnp.float32)
                    + land_core[lax.rem(g, 4), yx].astype(jnp.float32)
                ).astype(jnp.bfloat16)

        @pl.when(g < total - 4)
        def _():
            pl.semaphore_signal(credit, inc=1, device_id=core_peer, device_id_type=MESH_IDS)
        first_copy(g).start()

    def stage_second(g):
        p = lax.rem(g, 2)
        mine = (1 - p) * xb + p * yb

        @pl.when(g >= 3)
        def _():
            second_copy(g - 3).wait_send()
        first_copy(g).wait_recv()
        for s in range(2):
            second[lax.rem(g, 3), s] = (
                first[lax.rem(g, 3), mine, s].astype(jnp.float32) + land_first[g, s].astype(jnp.float32)
            ).astype(jnp.bfloat16)
        second_copy(g).start()

    def stage_last(g):
        p = lax.rem(g, 2)
        mine = (1 - p) * yb + p * xb

        @pl.when(g >= 3)
        def _():
            for copy in last_copies(g - 3):
                copy.wait_send()
        second_copy(g).wait_recv()
        summed = second[lax.rem(g, 3), mine].astype(jnp.float32) + land_second[g].astype(jnp.float32)
        for k in range(nz):
            block = fold(summed[k * part : (k + 1) * part])
            last[lax.rem(g, 3), k] = block
            last_low[lax.rem(g, 3), k] = block.astype(jnp.bfloat16)
        for copy in last_copies(g):
            copy.start()

    def stage_out(g):
        for copy in last_copies(g):
            copy.wait_recv()
        value = last[lax.rem(g, 3), z]
        for s in range(1, nz):
            value = value + land_last[g, s - 1].astype(jnp.float32)
        for k in range(folds):
            out_ref[g, :, pl.ds(k * low_width, low_width)] = value[k * part : (k + 1) * part]

    lags = (0, 1, 3, 5, 7)
    prefetch(0)

    @pl.loop(0, total + lags[-1])
    def _(i):
        for stage, lag in zip((stage_out, stage_last, stage_second, stage_first), lags[:0:-1]):
            @pl.when((i >= lag) & (i < total + lag))
            def _():
                stage(i - lag)

        @pl.when(i + 1 < computed)
        def _():
            prefetch(i + 1)

        @pl.when(i < total)
        def _():
            stage_core(i)

    for g in range(max(total - 2, 0), total):
        core_copy(g).wait_send()
    for g in range(max(total - 3, 0), total):
        first_copy(g).wait_send()
        second_copy(g).wait_send()
        for copy in last_copies(g):
            copy.wait_send()


def reduce_products(pairs, extras, row_count, width, low_shape, nz, collective_id):
    bf, tokens = jnp.bfloat16, pairs[0][0].shape[0]
    group, part = row_count // 8, row_count // 8 // nz
    jobs = [(x.shape[1], y.shape[1]) for x, y in pairs]
    total = sum(columns // width for _, columns in jobs)
    extra_count = 0 if extras is None else extras.shape[0]
    total += extra_count
    low_rows, low_width = low_shape
    dma, reg = pltpu.SemaphoreType.DMA, pltpu.SemaphoreType.REGULAR
    operands = [x for x, _ in pairs] + [y for _, y in pairs]
    specs = [pl.BlockSpec(memory_space=pl.ANY)] * len(operands)
    if extra_count:
        operands.append(extras)
        specs.append(pl.BlockSpec(memory_space=pltpu.VMEM))
    return pl.pallas_call(
        functools.partial(rs_kernel, nz, row_count, width, jobs, extra_count),
        out_shape=jax.ShapeDtypeStruct((total, part, width), jnp.float32),
        in_specs=specs,
        out_specs=pl.BlockSpec(memory_space=pltpu.VMEM),
        scratch_shapes=[
            pltpu.VMEM((2, tokens, row_count), bf),
            pltpu.VMEM((2, tokens, width), bf),
            pltpu.VMEM((2, 2, 4, group, width), bf),
            pltpu.VMEM((4, 4, group, width), bf),
            pltpu.VMEM((3, 2, 2, group, width), bf),
            pltpu.VMEM((total, 2, group, width), bf),
            pltpu.VMEM((3, 2, group, width), bf),
            pltpu.VMEM((total, group, width), bf),
            pltpu.VMEM((3, nz, low_rows, low_width), jnp.float32),
            pltpu.VMEM((3, nz, low_rows, low_width), bf),
            pltpu.VMEM((total, nz - 1, low_rows, low_width), bf),
            dma((2, 2)), dma((2,)), dma((4,)), dma((3,)), dma((total,)), dma((3,)), dma((total,)),
            dma((3, nz - 1)), dma((total, nz - 1)), reg,
        ],
        compiler_params=pltpu.CompilerParams(
            collective_id=collective_id, has_side_effects=True, vmem_limit_bytes=56 * 2**20
        ),
    )(*operands)


def ag_kernel(nz, chunks, source_count, *refs):
    sources, refs = refs[:source_count], refs[source_count:]
    result_count = 1 + max(chunk[3] for chunk in chunks)
    results, sems = refs[:result_count], refs[result_count:]
    own_sem, last_send, last_recv, first_send, first_recv, second_send, second_recv, core_send, core_recv = sems
    dp, z = lax.axis_index("dp"), lax.axis_index("fsdp")
    core, xb, yb = lax.rem(dp, 2), lax.rem(dp // 2, 2), dp // 4
    core_peer = (dp + 1 - 2 * core, z)
    x_peer, y_peer = (dp + 2 - 4 * xb, z), (dp + 4 - 8 * yb, z)
    z_peers = [(dp, lax.rem(z + s, nz)) for s in range(1, nz)]
    barrier = pltpu.get_barrier_semaphore()
    for peer in [core_peer, x_peer, y_peer] + z_peers:
        pl.semaphore_signal(barrier, inc=1, device_id=peer, device_id_type=MESH_IDS)
    pl.semaphore_wait(barrier, 2 + nz)

    def remote(source, target, send, recv, peer):
        return pltpu.make_async_remote_copy(
            src_ref=source, dst_ref=target, send_sem=send, recv_sem=recv, device_id=peer, device_id_type=MESH_IDS
        )

    def source_of(k):
        source, index, column, _, _, width = chunks[k]
        ref = sources[source] if index is None else sources[source].at[index]
        return ref.at[:, pl.ds(column, width)]

    def result_of(k):
        _, _, _, result, column, width = chunks[k]
        return results[result].at[:, :, :, :, :, pl.ds(column, width)]

    def own(k):
        return pltpu.make_async_copy(source_of(k), result_of(k).at[yb, xb, core, z], own_sem.at[k])

    def z_copies(k):
        return [
            remote(source_of(k), result_of(k).at[yb, xb, core, z], last_send.at[k, s], last_recv.at[k, s], z_peers[s])
            for s in range(nz - 1)
        ]

    def first(k):
        ref = result_of(k).at[yb, xb, core]
        return remote(ref, ref, first_send.at[k], first_recv.at[k], y_peer if k % 2 else x_peer)

    def second(k):
        ref = result_of(k).at[:, xb, core] if k % 2 else result_of(k).at[yb, :, core]
        return remote(ref, ref, second_send.at[k], second_recv.at[k], x_peer if k % 2 else y_peer)

    def across(k):
        ref = result_of(k).at[:, :, core]
        return remote(ref, ref, core_send.at[k], core_recv.at[k], core_peer)

    total = len(chunks)
    for i in range(total + 6):
        k = i - 6
        if k >= 0:
            second(k).wait_recv()
            across(k).start()
        k = i - 4
        if 0 <= k < total:
            first(k).wait_recv()
            second(k).start()
        k = i - 2
        if 0 <= k < total:
            own(k).wait()
            for copy in z_copies(k):
                copy.wait_recv()
            first(k).start()
        if i < total:
            own(i).start()
            for copy in z_copies(i):
                copy.start()
    for k in range(total):
        for copy in z_copies(k) + [first(k), second(k), across(k)]:
            copy.wait_send()
        across(k).wait_recv()


def gather_rows(sources, chunks, widths, rows, nz, collective_id):
    dma = pltpu.SemaphoreType.DMA
    total = len(chunks)
    return pl.pallas_call(
        functools.partial(ag_kernel, nz, chunks, len(sources)),
        out_shape=[jax.ShapeDtypeStruct((2, 2, 2, nz, rows, width), jnp.bfloat16) for width in widths],
        in_specs=[pl.BlockSpec(memory_space=pl.ANY)] * len(sources),
        out_specs=[pl.BlockSpec(memory_space=pl.ANY)] * len(widths),
        scratch_shapes=[
            dma((total,)), dma((total, nz - 1)), dma((total, nz - 1)),
            dma((total,)), dma((total,)), dma((total,)), dma((total,)), dma((total,)), dma((total,)),
        ],
        compiler_params=pltpu.CompilerParams(
            collective_id=collective_id, has_side_effects=True, vmem_limit_bytes=4 * 2**20
        ),
    )(*sources)


def exchange_kernel(dp_count, nz, in_ref, out_ref, send_sem, recv_sem):
    devices = dp_count * nz
    me = lax.axis_index("dp") * nz + lax.axis_index("fsdp")

    def peer(step):
        there = lax.rem(me + step, devices)
        return (there // nz, lax.rem(there, nz))

    barrier = pltpu.get_barrier_semaphore()

    @pl.loop(1, devices)
    def _(step):
        pl.semaphore_signal(barrier, inc=1, device_id=peer(step), device_id_type=MESH_IDS)

    pl.semaphore_wait(barrier, devices - 1)

    def copy(step):
        return pltpu.make_async_remote_copy(
            src_ref=in_ref,
            dst_ref=out_ref.at[me],
            send_sem=send_sem.at[step - 1],
            recv_sem=recv_sem.at[step - 1],
            device_id=peer(step),
            device_id_type=MESH_IDS,
        )

    @pl.loop(1, devices)
    def _(step):
        copy(step).start()

    out_ref[me] = in_ref[...]

    @pl.loop(1, devices)
    def _(step):
        copy(step).wait()


def exchange(values, dp_count, nz, collective_id):
    devices = dp_count * nz
    tile = jnp.broadcast_to(jnp.pad(values, (0, 128 - values.shape[0])), (8, 128))
    out = pl.pallas_call(
        functools.partial(exchange_kernel, dp_count, nz),
        out_shape=jax.ShapeDtypeStruct((devices, 8, 128), jnp.float32),
        in_specs=[pl.BlockSpec(memory_space=pltpu.VMEM)],
        out_specs=pl.BlockSpec(memory_space=pltpu.VMEM),
        scratch_shapes=[pltpu.SemaphoreType.DMA((devices - 1,)), pltpu.SemaphoreType.DMA((devices - 1,))],
        compiler_params=pltpu.CompilerParams(
            collective_id=collective_id, has_side_effects=True, vmem_limit_bytes=4 * 2**20
        ),
    )(tile)
    return out[:, 0, : values.shape[0]]


def dot_plain(left, right):
    return jnp.dot(left, right, preferred_element_type=jnp.float32)


def dot_left(left, right):
    return lax.dot_general(
        left, right, (((0,), (0,)), ((), ())), preferred_element_type=jnp.float32
    )


def dot_right(left, right):
    return lax.dot_general(
        left, right, (((1,), (1,)), ((), ())), preferred_element_type=jnp.float32
    )


def normalize(values):
    centred = values - jnp.mean(values, -1, keepdims=True)
    inverse = lax.rsqrt(jnp.mean(centred * centred, -1, keepdims=True) + NORM_EPS)
    return (centred * inverse, inverse)


def norm_back(upstream, normed, inverse):
    return inverse * (
        upstream
        - jnp.mean(upstream, -1, keepdims=True)
        - normed * jnp.mean(upstream * normed, -1, keepdims=True)
    )


def local_grad(function, inputs, upstream):
    return jax.vjp(function, inputs)[1](upstream)[0]


def column_sum(values):
    return jnp.sum(values.astype(jnp.float32), 0)


def layer_forward(hidden, weights, gains, key_keep):
    w_qkv, w_out, w_up, w_down = weights
    first_norm, first_inv = normalize(hidden)
    normed = (first_norm * gains[0]).astype(jnp.bfloat16)
    packed = dot_plain(normed, w_qkv).astype(jnp.bfloat16)
    query_rows = packed[:, :D].reshape(SEQ, HEADS, HD)
    key_rows = packed[:, D : 2 * D].reshape(SEQ, HEADS, HD)
    value_rows = packed[:, 2 * D :].reshape(SEQ, HEADS, HD)
    scores = jnp.einsum(
        "qhd,khd->hqk", query_rows, key_rows, preferred_element_type=jnp.float32
    ) * HD ** (-0.5)
    if key_keep is not None:
        scores = jnp.where(key_keep[None, None, :] > 0, scores, -1e30)
    attention = jax.nn.softmax(scores, -1)
    attention_low = attention.astype(jnp.bfloat16)
    mixed_heads = (
        jnp.einsum("hqk,khd->qhd", attention_low, value_rows, preferred_element_type=jnp.float32)
        .reshape(-1, D)
        .astype(jnp.bfloat16)
    )
    middle = hidden + dot_plain(mixed_heads, w_out)
    second_norm, second_inv = normalize(middle)
    second = (second_norm * gains[1]).astype(jnp.bfloat16)
    inner_rows = dot_plain(second, w_up)
    upper_rows = jax.nn.gelu(inner_rows).astype(jnp.bfloat16)
    output = middle + dot_right(upper_rows, w_down)
    saved = (
        first_norm, first_inv, normed, query_rows, key_rows, value_rows, attention,
        attention_low, mixed_heads, second_norm, second_inv, second, inner_rows, upper_rows,
    )
    return (output, saved)


def layer_backward(upstream, weights, gains, saved):
    w_qkv, w_out, w_up, w_down = weights
    (
        first_norm, first_inv, normed, query_rows, key_rows, value_rows, attention,
        attention_low, mixed_heads, second_norm, second_inv, second, inner_rows, upper_rows,
    ) = saved
    back_branch = upstream.astype(jnp.bfloat16)
    back_upper = dot_plain(back_branch, w_down)
    back_inner = local_grad(jax.nn.gelu, inner_rows, back_upper).astype(jnp.bfloat16)
    back_second = dot_right(back_inner, w_up)
    grad_gain_two = jnp.sum(back_second * second_norm, 0)
    back_middle = upstream + norm_back(back_second * gains[1], second_norm, second_inv)
    back_attn_out = back_middle.astype(jnp.bfloat16)
    back_mixed = dot_right(back_attn_out, w_out).astype(jnp.bfloat16).reshape(SEQ, HEADS, HD)
    back_attention = jnp.einsum(
        "qhd,khd->hqk", back_mixed, value_rows, preferred_element_type=jnp.float32
    )
    back_values = jnp.einsum(
        "hqk,qhd->khd", attention_low, back_mixed, preferred_element_type=jnp.float32
    )
    back_scores = (
        attention * (back_attention - jnp.sum(back_attention * attention, -1, keepdims=True))
    ).astype(jnp.bfloat16)
    back_queries = jnp.einsum(
        "hqk,khd->qhd", back_scores, key_rows, preferred_element_type=jnp.float32
    ) * HD ** (-0.5)
    back_keys = jnp.einsum(
        "hqk,qhd->khd", back_scores, query_rows, preferred_element_type=jnp.float32
    ) * HD ** (-0.5)
    back_packed = jnp.concatenate(
        [back_queries.reshape(-1, D), back_keys.reshape(-1, D), back_values.reshape(-1, D)], 1
    ).astype(jnp.bfloat16)
    back_normed = dot_right(back_packed, w_qkv)
    grad_gain_one = jnp.sum(back_normed * first_norm, 0)
    back_hidden = back_middle + norm_back(back_normed * gains[0], first_norm, first_inv)
    pairs = [
        (normed, back_packed), (mixed_heads, back_attn_out), (second, back_inner), (back_branch, upper_rows)
    ]
    return (back_hidden, pairs, [grad_gain_one, grad_gain_two])


def head_pass(
    blocks, edges, biases, cond_rows, clean_rows, noise_rows, step_rows, weight_rows, weight_total
):
    cond_t, time_two_t, shift_t, scale_t, time_one_t, in_t, out_t = edges
    token_count = cond_rows.shape[0]
    extra = biases[HB]
    half_freq = FREQ // 2
    frequencies = jnp.exp(-math.log(10000.0) * jnp.arange(half_freq, dtype=jnp.float32) / half_freq)
    step_times = step_rows.astype(jnp.float32)
    angles = step_times.reshape(-1)[:, None] * frequencies
    time_embed = jnp.concatenate([jnp.cos(angles), jnp.sin(angles)], -1).astype(jnp.bfloat16)
    time_inner = dot_right(time_embed, time_one_t) + extra[:HW]
    time_hidden = jax.nn.silu(time_inner).astype(jnp.bfloat16)
    time_vector = dot_right(time_hidden, time_two_t) + extra[HW : 2 * HW]
    projected = dot_right(cond_rows, cond_t)
    conditioning = (projected[:, None, :] + time_vector.reshape(token_count, COPIES, HW)).reshape(
        -1, HW
    )
    silu_cond = jax.nn.silu(conditioning).astype(jnp.bfloat16)
    phase_angle = (step_times / TSTEPS + 0.008) / 1.008 * (math.pi / 2)
    keep_part = jnp.cos(phase_angle)[..., None]
    noise_part = jnp.sin(phase_angle)[..., None]
    clean_copies = clean_rows.astype(jnp.float32)[:, None, :]
    fresh_noise = noise_rows.astype(jnp.float32).reshape(token_count, COPIES, CH)
    noisy_rows = (
        (keep_part * clean_copies + noise_part * fresh_noise).reshape(-1, CH).astype(jnp.bfloat16)
    )
    target = (keep_part * fresh_noise - noise_part * clean_copies).reshape(-1, CH)
    stream = dot_right(noisy_rows, in_t) + extra[4 * HW :]
    saved = []
    for block_number in range(HB):
        w_mod, w_up, w_down = blocks[block_number]
        bias_row = biases[block_number]
        modulation = dot_plain(silu_cond, w_mod) + bias_row[: 3 * HW]
        normed, inverse = normalize(stream)
        shaped = (normed * (1.0 + modulation[:, HW : 2 * HW]) + modulation[:, :HW]).astype(
            jnp.bfloat16
        )
        inner_rows = dot_plain(shaped, w_up) + bias_row[3 * HW : 4 * HW]
        hidden = jax.nn.silu(inner_rows).astype(jnp.bfloat16)
        branch = dot_right(hidden, w_down) + bias_row[4 * HW :]
        saved.append((modulation, normed, inverse, shaped, inner_rows, hidden, branch))
        stream = stream + modulation[:, 2 * HW :] * branch
    final_shift = dot_right(silu_cond, shift_t) + extra[2 * HW : 3 * HW]
    final_scale = dot_right(silu_cond, scale_t) + extra[3 * HW : 4 * HW]
    final_norm, final_inv = normalize(stream)
    final_low = (final_norm * (1.0 + final_scale) + final_shift).astype(jnp.bfloat16)
    predicted = dot_plain(final_low, out_t)
    flat_weights = weight_rows.reshape(-1)
    errors = jnp.mean((predicted - target) ** 2, -1)
    loss_local = jnp.sum(flat_weights * errors)
    back_pred = (flat_weights[:, None] * 2.0 * (predicted - target) / (CH * weight_total)).astype(
        jnp.bfloat16
    )
    grad_out_t = dot_left(final_low, back_pred)
    back_final = dot_right(back_pred, out_t)
    back_shift = back_final.astype(jnp.bfloat16)
    back_scale = (back_final * final_norm).astype(jnp.bfloat16)
    back_silu = dot_plain(back_shift, shift_t) + dot_plain(back_scale, scale_t)
    back_stream = norm_back(back_final * (1.0 + final_scale), final_norm, final_inv)
    block_pairs = [None] * HB
    bias_grads = [None] * (HB + 1)
    for block_number in reversed(range(HB)):
        w_mod, w_up, w_down = blocks[block_number]
        modulation, normed, inverse, shaped, inner_rows, hidden, branch = saved[block_number]
        back_branch = (back_stream * modulation[:, 2 * HW :]).astype(jnp.bfloat16)
        back_gate = back_stream * branch
        back_hidden = dot_plain(back_branch, w_down)
        back_inner = local_grad(jax.nn.silu, inner_rows, back_hidden).astype(jnp.bfloat16)
        back_shaped = dot_right(back_inner, w_up)
        back_stream = back_stream + norm_back(
            back_shaped * (1.0 + modulation[:, HW : 2 * HW]), normed, inverse
        )
        back_modulation = jnp.concatenate([back_shaped, back_shaped * normed, back_gate], 1).astype(
            jnp.bfloat16
        )
        back_silu = back_silu + dot_right(back_modulation, w_mod)
        block_pairs[block_number] = [
            (silu_cond, back_modulation), (shaped, back_inner), (back_branch, hidden)
        ]
        bias_grads[block_number] = jnp.concatenate(
            [column_sum(back_modulation), column_sum(back_inner), column_sum(back_branch)]
        )
    back_stream_low = back_stream.astype(jnp.bfloat16)
    grad_in_t = dot_left(back_stream_low, noisy_rows)
    back_conditioning = local_grad(jax.nn.silu, conditioning, back_silu)
    back_time = back_conditioning.astype(jnp.bfloat16)
    back_time_hidden = dot_plain(back_time, time_two_t)
    back_time_inner = local_grad(jax.nn.silu, time_inner, back_time_hidden).astype(jnp.bfloat16)
    grad_time_one_t = dot_left(back_time_inner, time_embed)
    back_cond = back_conditioning.reshape(token_count, COPIES, HW).sum(1).astype(jnp.bfloat16)
    grad_cond_t = dot_left(back_cond, cond_rows)
    back_tokens = dot_plain(back_cond, cond_t)
    bias_grads[HB] = jnp.concatenate(
        [
            column_sum(back_time_inner), column_sum(back_time), column_sum(back_shift),
            column_sum(back_scale), column_sum(back_stream_low),
        ]
    )
    pairs = [pair for group in block_pairs for pair in group] + [
        (back_time, time_hidden), (back_shift, silu_cond), (back_scale, silu_cond)
    ]
    small = (grad_cond_t, grad_time_one_t, grad_in_t, grad_out_t)
    return (loss_local, pairs, small, jnp.stack(bias_grads), back_tokens)


def adamw(master, first, second, gradient, factor, step_rate):
    clipped = gradient * factor
    first_new = BETA_ONE * first + (1.0 - BETA_ONE) * clipped
    second_new = BETA_TWO * second + (1.0 - BETA_TWO) * clipped * clipped
    mean_hat = first_new / (1.0 - BETA_ONE**ADAM_STEP)
    var_hat = second_new / (1.0 - BETA_TWO**ADAM_STEP)
    updated = master - step_rate * (mean_hat / (jnp.sqrt(var_hat) + ADAM_EPS) + DECAY_RATE * master)
    return (updated, first_new, second_new)


TRUNK_PARTS = (3 * D, D, FF, FF)
HEAD_PARTS = (3 * HW, HW, HW)
EDGE_PARTS = (D, HW, HW, HW, FREQ, 128)
TRUNK_WIDTH = 768
HEAD_WIDTH = 512


def gather_plan(part_sets, edge_parts, limit):
    chunks, widths = [], []
    for index, parts in enumerate(part_sets):
        column = 0
        for part in parts:
            for k in range(0, part, limit):
                chunks.append((0, index, column + k, len(widths), k, min(limit, part - k)))
            widths.append(part)
            column += part
    edge_chunks, column = [], 0
    for part in edge_parts:
        for k in range(0, part, limit):
            edge_chunks.append((1, None, column + k, len(widths), k, min(limit, part - k)))
        widths.append(part)
        column += part
    return edge_chunks + chunks, widths


def plain_gather(sources, chunks, widths):
    ends = {}
    for source, index, column, result, at, width in chunks:
        start, stop = ends.get(result, (source, index, column, column))[2:]
        ends[result] = (source, index, min(start, column), max(stop, column + width))
    wholes = {}
    results = []
    for number in range(len(widths)):
        source, index, start, stop = ends[number]
        if (source, index) not in wholes:
            block = sources[source] if index is None else sources[source][index]
            wholes[source, index] = lax.all_gather(block, AXES, axis=0, tiled=True)
        results.append(wholes[source, index][:, start:stop])
    return results


def scatter_sum(values):
    low = lax.psum_scatter(values, "dp", scatter_dimension=0, tiled=True)
    return lax.psum_scatter(low, "fsdp", scatter_dimension=0, tiled=True)


def on_device(
    mesh_shape,
    latents, orders, mask_counts, noise, timesteps, loss_weights,
    block_weights, block_gains, entry_table, head_weights, head_biases, head_edges,
    first_blocks, first_gains, first_entry, first_head, first_biases, first_edges,
    second_blocks, second_gains, second_entry, second_head, second_biases, second_edges,
):
    dp_count, nz = mesh_shape["dp"], mesh_shape["fsdp"]
    devices = dp_count * nz
    me = lax.axis_index("dp") * nz + lax.axis_index("fsdp")
    r0, r1 = D // devices, HW // devices
    direct = dp_count == 8 and nz > 1 and (D // 8) % 16 == 0
    bf = jnp.bfloat16

    low_blocks = block_weights.astype(bf)
    low_entry = jnp.concatenate(
        [entry_table.T.astype(bf), block_gains.reshape(4, r0).T.astype(bf), jnp.zeros((r0, 108), bf)], 1
    )
    low_head = head_weights.astype(bf)
    edge = head_edges.T.astype(bf)
    base = D + 2 * CH
    low_edges = jnp.concatenate(
        [
            edge[:, :D], edge[:, base + FREQ :], edge[:, base : base + FREQ], edge[:, D:base],
            head_biases.reshape((HB + 1) * 5, r1).T.astype(bf), jnp.zeros((r1, 81), bf),
        ],
        1,
    )
    trunk_chunks, trunk_widths = gather_plan([TRUNK_PARTS] * 2, (TRUNK_WIDTH,), TRUNK_WIDTH)
    head_chunks, head_widths = gather_plan([HEAD_PARTS] * HB, EDGE_PARTS, HEAD_WIDTH)
    if direct:
        trunk = [
            a.reshape(D, -1) for a in gather_rows([low_blocks, low_entry], trunk_chunks, trunk_widths, r0, nz, 1)
        ]
    else:
        trunk = plain_gather([low_blocks, low_entry], trunk_chunks, trunk_widths)
    if direct and HEAD_DIRECT:
        head = [
            a.reshape(HW, -1) for a in gather_rows([low_head, low_edges], head_chunks, head_widths, r1, nz, 2)
        ]
    else:
        head = plain_gather([low_head, low_edges], head_chunks, head_widths)

    local_total = jnp.sum(mask_counts)
    early = exchange(
        jnp.stack([local_total.astype(jnp.float32), jnp.sum(loss_weights)]), dp_count, nz, 3
    )
    counts = early[:, 0].astype(jnp.int32)
    weight_total = jnp.sum(early[:, 1])
    count_ends = jnp.cumsum(counts)
    count_starts = count_ends - counts
    offset = jnp.sum(jnp.where(jnp.arange(devices) == me, count_starts, 0))

    order_row = orders[0]
    clean = latents[0]
    ids = jnp.arange(LAT, dtype=jnp.int32)
    masked = jnp.any((order_row[:, None] == ids[None, :]) & (ids < local_total)[:, None], 0)
    key_keep = jnp.concatenate([jnp.ones((BUF,), jnp.float32), 1.0 - masked.astype(jnp.float32)])
    layers = (trunk[:4], trunk[4:8])
    entry = trunk[8].T
    entry_rows = entry[: 2 * SEQ].astype(jnp.float32)
    gain_rows = entry[2 * SEQ + CH : 2 * SEQ + CH + 4].astype(jnp.float32)
    projected = dot_plain(clean, entry[2 * SEQ : 2 * SEQ + CH])
    start_rows = entry_rows[:SEQ] + jnp.concatenate([jnp.zeros((BUF, D), jnp.float32), projected], 0)
    encoded, encoder_saved = layer_forward(start_rows, layers[0], gain_rows[:2], key_keep)
    decoder_input = encoded * key_keep[:, None] + entry_rows[SEQ : 2 * SEQ]
    top_rows, decoder_saved = layer_forward(decoder_input, layers[1], gain_rows[2:], None)

    capacity = (LAT + devices - 1) // devices
    slots = devices * capacity
    slot_ids = jnp.arange(slots, dtype=jnp.int32)
    slot_token = jnp.mod(slot_ids // capacity - offset, devices) + devices * (slot_ids % capacity)
    slot_position = jnp.sum(
        jnp.where(slot_token[:, None] == ids[None, :], order_row[None, :], 0), 1
    )
    pick = (
        (slot_position[:, None] == ids[None, :]) & (slot_token < local_total)[:, None]
    ).astype(bf)
    outgoing = dot_plain(
        pick, jnp.concatenate([top_rows[BUF:].astype(bf), clean, jnp.zeros((LAT, 112), bf)], 1)
    ).astype(bf)
    incoming = lax.all_to_all(
        outgoing.reshape(devices, capacity, -1), AXES, split_axis=0, concat_axis=0, tiled=True
    ).reshape(slots, -1)
    head_rows = noise.shape[0]
    token_ids = jnp.arange(head_rows, dtype=jnp.int32) * devices + me
    inside = (token_ids[:, None] >= count_starts[None, :]) & (token_ids[:, None] < count_ends[None, :])
    first_token = count_starts + jnp.mod(me - count_starts, devices)
    source_slot = (
        jnp.arange(devices, dtype=jnp.int32)[None, :] * capacity
        + (token_ids[:, None] - first_token[None, :]) // devices
    )
    row_slot = jnp.sum(jnp.where(inside, source_slot, 0), 1)
    place = (row_slot[:, None] == slot_ids[None, :]).astype(bf)
    received = dot_plain(place, incoming).astype(bf)

    head_blocks = [head[3 * b : 3 * b + 3] for b in range(HB)]
    edge_mats = head[3 * HB :]
    misc = edge_mats[5]
    biases = (
        misc[:, 2 * CH : 2 * CH + 5 * (HB + 1)]
        .reshape(devices, r1, HB + 1, 5)
        .transpose(2, 0, 3, 1)
        .reshape(HB + 1, 5 * HW)
        .astype(jnp.float32)
    )
    loss_local, head_pairs, small, bias_grad, back_tokens = head_pass(
        head_blocks,
        edge_mats[:5] + [misc[:, :CH], misc[:, CH : 2 * CH]],
        biases,
        received[:, :D],
        received[:, D : D + CH],
        noise,
        timesteps,
        loss_weights,
        weight_total,
    )
    grad_cond_t, grad_time_one_t, grad_in_t, grad_out_t = small
    bias_t = (
        bias_grad.reshape(HB + 1, devices, 5, r1).transpose(1, 3, 0, 2).reshape(HW, 5 * (HB + 1))
    )
    head_small = jnp.concatenate(
        [grad_cond_t, grad_time_one_t, grad_in_t, grad_out_t, bias_t, jnp.zeros((HW, 465), jnp.float32)], 1
    ).astype(bf)
    small_columns = head_small.shape[1]
    if direct:
        extras = jnp.stack(
            [head_small[:, k : k + HEAD_WIDTH] for k in range(0, small_columns, HEAD_WIDTH)]
        )
        tall = reduce_products(head_pairs, extras, HW, HEAD_WIDTH, (r1, HEAD_WIDTH), nz, 4)
        tall = tall.transpose(1, 0, 2).reshape(r1, -1)
    else:
        tall = jnp.concatenate(
            [scatter_sum(dot_left(x, y)) for x, y in head_pairs]
            + [scatter_sum(head_small.astype(jnp.float32))],
            1,
        )

    returning = dot_left(place, back_tokens.astype(bf)).astype(bf)
    returned = lax.all_to_all(
        returning.reshape(devices, capacity, D), AXES, split_axis=0, concat_axis=0, tiled=True
    ).reshape(slots, D)
    back_top = jnp.concatenate([jnp.zeros((BUF, D), jnp.float32), dot_left(pick, returned)], 0)
    back_decoder, decoder_pairs, decoder_gains = layer_backward(
        back_top, layers[1], gain_rows[2:], decoder_saved
    )
    back_encoded = back_decoder * key_keep[:, None]
    back_start, encoder_pairs, encoder_gains = layer_backward(
        back_encoded, layers[0], gain_rows[:2], encoder_saved
    )
    grad_input_t = dot_left(back_start[BUF:].astype(bf), clean)
    trunk_small = jnp.concatenate(
        [
            back_start.T, back_decoder.T, grad_input_t,
            jnp.stack(encoder_gains + decoder_gains, 1), jnp.zeros((D, 108), jnp.float32),
        ],
        1,
    ).astype(bf)
    trunk_pairs = encoder_pairs + decoder_pairs
    if direct:
        wide = reduce_products(
            trunk_pairs, trunk_small[None], D, TRUNK_WIDTH, (2 * r0, TRUNK_WIDTH // 2), nz, 5
        )
        wide = wide.transpose(1, 0, 2).reshape(r0, -1)
    else:
        wide = jnp.concatenate(
            [scatter_sum(dot_left(x, y)) for x, y in trunk_pairs]
            + [scatter_sum(trunk_small.astype(jnp.float32))],
            1,
        )
    block_columns, head_columns = sum(TRUNK_PARTS), sum(HEAD_PARTS)
    block_grad = jnp.stack([wide[:, l * block_columns : (l + 1) * block_columns] for l in range(2)])
    rest = wide[:, 2 * block_columns :]
    entry_grad = rest[:, : 2 * SEQ + CH].T
    gain_grad = rest[:, 2 * SEQ + CH : 2 * SEQ + CH + 4].T.reshape(2, 2, r0)
    head_grad = jnp.stack([tall[:, b * head_columns : (b + 1) * head_columns] for b in range(HB)])
    rest = tall[:, HB * head_columns :]
    shared = rest[:, 3 * HW :]
    edge_grad = jnp.concatenate(
        [
            shared[:, :D], shared[:, D + FREQ : D + FREQ + 2 * CH], shared[:, D : D + FREQ],
            rest[:, : 3 * HW],
        ],
        1,
    ).T
    bias_grad = (
        shared[:, D + FREQ + 2 * CH : D + FREQ + 2 * CH + 5 * (HB + 1)].T.reshape(HB + 1, 5 * r1)
    )
    squares = jnp.sum(wide * wide) + jnp.sum(tall * tall)
    late = exchange(jnp.stack([loss_local, squares]), dp_count, nz, 6)
    loss_sum = jnp.sum(late[:, 0])
    grad_norm = jnp.sqrt(jnp.sum(late[:, 1]))
    factor = CLIP_NORM / jnp.maximum(grad_norm, CLIP_NORM)
    new = [
        adamw(block_weights, first_blocks, second_blocks, block_grad, factor, LEARN_RATE),
        adamw(block_gains, first_gains, second_gains, gain_grad, factor, GAIN_RATE),
        adamw(entry_table, first_entry, second_entry, entry_grad, factor, LEARN_RATE),
        adamw(head_weights, first_head, second_head, head_grad, factor, LEARN_RATE),
        adamw(head_biases, first_biases, second_biases, bias_grad, factor, LEARN_RATE),
        adamw(head_edges, first_edges, second_edges, edge_grad, factor, LEARN_RATE),
    ]
    return tuple(new[i][k] for k in range(3) for i in range(6)) + (loss_sum, weight_total, grad_norm)


def solution(mesh):
    rows = [P(AXES, None, None), P(AXES, None), P(AXES), P(AXES, None), P(AXES, None), P(AXES, None)]
    state = [
        P(None, AXES, None), P(None, None, AXES), P(None, AXES),
        P(None, AXES, None), P(None, AXES), P(None, AXES),
    ]
    return jax.shard_map(
        functools.partial(on_device, dict(mesh.shape)),
        mesh=mesh,
        in_specs=tuple(rows + state * 3),
        out_specs=tuple(state * 3 + [P(), P(), P()]),
        check_vma=False,
    )
```

```python
import functools
import math

import jax
import jax.numpy as jnp
from jax import lax
from jax.experimental import pallas as pl
from jax.experimental.pallas import tpu as pltpu
from jax.sharding import PartitionSpec as P

D = 768
HEADS = 12
HD = 64
FF = 3072
HW = 1024
CH = 16
FREQ = 256
LAT = 256
BUF = 64
HB = 2
COPIES = 4
TSTEPS = 1000
ADAM_STEP = 5
SEQ = 320

BETA_ONE = 0.5
BETA_TWO = 0.5
LEARN_RATE = 0.03
GAIN_RATE = 0.3
DECAY_RATE = 0.02
ADAM_EPS = 1e-08
CLIP_NORM = 0.002
NORM_EPS = 1e-06
AXES = ("dp", "fsdp")
MESH_IDS = pl.DeviceIdType.MESH


def rs_kernel(nz, row_count, width, jobs, extra_count, *refs):
    job_count = len(jobs)
    x_refs, y_refs = refs[:job_count], refs[job_count : 2 * job_count]
    position = 2 * job_count
    extra_ref = None
    if extra_count:
        extra_ref = refs[position]
        position += 1
    out_ref = refs[position]
    (
        x_buf, y_buf, whole, land_core, first, land_first, second, land_second,
        last, last_low, land_last,
        load_sem, core_send, core_recv, first_send, first_recv, second_send, second_recv,
        last_send, last_recv, credit,
    ) = refs[position + 1 :]
    dp, z = lax.axis_index("dp"), lax.axis_index("fsdp")
    core, xb, yb = lax.rem(dp, 2), lax.rem(dp // 2, 2), dp // 4
    group = row_count // 8
    part = group // nz
    starts, total = [], 0
    for _, columns in jobs:
        starts.append(total)
        total += columns // width
    computed = total
    total += extra_count

    core_peer = (dp + 1 - 2 * core, z)
    x_step, y_step = 2 - 4 * xb, 4 - 8 * yb
    z_peers = [(dp, lax.rem(z + s, nz)) for s in range(1, nz)]
    barrier = pltpu.get_barrier_semaphore()
    for peer in [core_peer, (dp + x_step, z), (dp + y_step, z)] + z_peers:
        pl.semaphore_signal(barrier, inc=1, device_id=peer, device_id_type=MESH_IDS)
    pl.semaphore_wait(barrier, 2 + nz)

    def loads(x_ref, y_ref, column, slot):
        return (
            pltpu.make_async_copy(x_ref, x_buf.at[slot], load_sem.at[0, slot]),
            pltpu.make_async_copy(
                y_ref.at[:, pl.ds(pl.multiple_of(column, 128), width)], y_buf.at[slot], load_sem.at[1, slot]
            ),
        )

    def prefetch(g):
        for number, (_, columns) in enumerate(jobs):
            start, stop = starts[number], starts[number] + columns // width

            @pl.when((g >= start) & (g < stop))
            def _():
                for copy in loads(x_refs[number], y_refs[number], (g - start) * width, lax.rem(g, 2)):
                    copy.start()

    def core_copy(g):
        return pltpu.make_async_remote_copy(
            src_ref=whole.at[lax.rem(g, 2), 1 - core],
            dst_ref=land_core.at[lax.rem(g, 4)],
            send_sem=core_send.at[lax.rem(g, 2)],
            recv_sem=core_recv.at[lax.rem(g, 4)],
            device_id=core_peer,
            device_id_type=MESH_IDS,
        )

    def first_copy(g):
        p = lax.rem(g, 2)
        mine = (1 - p) * xb + p * yb
        return pltpu.make_async_remote_copy(
            src_ref=first.at[lax.rem(g, 3), 1 - mine],
            dst_ref=land_first.at[g],
            send_sem=first_send.at[lax.rem(g, 3)],
            recv_sem=first_recv.at[g],
            device_id=(dp + (1 - p) * x_step + p * y_step, z),
            device_id_type=MESH_IDS,
        )

    def second_copy(g):
        p = lax.rem(g, 2)
        mine = (1 - p) * yb + p * xb
        return pltpu.make_async_remote_copy(
            src_ref=second.at[lax.rem(g, 3), 1 - mine],
            dst_ref=land_second.at[g],
            send_sem=second_send.at[lax.rem(g, 3)],
            recv_sem=second_recv.at[g],
            device_id=(dp + (1 - p) * y_step + p * x_step, z),
            device_id_type=MESH_IDS,
        )

    def last_copies(g):
        return [
            pltpu.make_async_remote_copy(
                src_ref=last_low.at[lax.rem(g, 3), lax.rem(z + s, nz)],
                dst_ref=land_last.at[g, s - 1],
                send_sem=last_send.at[lax.rem(g, 3), s - 1],
                recv_sem=last_recv.at[g, s - 1],
                device_id=z_peers[s - 1],
                device_id_type=MESH_IDS,
            )
            for s in range(1, nz)
        ]

    low_rows, low_width = last_low.shape[2:]
    folds = width // low_width

    def fold(block):
        return jnp.concatenate([block[:, k * low_width : (k + 1) * low_width] for k in range(folds)], 0)

    def stage_core(g):
        slot = lax.rem(g, 2)

        @pl.when(g >= 2)
        def _():
            core_copy(g - 2).wait_send()

        def put(number, value):
            yx, c = number // 2, number % 2
            whole[slot, c, yx] = value

        @pl.when(g < computed)
        def _():
            for copy in loads(x_refs[0], y_refs[0], 0, slot):
                copy.wait()
            for number in range(8):
                put(number, lax.dot_general(
                    x_buf[slot, :, pl.ds(number * group, group)], y_buf[slot],
                    (((0,), (0,)), ((), ())), preferred_element_type=jnp.float32,
                ).astype(jnp.bfloat16))

        if extra_count:
            @pl.when(g >= computed)
            def _():
                for number in range(8):
                    put(number, extra_ref[g - computed, pl.ds(number * group, group), :])

        @pl.when(g >= 4)
        def _():
            pl.semaphore_wait(credit, 1)
        core_copy(g).start()

    def stage_first(g):
        p = lax.rem(g, 2)

        @pl.when(g >= 3)
        def _():
            first_copy(g - 3).wait_send()
        core_copy(g).wait_recv()
        for f in range(2):
            for s in range(2):
                yx = (1 - p) * (2 * s + f) + p * (2 * f + s)
                first[lax.rem(g, 3), f, s] = (
                    whole[lax.rem(g, 2), core, yx].astype(jnp.float32)
                    + land_core[lax.rem(g, 4), yx].astype(jnp.float32)
                ).astype(jnp.bfloat16)

        @pl.when(g < total - 4)
        def _():
            pl.semaphore_signal(credit, inc=1, device_id=core_peer, device_id_type=MESH_IDS)
        first_copy(g).start()

    def stage_second(g):
        p = lax.rem(g, 2)
        mine = (1 - p) * xb + p * yb

        @pl.when(g >= 3)
        def _():
            second_copy(g - 3).wait_send()
        first_copy(g).wait_recv()
        for s in range(2):
            second[lax.rem(g, 3), s] = (
                first[lax.rem(g, 3), mine, s].astype(jnp.float32) + land_first[g, s].astype(jnp.float32)
            ).astype(jnp.bfloat16)
        second_copy(g).start()

    def stage_last(g):
        p = lax.rem(g, 2)
        mine = (1 - p) * yb + p * xb

        @pl.when(g >= 3)
        def _():
            for copy in last_copies(g - 3):
                copy.wait_send()
        second_copy(g).wait_recv()
        summed = second[lax.rem(g, 3), mine].astype(jnp.float32) + land_second[g].astype(jnp.float32)
        for k in range(nz):
            block = fold(summed[k * part : (k + 1) * part])
            last[lax.rem(g, 3), k] = block
            last_low[lax.rem(g, 3), k] = block.astype(jnp.bfloat16)
        for copy in last_copies(g):
            copy.start()

    def stage_out(g):
        for copy in last_copies(g):
            copy.wait_recv()
        value = last[lax.rem(g, 3), z]
        for s in range(1, nz):
            value = value + land_last[g, s - 1].astype(jnp.float32)
        for k in range(folds):
            out_ref[g, :, pl.ds(k * low_width, low_width)] = value[k * part : (k + 1) * part]

    lags = (0, 1, 3, 5, 7)
    prefetch(0)

    @pl.loop(0, total + lags[-1])
    def _(i):
        for stage, lag in zip((stage_out, stage_last, stage_second, stage_first), lags[:0:-1]):
            @pl.when((i >= lag) & (i < total + lag))
            def _():
                stage(i - lag)

        @pl.when(i + 1 < computed)
        def _():
            prefetch(i + 1)

        @pl.when(i < total)
        def _():
            stage_core(i)

    for g in range(max(total - 2, 0), total):
        core_copy(g).wait_send()
    for g in range(max(total - 3, 0), total):
        first_copy(g).wait_send()
        second_copy(g).wait_send()
        for copy in last_copies(g):
            copy.wait_send()


def reduce_products(pairs, extras, row_count, width, low_shape, nz, collective_id):
    bf, tokens = jnp.bfloat16, pairs[0][0].shape[0]
    group, part = row_count // 8, row_count // 8 // nz
    jobs = [(x.shape[1], y.shape[1]) for x, y in pairs]
    total = sum(columns // width for _, columns in jobs)
    extra_count = 0 if extras is None else extras.shape[0]
    total += extra_count
    low_rows, low_width = low_shape
    dma, reg = pltpu.SemaphoreType.DMA, pltpu.SemaphoreType.REGULAR
    operands = [x for x, _ in pairs] + [y for _, y in pairs]
    specs = [pl.BlockSpec(memory_space=pl.ANY)] * len(operands)
    if extra_count:
        operands.append(extras)
        specs.append(pl.BlockSpec(memory_space=pltpu.VMEM))
    return pl.pallas_call(
        functools.partial(rs_kernel, nz, row_count, width, jobs, extra_count),
        out_shape=jax.ShapeDtypeStruct((total, part, width), jnp.float32),
        in_specs=specs,
        out_specs=pl.BlockSpec(memory_space=pltpu.VMEM),
        scratch_shapes=[
            pltpu.VMEM((2, tokens, row_count), bf),
            pltpu.VMEM((2, tokens, width), bf),
            pltpu.VMEM((2, 2, 4, group, width), bf),
            pltpu.VMEM((4, 4, group, width), bf),
            pltpu.VMEM((3, 2, 2, group, width), bf),
            pltpu.VMEM((total, 2, group, width), bf),
            pltpu.VMEM((3, 2, group, width), bf),
            pltpu.VMEM((total, group, width), bf),
            pltpu.VMEM((3, nz, low_rows, low_width), jnp.float32),
            pltpu.VMEM((3, nz, low_rows, low_width), bf),
            pltpu.VMEM((total, nz - 1, low_rows, low_width), bf),
            dma((2, 2)), dma((2,)), dma((4,)), dma((3,)), dma((total,)), dma((3,)), dma((total,)),
            dma((3, nz - 1)), dma((total, nz - 1)), reg,
        ],
        compiler_params=pltpu.CompilerParams(
            collective_id=collective_id, has_side_effects=True, vmem_limit_bytes=56 * 2**20
        ),
    )(*operands)


def ag_kernel(nz, chunks, source_count, *refs):
    sources, refs = refs[:source_count], refs[source_count:]
    result_count = 1 + max(chunk[3] for chunk in chunks)
    results, sems = refs[:result_count], refs[result_count:]
    own_sem, last_send, last_recv, first_send, first_recv, second_send, second_recv, core_send, core_recv = sems
    dp, z = lax.axis_index("dp"), lax.axis_index("fsdp")
    core, xb, yb = lax.rem(dp, 2), lax.rem(dp // 2, 2), dp // 4
    core_peer = (dp + 1 - 2 * core, z)
    x_peer, y_peer = (dp + 2 - 4 * xb, z), (dp + 4 - 8 * yb, z)
    z_peers = [(dp, lax.rem(z + s, nz)) for s in range(1, nz)]
    barrier = pltpu.get_barrier_semaphore()
    for peer in [core_peer, x_peer, y_peer] + z_peers:
        pl.semaphore_signal(barrier, inc=1, device_id=peer, device_id_type=MESH_IDS)
    pl.semaphore_wait(barrier, 2 + nz)

    def remote(source, target, send, recv, peer):
        return pltpu.make_async_remote_copy(
            src_ref=source, dst_ref=target, send_sem=send, recv_sem=recv, device_id=peer, device_id_type=MESH_IDS
        )

    def source_of(k):
        source, index, column, _, _, width = chunks[k]
        ref = sources[source] if index is None else sources[source].at[index]
        return ref.at[:, pl.ds(column, width)]

    def result_of(k):
        _, _, _, result, column, width = chunks[k]
        return results[result].at[:, :, :, :, :, pl.ds(column, width)]

    def own(k):
        return pltpu.make_async_copy(source_of(k), result_of(k).at[yb, xb, core, z], own_sem.at[k])

    def z_copies(k):
        return [
            remote(source_of(k), result_of(k).at[yb, xb, core, z], last_send.at[k, s], last_recv.at[k, s], z_peers[s])
            for s in range(nz - 1)
        ]

    def first(k):
        ref = result_of(k).at[yb, xb, core]
        return remote(ref, ref, first_send.at[k], first_recv.at[k], y_peer if k % 2 else x_peer)

    def second(k):
        ref = result_of(k).at[:, xb, core] if k % 2 else result_of(k).at[yb, :, core]
        return remote(ref, ref, second_send.at[k], second_recv.at[k], x_peer if k % 2 else y_peer)

    def across(k):
        ref = result_of(k).at[:, :, core]
        return remote(ref, ref, core_send.at[k], core_recv.at[k], core_peer)

    total = len(chunks)
    for i in range(total + 6):
        k = i - 6
        if k >= 0:
            second(k).wait_recv()
            across(k).start()
        k = i - 4
        if 0 <= k < total:
            first(k).wait_recv()
            second(k).start()
        k = i - 2
        if 0 <= k < total:
            own(k).wait()
            for copy in z_copies(k):
                copy.wait_recv()
            first(k).start()
        if i < total:
            own(i).start()
            for copy in z_copies(i):
                copy.start()
    for k in range(total):
        for copy in z_copies(k) + [first(k), second(k), across(k)]:
            copy.wait_send()
        across(k).wait_recv()


def gather_rows(sources, chunks, shapes, nz, collective_id):
    dma = pltpu.SemaphoreType.DMA
    total = len(chunks)
    return pl.pallas_call(
        functools.partial(ag_kernel, nz, chunks, len(sources)),
        out_shape=[jax.ShapeDtypeStruct((2, 2, 2, nz, *shape), jnp.bfloat16) for shape in shapes],
        in_specs=[pl.BlockSpec(memory_space=pl.ANY)] * len(sources),
        out_specs=[pl.BlockSpec(memory_space=pl.ANY)] * len(shapes),
        scratch_shapes=[
            dma((total,)), dma((total, nz - 1)), dma((total, nz - 1)),
            dma((total,)), dma((total,)), dma((total,)), dma((total,)), dma((total,)), dma((total,)),
        ],
        compiler_params=pltpu.CompilerParams(
            collective_id=collective_id, has_side_effects=True, vmem_limit_bytes=4 * 2**20
        ),
    )(*sources)


def exchange_kernel(dp_count, nz, in_ref, out_ref, send_sem, recv_sem):
    devices = dp_count * nz
    me = lax.axis_index("dp") * nz + lax.axis_index("fsdp")

    def peer(step):
        there = lax.rem(me + step, devices)
        return (there // nz, lax.rem(there, nz))

    barrier = pltpu.get_barrier_semaphore()

    @pl.loop(1, devices)
    def _(step):
        pl.semaphore_signal(barrier, inc=1, device_id=peer(step), device_id_type=MESH_IDS)

    pl.semaphore_wait(barrier, devices - 1)

    def copy(step):
        return pltpu.make_async_remote_copy(
            src_ref=in_ref,
            dst_ref=out_ref.at[me],
            send_sem=send_sem.at[step - 1],
            recv_sem=recv_sem.at[step - 1],
            device_id=peer(step),
            device_id_type=MESH_IDS,
        )

    @pl.loop(1, devices)
    def _(step):
        copy(step).start()

    out_ref[me] = in_ref[...]

    @pl.loop(1, devices)
    def _(step):
        copy(step).wait()


def exchange(values, dp_count, nz, collective_id):
    devices = dp_count * nz
    tile = jnp.broadcast_to(jnp.pad(values, (0, 128 - values.shape[0])), (8, 128))
    out = pl.pallas_call(
        functools.partial(exchange_kernel, dp_count, nz),
        out_shape=jax.ShapeDtypeStruct((devices, 8, 128), jnp.float32),
        in_specs=[pl.BlockSpec(memory_space=pltpu.VMEM)],
        out_specs=pl.BlockSpec(memory_space=pltpu.VMEM),
        scratch_shapes=[pltpu.SemaphoreType.DMA((devices - 1,)), pltpu.SemaphoreType.DMA((devices - 1,))],
        compiler_params=pltpu.CompilerParams(
            collective_id=collective_id, has_side_effects=True, vmem_limit_bytes=4 * 2**20
        ),
    )(tile)
    return out[:, 0, : values.shape[0]]


def dot_plain(left, right):
    return jnp.dot(left, right, preferred_element_type=jnp.float32)


def dot_left(left, right):
    return lax.dot_general(
        left, right, (((0,), (0,)), ((), ())), preferred_element_type=jnp.float32
    )


def dot_right(left, right):
    return lax.dot_general(
        left, right, (((1,), (1,)), ((), ())), preferred_element_type=jnp.float32
    )


KEPT = (
    ("normed", D, jnp.bfloat16), ("packed", 3 * D, jnp.bfloat16), ("mixed", D, jnp.bfloat16),
    ("second", D, jnp.bfloat16), ("upper", FF, jnp.bfloat16), ("inner", FF, jnp.float32),
    ("norm_one", D, jnp.float32), ("norm_two", D, jnp.float32), ("inv_one", 128, jnp.float32),
    ("inv_two", 128, jnp.float32),
)
KEPT_INDEX = {name: k for k, (name, _, _) in enumerate(KEPT)}
BACK = (("back_packed", 3 * D), ("back_attn", D), ("back_inner", FF), ("back_branch", D))
GELU_SCALE = math.sqrt(2.0 / math.pi)


def in_nn(x, w):
    return jnp.dot(x, w, preferred_element_type=jnp.float32)


def in_nt(x, w):
    return lax.dot_general(x, w, (((1,), (1,)), ((), ())), preferred_element_type=jnp.float32)


def in_tn(x, w):
    return lax.dot_general(x, w, (((0,), (0,)), ((), ())), preferred_element_type=jnp.float32)


def softmax_rows(scores):
    raised = jnp.exp(scores - jnp.max(scores, -1, keepdims=True))
    return raised * (1.0 / jnp.sum(raised, -1, keepdims=True))


def low_half():
    return lax.broadcasted_iota(jnp.int32, (SEQ, 2 * HD), 1) < HD


def forward_pieces(weights, entry, select_ref, mask_ref, hidden, kept, top_ref, need, leave):
    bf = jnp.bfloat16
    pieces = []
    gain = lambda row: in_nt(select_ref[2 * SEQ :, :], entry[...])[row : row + 1, :]

    def start():
        need(entry)
        hidden[...] = in_nt(select_ref[:SEQ, :], entry[...])
    pieces.append(start)

    def norm(layer, which):
        value = hidden[...]
        centred = value - jnp.mean(value, -1, keepdims=True)
        inv = lax.rsqrt(jnp.mean(centred * centred, -1, keepdims=True) + NORM_EPS)
        n = centred * inv
        names = ("norm_one", "inv_one", "normed") if which == 0 else ("norm_two", "inv_two", "second")
        kept[names[0]][layer] = n
        kept[names[1]][layer] = jnp.broadcast_to(inv, (SEQ, 128))
        kept[names[2]][layer] = (n * gain(2 * layer + which)).astype(bf)
        for name in names:
            leave(layer, name)

    def project(layer):
        norm(layer, 0)
        need(weights[4 * layer])
        kept["packed"][layer] = in_nn(kept["normed"][layer], weights[4 * layer][...]).astype(bf)
        leave(layer, "packed")

    def attend(layer, pair):
        packed = kept["packed"]
        cut = lambda k: packed[layer, :, k * D + pair * 2 * HD : k * D + (pair + 1) * 2 * HD]
        q, k, v = cut(0), cut(1), cut(2)
        low = low_half()
        parts = []
        for side in range(2):
            one = jnp.where(low if side == 0 else ~low, q, jnp.zeros((), bf))
            scores = in_nt(one, k) * HD ** (-0.5)
            if layer == 0:
                scores = jnp.where(mask_ref[...] > 0, scores, -1e30)
            parts.append(in_nn(softmax_rows(scores).astype(bf), v))
        kept["mixed"][layer, :, pair * 2 * HD : (pair + 1) * 2 * HD] = jnp.where(low, parts[0], parts[1]).astype(bf)

    def close(layer):
        leave(layer, "mixed")
        need(weights[4 * layer + 1])
        hidden[...] += in_nn(kept["mixed"][layer], weights[4 * layer + 1][...])
        norm(layer, 1)
        need(weights[4 * layer + 2])

    def up(layer, part, parts):
        columns = slice(part * FF // parts, (part + 1) * FF // parts)
        inner = in_nn(kept["second"][layer], weights[4 * layer + 2][:, columns])
        kept["inner"][layer, :, columns] = inner
        kept["upper"][layer, :, columns] = (
            0.5 * inner * (1.0 + jnp.tanh(GELU_SCALE * (inner + 0.044715 * inner * inner * inner)))
        ).astype(bf)

    def down(layer):
        leave(layer, "inner")
        leave(layer, "upper")
        need(weights[4 * layer + 3])
        hidden[...] += in_nt(kept["upper"][layer], weights[4 * layer + 3][...])

    def between():
        keep = mask_ref[...].reshape(1, SEQ)
        hidden[...] = hidden[...] * keep_column(keep) + in_nt(select_ref[SEQ : 2 * SEQ, :], entry[...])

    def keep_column(keep):
        return jnp.transpose(jnp.broadcast_to(keep, (128, SEQ)))[:, :1]

    for layer in range(2):
        pieces.append(functools.partial(project, layer))
        for pair in range(HEADS // 2):
            pieces.append(functools.partial(attend, layer, pair))
        pieces.append(functools.partial(close, layer))
        for part in range(3):
            pieces.append(functools.partial(up, layer, part, 3))
        pieces.append(functools.partial(down, layer))
        if layer == 0:
            pieces.append(between)

    def finish():
        top_ref[...] = hidden[BUF:, :].astype(bf)
    pieces.append(finish)
    return pieces


def forward_kernel(*refs):
    entry_hbm, weight_hbm, (select_ref, mask_ref), refs = refs[0], refs[1:9], refs[9:11], refs[11:]
    kept_hbm, (top_ref,), refs = refs[: len(KEPT)], refs[len(KEPT) : len(KEPT) + 1], refs[len(KEPT) + 1 :]
    entry, weights, kept_refs, (hidden, weight_sem, kept_sem) = refs[0], refs[1:9], refs[9 : 9 + len(KEPT)], refs[9 + len(KEPT) :]
    kept = {name: ref for (name, _, _), ref in zip(KEPT, kept_refs)}
    local = [(entry_hbm, entry)] + list(zip(weight_hbm, weights))
    fetches = {id(ref): pltpu.make_async_copy(hbm, ref, weight_sem.at[k]) for k, (hbm, ref) in enumerate(local)}
    for copy in fetches.values():
        copy.start()
    leaving = []

    def leave(layer, name):
        k = KEPT_INDEX[name]
        copy = pltpu.make_async_copy(kept_refs[k].at[layer], kept_hbm[k].at[layer], kept_sem.at[layer, k])
        copy.start()
        leaving.append(copy)

    for piece in forward_pieces(
        weights, entry, select_ref, mask_ref, hidden, kept, top_ref, lambda ref: fetches[id(ref)].wait(), leave
    ):
        piece()
    for copy in leaving:
        copy.wait()


def trunk_forward(entry, weights, select, mask):
    bf, f32 = jnp.bfloat16, jnp.float32
    vmem, hbm = pl.BlockSpec(memory_space=pltpu.VMEM), pl.BlockSpec(memory_space=pl.ANY)
    shapes = [(2, SEQ, columns) for _, columns, _ in KEPT]
    outs = pl.pallas_call(
        forward_kernel,
        out_shape=[jax.ShapeDtypeStruct(s, dtype) for s, (_, _, dtype) in zip(shapes, KEPT)]
        + [jax.ShapeDtypeStruct((LAT, D), bf)],
        in_specs=[hbm] * 9 + [vmem] * 2,
        out_specs=[hbm] * len(KEPT) + [vmem],
        scratch_shapes=[pltpu.VMEM(w.shape, bf) for w in [entry] + weights]
        + [pltpu.VMEM(s, dtype) for s, (_, _, dtype) in zip(shapes, KEPT)]
        + [pltpu.VMEM((SEQ, D), f32), pltpu.SemaphoreType.DMA((9,)), pltpu.SemaphoreType.DMA((2, len(KEPT)))],
        compiler_params=pltpu.CompilerParams(vmem_limit_bytes=60 * 2**20),
    )(entry, *weights, select, mask)
    return outs[-1], outs[:-1]


def backward_pieces(layer, weights, gain, mask_ref, hidden, middle, kept, back, gain_grad, need, leave):
    bf = jnp.bfloat16
    w_qkv, w_out, w_up, w_down = weights
    pieces = []

    def norm_step(upstream, n, inv):
        return inv * (
            upstream - jnp.mean(upstream, -1, keepdims=True) - n * jnp.mean(upstream * n, -1, keepdims=True)
        )

    def branch():
        back["back_branch"][...] = hidden[...].astype(bf)
        leave("back_branch")
        need(w_down, "inner")

    def widen(part, parts):
        columns = slice(part * FF // parts, (part + 1) * FF // parts)
        up = in_nn(back["back_branch"][...], w_down[:, columns])
        x = kept["inner"][:, columns]
        t = jnp.tanh(GELU_SCALE * (x + 0.044715 * x * x * x))
        slope = 0.5 * (1.0 + t) + 0.5 * x * (1.0 - t * t) * (GELU_SCALE * (1.0 + 3.0 * 0.044715 * x * x))
        back["back_inner"][:, columns] = (slope * up).astype(bf)

    def narrow():
        leave("back_inner")
        need(w_up, "norm_two", "inv_two")
        value = in_nt(back["back_inner"][...], w_up[...])
        n = kept["norm_two"][...]
        gain_grad[2 * layer + 1 : 2 * layer + 2, :] = jnp.sum(value * n, 0, keepdims=True)
        middle[...] = hidden[...] + norm_step(value * gain(2 * layer + 1), n, kept["inv_two"][:, :1])
        back["back_attn"][...] = middle[...].astype(bf)
        leave("back_attn")

    def unmix():
        need(w_out, "packed")
        back["mixed"][...] = in_nt(back["back_attn"][...], w_out[...]).astype(bf)

    def attend(pair):
        low = low_half()
        at = lambda k: slice(k * D + pair * 2 * HD, k * D + (pair + 1) * 2 * HD)
        q, k, v = (kept["packed"][:, at(i)] for i in range(3))
        up = back["mixed"][:, at(0)]
        zero = jnp.zeros((), bf)
        parts = []
        for side in range(2):
            mine = low if side == 0 else ~low
            scores = in_nt(jnp.where(mine, q, zero), k) * HD ** (-0.5)
            if layer == 0:
                scores = jnp.where(mask_ref[...] > 0, scores, -1e30)
            attention = softmax_rows(scores)
            back_attention = in_nt(jnp.where(mine, up, zero), v)
            back_values = in_tn(attention.astype(bf), up)
            back_scores = (
                attention * (back_attention - jnp.sum(back_attention * attention, -1, keepdims=True))
            ).astype(bf)
            parts.append((in_nn(back_scores, k) * HD ** (-0.5), in_tn(back_scores, q) * HD ** (-0.5), back_values))
        for i in range(3):
            back["back_packed"][:, at(i)] = jnp.where(low, parts[0][i], parts[1][i]).astype(bf)

    def close():
        leave("back_packed")
        need(w_qkv, "norm_one", "inv_one")
        value = in_nt(back["back_packed"][...], w_qkv[...])
        n = kept["norm_one"][...]
        gain_grad[2 * layer : 2 * layer + 1, :] = jnp.sum(value * n, 0, keepdims=True)
        hidden[...] = middle[...] + norm_step(value * gain(2 * layer), n, kept["inv_one"][:, :1])

    pieces.append(branch)
    for part in range(3):
        pieces.append(functools.partial(widen, part, 3))
    pieces += [narrow, unmix]
    for pair in range(HEADS // 2):
        pieces.append(functools.partial(attend, pair))
    pieces.append(close)
    return pieces


BACK_KEPT = ("packed", "inner", "norm_one", "norm_two", "inv_one", "inv_two")


def backward_kernel(*refs):
    entry_ref, weight_hbm, (select_ref, mask_ref, top_ref), refs = refs[0], refs[1:9], refs[9:12], refs[12:]
    kept_hbm, refs = refs[: len(BACK_KEPT)], refs[len(BACK_KEPT) :]
    back_hbm, small_ref, refs = refs[: len(BACK)], refs[len(BACK)], refs[len(BACK) + 1 :]
    weights, refs = refs[:4], refs[4:]
    kept_refs, refs = refs[: len(BACK_KEPT)], refs[len(BACK_KEPT) :]
    back_refs, (mixed, hidden, middle, decoder, gain_grad, weight_sem, kept_sem, back_sem) = refs[: len(BACK)], refs[len(BACK) :]
    bf = jnp.bfloat16
    gains = lambda row: in_nt(select_ref[2 * SEQ :, :], entry_ref[...])[row : row + 1, :]
    hidden[...] = top_ref[...]
    gain_grad[...] = jnp.zeros_like(gain_grad)
    back = {name: ref for (name, _), ref in zip(BACK, back_refs)}
    back["mixed"] = mixed
    order = [3, 2, 1, 0]
    kept_order = {3: ["inner"], 2: ["norm_two", "inv_two"], 1: ["packed"], 0: ["norm_one", "inv_one"]}

    def fetches(layer):
        moves = {}
        for k in order:
            moves[id(weights[k])] = pltpu.make_async_copy(weight_hbm[4 * layer + k], weights[k], weight_sem.at[k])
            for name in kept_order[k]:
                i = BACK_KEPT.index(name)
                moves[name] = pltpu.make_async_copy(kept_hbm[i].at[layer], kept_refs[i], kept_sem.at[i])
        return moves

    moves = fetches(1)
    for copy in moves.values():
        copy.start()
    for layer in (1, 0):
        leaving = []

        def need(*names):
            for name in names:
                moves[name if isinstance(name, str) else id(name)].wait()

        def leave(name):
            k = [n for n, _ in BACK].index(name)
            copy = pltpu.make_async_copy(back_refs[k], back_hbm[k].at[layer], back_sem.at[k])
            copy.start()
            leaving.append(copy)

        later = fetches(0) if layer == 1 else {}
        kept = {name: ref for name, ref in zip(BACK_KEPT, kept_refs)}
        for piece in backward_pieces(
            layer, weights, gains, mask_ref, hidden, middle, kept, back, gain_grad, need, leave
        ):
            piece()
            if layer == 1:
                name = getattr(piece, "__name__", "")
                if name == "narrow":
                    free = [id(weights[3]), "inner", id(weights[2]), "norm_two", "inv_two"]
                elif name == "unmix":
                    free = [id(weights[1])]
                elif name == "close":
                    free = ["packed", id(weights[0]), "norm_one", "inv_one"]
                else:
                    free = []
                for key in free:
                    later[key].start()
        for copy in leaving:
            copy.wait()
        if layer == 1:
            moves = later
            decoder[...] = hidden[...].astype(bf)
            keep = jnp.transpose(jnp.broadcast_to(mask_ref[...], (128, SEQ)))[:, :1]
            hidden[...] = hidden[...] * keep
    small_ref[...] = (
        in_tn(hidden[...].astype(bf), select_ref[:SEQ, :])
        + in_tn(decoder[...], select_ref[SEQ : 2 * SEQ, :])
        + in_tn(gain_grad[...].astype(bf), select_ref[2 * SEQ :, :])
    ).astype(bf)


def trunk_backward(entry, weights, select, mask, back_top, kept):
    bf, f32 = jnp.bfloat16, jnp.float32
    vmem, hbm = pl.BlockSpec(memory_space=pltpu.VMEM), pl.BlockSpec(memory_space=pl.ANY)
    kept_in = [kept[KEPT_INDEX[name]] for name in BACK_KEPT]
    outs = pl.pallas_call(
        backward_kernel,
        out_shape=[jax.ShapeDtypeStruct((2, SEQ, columns), bf) for _, columns in BACK]
        + [jax.ShapeDtypeStruct((D, TRUNK_WIDTH), bf)],
        in_specs=[vmem] + [hbm] * 8 + [vmem] * 3 + [hbm] * len(BACK_KEPT),
        out_specs=[hbm] * len(BACK) + [vmem],
        scratch_shapes=[pltpu.VMEM(w.shape, bf) for w in weights[:4]]
        + [pltpu.VMEM(a.shape[1:], a.dtype) for a in kept_in]
        + [pltpu.VMEM((SEQ, columns), bf) for _, columns in BACK]
        + [
            pltpu.VMEM((SEQ, D), bf), pltpu.VMEM((SEQ, D), f32), pltpu.VMEM((SEQ, D), f32), pltpu.VMEM((SEQ, D), bf),
            pltpu.VMEM((16, D), f32),
            pltpu.SemaphoreType.DMA((4,)), pltpu.SemaphoreType.DMA((len(BACK_KEPT),)),
            pltpu.SemaphoreType.DMA((len(BACK),)),
        ],
        compiler_params=pltpu.CompilerParams(vmem_limit_bytes=60 * 2**20),
    )(entry, *weights, select, mask, back_top, *kept_in)
    back = dict(zip([name for name, _ in BACK], outs[:-1]))
    pairs = []
    for layer in range(2):
        part = lambda name: kept[KEPT_INDEX[name]][layer]
        pairs += [
            (part("normed"), back["back_packed"][layer]), (part("mixed"), back["back_attn"][layer]),
            (part("second"), back["back_inner"][layer]), (back["back_branch"][layer], part("upper")),
        ]
    return pairs, outs[-1]


ROWS_AT_ONCE = 192
HEAD_WEIGHTS = ((HW, 3 * HW), (HW, HW), (HW, HW)) * HB + (
    (HW, D), (HW, HW), (HW, HW), (HW, HW), (HW, FREQ), (HW, 128), (HW, 128)
)
HEAD_LEFT = (3, 1, 1, 1, 1) * HB + (1, 1, 1, 1, 1, 1, 1, 1)


def sigmoid(x):
    return 0.5 + 0.5 * jnp.tanh(0.5 * x)


def head_kernel(tokens, *refs):
    (embed_ref, noisy_ref, target_ref, grad_col_ref, loss_col_ref, bias_ref, cond_ref), refs = refs[:7], refs[7:]
    count = len(HEAD_WEIGHTS)
    block_hbm, edge_hbm, refs = refs[:HB], refs[HB : HB + 7], refs[HB + 7 :]
    weight_hbm = [
        block.at[:, pl.ds(column, width)]
        for block in block_hbm
        for column, width in ((0, 3 * HW), (3 * HW, HW), (4 * HW, HW))
    ] + list(edge_hbm)
    left_hbm, refs = refs[: len(HEAD_LEFT)], refs[len(HEAD_LEFT) :]
    (pred_ref, back_cond_ref, back_token_ref, bias_grad_ref, loss_ref), refs = refs[:5], refs[5:]
    weights, refs = refs[:count], refs[count:]
    left, refs = refs[: len(HEAD_LEFT)], refs[len(HEAD_LEFT) :]
    (
        time_inner, conditioning, projected, cond_sum, stream, back_silu, t0, t1, t2,
        scale1, normed, inner, gate, branch, inverse, weight_sem, left_sem,
    ) = refs
    cond_t, time_two_t, shift_t, scale_t, time_one_t, in_t, out_t = weights[3 * HB :]
    per_block = 5
    silu_cond, time_hidden, back_time, back_time_inner, back_shift, back_scale, final_low, back_low = left[
        per_block * HB :
    ]
    bf = jnp.bfloat16

    def fetch(k):
        return pltpu.make_async_copy(weight_hbm[k], weights[k], weight_sem.at[k])

    order = [3 * HB, 3 * HB + 4, 3 * HB + 1, 3 * HB + 5]
    for b in range(HB):
        order += [3 * b, 3 * b + 1, 3 * b + 2]
    order += [3 * HB + 2, 3 * HB + 3, 3 * HB + 6]
    for k in order:
        fetch(k).start()

    def nn(x, w):
        return jnp.dot(x, w, preferred_element_type=jnp.float32)

    def nt(x, w):
        return lax.dot_general(x, w, (((1,), (1,)), ((), ())), preferred_element_type=jnp.float32)

    def by_rows(body):
        for i in range(0, tokens, ROWS_AT_ONCE):
            body(slice(i, i + ROWS_AT_ONCE))

    bias_grad_ref[...] = jnp.zeros_like(bias_grad_ref)
    loss_ref[...] = jnp.zeros_like(loss_ref)
    cond_sum[...] = jnp.zeros_like(cond_sum)

    def bias(row):
        return bias_ref[row : row + 1, :]

    def add_bias_grad(row, value):
        bias_grad_ref[row : row + 1, :] += jnp.sum(value.astype(jnp.float32), 0, keepdims=True)

    @pl.loop(0, COPIES)
    def _(c):
        def need(*numbers):
            @pl.when(c == 0)
            def _():
                for k in numbers:
                    fetch(k).wait()

        def leave(k):
            return pltpu.make_async_copy(left[k], left_hbm[k].at[c], left_sem.at[k])

        def room(*numbers):
            @pl.when(c > 0)
            def _():
                for k in numbers:
                    leave(k).wait()

        base = per_block * HB
        room(base, base + 1)
        need(3 * HB)

        @pl.when(c == 0)
        def _():
            projected[...] = nt(cond_ref[...], cond_t[...])

        need(3 * HB + 4, 3 * HB + 1, 3 * HB + 5)
        time_inner[...] = nt(embed_ref[c], time_one_t[...])

        def _(r):
            value = time_inner[r, :] + bias(10)
            time_inner[r, :] = value
            time_hidden[r, :] = (value * sigmoid(value)).astype(bf)
        by_rows(_)
        leave(base + 1).start()
        t0[...] = nt(time_hidden[...], time_two_t[...])
        stream[...] = nt(noisy_ref[c], in_t[...])

        def _(r):
            value = projected[r, :] + (t0[r, :] + bias(11))
            conditioning[r, :] = value
            silu_cond[r, :] = (value * sigmoid(value)).astype(bf)
            stream[r, :] = stream[r, :] + bias(14)
        by_rows(_)
        leave(base).start()

        for b in range(HB):
            w_mod, w_up, w_down = weights[3 * b : 3 * b + 3]
            bm, shaped, back_inner, back_branch, hidden = left[per_block * b : per_block * (b + 1)]
            room(*range(per_block * b, per_block * (b + 1)))
            need(3 * b)
            t0[...] = nn(silu_cond[...], w_mod[:, :HW])
            t1[...] = nn(silu_cond[...], w_mod[:, HW : 2 * HW])
            gate[b] = nn(silu_cond[...], w_mod[:, 2 * HW :])

            def _(r):
                value = stream[r, :]
                centred = value - jnp.mean(value, -1, keepdims=True)
                inv = lax.rsqrt(jnp.mean(centred * centred, -1, keepdims=True) + NORM_EPS)
                n = centred * inv
                s = 1.0 + (t1[r, :] + bias(5 * b + 1))
                inverse[b, r, :] = jnp.broadcast_to(inv, (ROWS_AT_ONCE, 128))
                normed[b, r, :] = n
                scale1[b, r, :] = s
                shaped[r, :] = (n * s + (t0[r, :] + bias(5 * b))).astype(bf)
            by_rows(_)
            leave(per_block * b + 1).start()
            need(3 * b + 1)
            inner[b] = nn(shaped[...], w_up[...])

            def _(r):
                value = inner[b, r, :] + bias(5 * b + 3)
                inner[b, r, :] = value
                hidden[r, :] = (value * sigmoid(value)).astype(bf)
            by_rows(_)
            leave(per_block * b + 4).start()
            need(3 * b + 2)
            branch[b] = nt(hidden[...], w_down[...])

            def _(r):
                value = branch[b, r, :] + bias(5 * b + 4)
                g = gate[b, r, :] + bias(5 * b + 2)
                branch[b, r, :] = value
                gate[b, r, :] = g
                stream[r, :] = stream[r, :] + g * value
            by_rows(_)

        need(3 * HB + 2, 3 * HB + 3, 3 * HB + 6)
        room(*range(base + 2, base + 8))
        t0[...] = nt(silu_cond[...], shift_t[...])
        t1[...] = nt(silu_cond[...], scale_t[...])
        def _(r):
            value = stream[r, :]
            centred = value - jnp.mean(value, -1, keepdims=True)
            inv = lax.rsqrt(jnp.mean(centred * centred, -1, keepdims=True) + NORM_EPS)
            n = centred * inv
            s = 1.0 + (t1[r, :] + bias(13))
            inverse[HB, r, :] = jnp.broadcast_to(inv, (ROWS_AT_ONCE, 128))
            t2[r, :] = n
            t1[r, :] = s
            final_low[r, :] = (n * s + (t0[r, :] + bias(12))).astype(bf)
        by_rows(_)
        leave(base + 6).start()
        difference = nn(final_low[...], out_t[...]) - target_ref[c]
        loss_ref[...] += loss_col_ref[c] * difference * difference
        pred_ref[c] = (grad_col_ref[c] * difference).astype(bf)
        t0[...] = nt(pred_ref[c], out_t[...])

        def _(r):
            back = t0[r, :]
            n = t2[r, :]
            low_shift, low_scale = back.astype(bf), (back * n).astype(bf)
            back_shift[r, :] = low_shift
            back_scale[r, :] = low_scale
            up = back * t1[r, :]
            add_bias_grad(12, low_shift)
            add_bias_grad(13, low_scale)
            stream[r, :] = inverse[HB, r, :1] * (
                up - jnp.mean(up, -1, keepdims=True) - n * jnp.mean(up * n, -1, keepdims=True)
            )
        by_rows(_)
        leave(base + 4).start()
        leave(base + 5).start()
        back_silu[...] = nn(back_shift[...], shift_t[...]) + nn(back_scale[...], scale_t[...])

        for b in reversed(range(HB)):
            w_mod, w_up, w_down = weights[3 * b : 3 * b + 3]
            bm, shaped, back_inner, back_branch, hidden = left[per_block * b : per_block * (b + 1)]

            def _(r):
                back = stream[r, :]
                low = (back * gate[b, r, :]).astype(bf)
                low_gate = (back * branch[b, r, :]).astype(bf)
                back_branch[r, :] = low
                bm[r, 2 * HW :] = low_gate
                add_bias_grad(5 * b + 4, low)
                add_bias_grad(5 * b + 2, low_gate)
            by_rows(_)
            leave(per_block * b + 3).start()
            t0[...] = nn(back_branch[...], w_down[...])

            def _(r):
                value = inner[b, r, :]
                s = sigmoid(value)
                low = (t0[r, :] * (s * (1.0 + value * (1.0 - s)))).astype(bf)
                back_inner[r, :] = low
                add_bias_grad(5 * b + 3, low)
            by_rows(_)
            leave(per_block * b + 2).start()
            t0[...] = nt(back_inner[...], w_up[...])

            def _(r):
                back = t0[r, :]
                n = normed[b, r, :]
                low_shift, low_scale = back.astype(bf), (back * n).astype(bf)
                bm[r, :HW] = low_shift
                bm[r, HW : 2 * HW] = low_scale
                add_bias_grad(5 * b, low_shift)
                add_bias_grad(5 * b + 1, low_scale)
                up = back * scale1[b, r, :]
                stream[r, :] = stream[r, :] + inverse[b, r, :1] * (
                    up - jnp.mean(up, -1, keepdims=True) - n * jnp.mean(up * n, -1, keepdims=True)
                )
            by_rows(_)
            leave(per_block * b).start()
            back_silu[...] += nt(bm[...], w_mod[...])

        def _(r):
            value = conditioning[r, :]
            s = sigmoid(value)
            back = back_silu[r, :] * (s * (1.0 + value * (1.0 - s)))
            low, low_stream = back.astype(bf), stream[r, :].astype(bf)
            cond_sum[r, :] = cond_sum[r, :] + back
            back_time[r, :] = low
            back_low[r, :] = low_stream
            add_bias_grad(11, low)
            add_bias_grad(14, low_stream)
        by_rows(_)
        leave(base + 2).start()
        leave(base + 7).start()
        t0[...] = nn(back_time[...], time_two_t[...])

        def _(r):
            value = time_inner[r, :]
            s = sigmoid(value)
            low = (t0[r, :] * (s * (1.0 + value * (1.0 - s)))).astype(bf)
            back_time_inner[r, :] = low
            add_bias_grad(10, low)
        by_rows(_)
        leave(base + 3).start()

    back_cond_ref[...] = cond_sum[...].astype(bf)
    back_token_ref[...] = nn(back_cond_ref[...], cond_t[...]).astype(bf)
    for k in range(len(HEAD_LEFT)):
        pltpu.make_async_copy(left[k], left_hbm[k].at[COPIES - 1], left_sem.at[k]).wait()


def head_pass(
    blocks, edges, biases, cond_rows, clean_rows, noise_rows, step_rows, weight_rows, weight_total
):
    bf = jnp.bfloat16
    tokens = cond_rows.shape[0]
    half_freq = FREQ // 2
    frequencies = jnp.exp(-math.log(10000.0) * jnp.arange(half_freq, dtype=jnp.float32) / half_freq)
    step_times = step_rows.astype(jnp.float32).T
    angles = step_times[..., None] * frequencies
    time_embed = jnp.concatenate([jnp.cos(angles), jnp.sin(angles)], -1).astype(bf)
    phase_angle = (step_times / TSTEPS + 0.008) / 1.008 * (math.pi / 2)
    keep_part = jnp.cos(phase_angle)[..., None]
    noise_part = jnp.sin(phase_angle)[..., None]
    clean_copies = clean_rows.astype(jnp.float32)[None]
    fresh_noise = noise_rows.astype(jnp.float32).reshape(tokens, COPIES, CH).transpose(1, 0, 2)
    wide = ((0, 0), (0, 0), (0, 128 - CH))
    noisy = jnp.pad((keep_part * clean_copies + noise_part * fresh_noise).astype(bf), wide)
    target = jnp.pad(keep_part * fresh_noise - noise_part * clean_copies, wide)
    by_copy = jnp.broadcast_to(weight_rows.T[..., None], (COPIES, tokens, 128))
    f32 = jnp.float32
    vmem, hbm = pl.BlockSpec(memory_space=pltpu.VMEM), pl.BlockSpec(memory_space=pl.ANY)
    lefts = [(COPIES, tokens, k * HW) for k in HEAD_LEFT]
    units = lambda *lead: pltpu.VMEM((*lead, tokens, HW), f32)
    outs = pl.pallas_call(
        functools.partial(head_kernel, tokens),
        out_shape=[jax.ShapeDtypeStruct(shape, bf) for shape in lefts]
        + [
            jax.ShapeDtypeStruct((COPIES, tokens, 128), bf),
            jax.ShapeDtypeStruct((tokens, HW), bf),
            jax.ShapeDtypeStruct((tokens, D), bf),
            jax.ShapeDtypeStruct((5 * (HB + 1) + 1, HW), f32),
            jax.ShapeDtypeStruct((tokens, 128), f32),
        ],
        in_specs=[vmem] * 7 + [hbm] * (HB + 7),
        out_specs=[hbm] * len(HEAD_LEFT) + [vmem] * 5,
        scratch_shapes=[pltpu.VMEM(shape, bf) for shape in HEAD_WEIGHTS]
        + [pltpu.VMEM((tokens, k * HW), bf) for k in HEAD_LEFT]
        + [units()] * 9
        + [units(HB)] * 5
        + [
            pltpu.VMEM((HB + 1, tokens, 128), f32),
            pltpu.SemaphoreType.DMA((len(HEAD_WEIGHTS),)), pltpu.SemaphoreType.DMA((len(HEAD_LEFT),)),
        ],
        compiler_params=pltpu.CompilerParams(vmem_limit_bytes=60 * 2**20),
    )(
        time_embed, noisy, target, by_copy * (2.0 / (CH * weight_total)), by_copy * (1.0 / CH),
        jnp.pad(biases.reshape(5 * (HB + 1), HW), ((0, 1), (0, 0))), cond_rows,
        *blocks, *edges,
    )
    left = [a.reshape(COPIES * tokens, -1) for a in outs[: len(HEAD_LEFT)]]
    back_pred, back_cond, back_tokens, bias_grad, loss_part = outs[len(HEAD_LEFT) :]
    silu_cond, time_hidden, back_time, back_time_inner, back_shift, back_scale, final_low, back_low = left[5 * HB :]
    pairs = []
    for b in range(HB):
        bm, shaped, back_inner, back_branch, hidden = left[5 * b : 5 * (b + 1)]
        pairs += [(silu_cond, bm), (shaped, back_inner), (back_branch, hidden)]
    pairs += [(back_time, time_hidden), (back_shift, silu_cond), (back_scale, silu_cond)]
    flat = lambda a: a.reshape(COPIES * tokens, -1)
    small = (
        dot_left(back_cond, cond_rows),
        dot_left(back_time_inner, flat(time_embed)),
        dot_left(back_low, flat(noisy))[:, :CH],
        dot_left(final_low, flat(back_pred))[:, :CH],
    )
    bias_grad = bias_grad[: 5 * (HB + 1)].reshape(HB + 1, 5 * HW)
    return (jnp.sum(loss_part), pairs, small, bias_grad, back_tokens)


def adamw(master, first, second, gradient, factor, step_rate):
    clipped = gradient * factor
    first_new = BETA_ONE * first + (1.0 - BETA_ONE) * clipped
    second_new = BETA_TWO * second + (1.0 - BETA_TWO) * clipped * clipped
    mean_hat = first_new / (1.0 - BETA_ONE**ADAM_STEP)
    var_hat = second_new / (1.0 - BETA_TWO**ADAM_STEP)
    updated = master - step_rate * (mean_hat / (jnp.sqrt(var_hat) + ADAM_EPS) + DECAY_RATE * master)
    return (updated, first_new, second_new)


TRUNK_PARTS = (3 * D, D, FF, FF)
HEAD_PARTS = (3 * HW, HW, HW)
EDGE_PARTS = (D, HW, HW, HW, FREQ, 128)
TRUNK_WIDTH = 768
HEAD_WIDTH = 512


def gather_plan(part_sets, limit):
    chunks, shapes = [], []
    for source, index, rows, parts in part_sets:
        column = 0
        for part in parts:
            for k in range(0, part, limit):
                chunks.append((source, index, column + k, len(shapes), k, min(limit, part - k)))
            shapes.append((rows, part))
            column += part
    return chunks, shapes


def plain_gather(sources, chunks, shapes):
    ends = {}
    for source, index, column, result, at, width in chunks:
        start, stop = ends.get(result, (source, index, column, column))[2:]
        ends[result] = (source, index, min(start, column), max(stop, column + width))
    wholes = {}
    results = []
    for number in range(len(shapes)):
        source, index, start, stop = ends[number]
        if (source, index) not in wholes:
            block = sources[source] if index is None else sources[source][index]
            wholes[source, index] = lax.all_gather(block, AXES, axis=0, tiled=True)
        results.append(wholes[source, index][:, start:stop])
    return results


def scatter_sum(values):
    low = lax.psum_scatter(values, "dp", scatter_dimension=0, tiled=True)
    return lax.psum_scatter(low, "fsdp", scatter_dimension=0, tiled=True)


def on_device(
    mesh_shape,
    latents, orders, mask_counts, noise, timesteps, loss_weights,
    block_weights, block_gains, entry_table, head_weights, head_biases, head_edges,
    first_blocks, first_gains, first_entry, first_head, first_biases, first_edges,
    second_blocks, second_gains, second_entry, second_head, second_biases, second_edges,
):
    dp_count, nz = mesh_shape["dp"], mesh_shape["fsdp"]
    devices = dp_count * nz
    me = lax.axis_index("dp") * nz + lax.axis_index("fsdp")
    r0, r1 = D // devices, HW // devices
    direct = dp_count == 8 and nz > 1 and (D // 8) % 16 == 0
    bf = jnp.bfloat16

    low_blocks = block_weights.astype(bf)
    low_entry = jnp.concatenate(
        [entry_table.T.astype(bf), block_gains.reshape(4, r0).T.astype(bf), jnp.zeros((r0, 108), bf)], 1
    )
    low_head = head_weights.astype(bf)
    edge = head_edges.T.astype(bf)
    base = D + 2 * CH
    low_edges = jnp.concatenate(
        [
            edge[:, :D], edge[:, base + FREQ :], edge[:, base : base + FREQ], edge[:, D:base],
            head_biases.reshape((HB + 1) * 5, r1).T.astype(bf), jnp.zeros((r1, 81), bf),
        ],
        1,
    )
    chunks, shapes = gather_plan(
        [(1, None, r0, (TRUNK_WIDTH,)), (0, 0, r0, TRUNK_PARTS), (0, 1, r0, TRUNK_PARTS), (2, None, r1, EDGE_PARTS)],
        TRUNK_WIDTH,
    )
    sources = [low_blocks, low_entry, low_edges]
    if direct:
        gathered = [a.reshape(devices * a.shape[4], -1) for a in gather_rows(sources, chunks, shapes, nz, 1)]
    else:
        gathered = plain_gather(sources, chunks, shapes)
    trunk, edge_mats = gathered[:9], gathered[9:]
    head_blocks = [lax.all_gather(low_head[b], AXES, axis=0, tiled=True) for b in range(HB)]

    local_total = jnp.sum(mask_counts)
    early = exchange(
        jnp.stack([local_total.astype(jnp.float32), jnp.sum(loss_weights)]), dp_count, nz, 3
    )
    counts = early[:, 0].astype(jnp.int32)
    weight_total = jnp.sum(early[:, 1])
    count_ends = jnp.cumsum(counts)
    count_starts = count_ends - counts
    offset = jnp.sum(jnp.where(jnp.arange(devices) == me, count_starts, 0))

    order_row = orders[0]
    clean = latents[0]
    ids = jnp.arange(LAT, dtype=jnp.int32)
    masked = jnp.any((order_row[:, None] == ids[None, :]) & (ids < local_total)[:, None], 0)
    key_keep = jnp.concatenate([jnp.ones((BUF,), jnp.float32), 1.0 - masked.astype(jnp.float32)])
    positions = jnp.arange(SEQ, dtype=jnp.int32)
    columns = jnp.arange(TRUNK_WIDTH, dtype=jnp.int32)
    pick_rows = jnp.concatenate([positions, SEQ + positions, 2 * SEQ + CH + jnp.arange(16, dtype=jnp.int32)])
    select = (pick_rows[:, None] == columns[None, :]).astype(bf) + jnp.pad(
        clean, ((BUF, SEQ + 16), (2 * SEQ, TRUNK_WIDTH - 2 * SEQ - CH))
    )
    top_rows, kept = trunk_forward(trunk[0], trunk[1:9], select, key_keep[None])

    capacity = (LAT + devices - 1) // devices
    slots = devices * capacity
    slot_ids = jnp.arange(slots, dtype=jnp.int32)
    slot_token = jnp.mod(slot_ids // capacity - offset, devices) + devices * (slot_ids % capacity)
    slot_position = jnp.sum(
        jnp.where(slot_token[:, None] == ids[None, :], order_row[None, :], 0), 1
    )
    pick = (
        (slot_position[:, None] == ids[None, :]) & (slot_token < local_total)[:, None]
    ).astype(bf)
    outgoing = dot_plain(
        pick, jnp.concatenate([top_rows, clean, jnp.zeros((LAT, 112), bf)], 1)
    ).astype(bf)
    incoming = lax.all_to_all(
        outgoing.reshape(devices, capacity, -1), AXES, split_axis=0, concat_axis=0, tiled=True
    ).reshape(slots, -1)
    head_rows = noise.shape[0]
    token_ids = jnp.arange(head_rows, dtype=jnp.int32) * devices + me
    inside = (token_ids[:, None] >= count_starts[None, :]) & (token_ids[:, None] < count_ends[None, :])
    first_token = count_starts + jnp.mod(me - count_starts, devices)
    source_slot = (
        jnp.arange(devices, dtype=jnp.int32)[None, :] * capacity
        + (token_ids[:, None] - first_token[None, :]) // devices
    )
    row_slot = jnp.sum(jnp.where(inside, source_slot, 0), 1)
    place = (row_slot[:, None] == slot_ids[None, :]).astype(bf)
    received = dot_plain(place, incoming).astype(bf)

    misc = edge_mats[5]
    biases = (
        misc[:, 2 * CH : 2 * CH + 5 * (HB + 1)]
        .reshape(devices, r1, HB + 1, 5)
        .transpose(2, 0, 3, 1)
        .reshape(HB + 1, 5 * HW)
        .astype(jnp.float32)
    )
    loss_local, head_pairs, small, bias_grad, back_tokens = head_pass(
        head_blocks,
        edge_mats[:5]
        + [
            jnp.pad(misc[:, :CH], ((0, 0), (0, 128 - CH))),
            jnp.pad(misc[:, CH : 2 * CH], ((0, 0), (0, 128 - CH))),
        ],
        biases,
        received[:, :D],
        received[:, D : D + CH],
        noise,
        timesteps,
        loss_weights,
        weight_total,
    )
    grad_cond_t, grad_time_one_t, grad_in_t, grad_out_t = small
    bias_t = (
        bias_grad.reshape(HB + 1, devices, 5, r1).transpose(1, 3, 0, 2).reshape(HW, 5 * (HB + 1))
    )
    head_small = jnp.concatenate(
        [grad_cond_t, grad_time_one_t, grad_in_t, grad_out_t, bias_t, jnp.zeros((HW, 465), jnp.float32)], 1
    ).astype(bf)
    small_columns = head_small.shape[1]
    if direct:
        extras = jnp.stack(
            [head_small[:, k : k + HEAD_WIDTH] for k in range(0, small_columns, HEAD_WIDTH)]
        )
        tall = reduce_products(head_pairs, extras, HW, HEAD_WIDTH, (r1, HEAD_WIDTH), nz, 4)
        tall = tall.transpose(1, 0, 2).reshape(r1, -1)
    else:
        tall = jnp.concatenate(
            [scatter_sum(dot_left(x, y)) for x, y in head_pairs]
            + [scatter_sum(head_small.astype(jnp.float32))],
            1,
        )

    returning = dot_left(place, back_tokens.astype(bf)).astype(bf)
    returned = lax.all_to_all(
        returning.reshape(devices, capacity, D), AXES, split_axis=0, concat_axis=0, tiled=True
    ).reshape(slots, D)
    back_top = jnp.concatenate([jnp.zeros((BUF, D), jnp.float32), dot_left(pick, returned)], 0)
    trunk_pairs, trunk_small = trunk_backward(trunk[0], trunk[1:9], select, key_keep[None], back_top, kept)
    if direct:
        wide = reduce_products(
            trunk_pairs, trunk_small[None], D, TRUNK_WIDTH, (2 * r0, TRUNK_WIDTH // 2), nz, 5
        )
        wide = wide.transpose(1, 0, 2).reshape(r0, -1)
    else:
        wide = jnp.concatenate(
            [scatter_sum(dot_left(x, y)) for x, y in trunk_pairs]
            + [scatter_sum(trunk_small.astype(jnp.float32))],
            1,
        )
    block_columns, head_columns = sum(TRUNK_PARTS), sum(HEAD_PARTS)
    block_grad = jnp.stack([wide[:, l * block_columns : (l + 1) * block_columns] for l in range(2)])
    rest = wide[:, 2 * block_columns :]
    entry_grad = rest[:, : 2 * SEQ + CH].T
    gain_grad = rest[:, 2 * SEQ + CH : 2 * SEQ + CH + 4].T.reshape(2, 2, r0)
    head_grad = jnp.stack([tall[:, b * head_columns : (b + 1) * head_columns] for b in range(HB)])
    rest = tall[:, HB * head_columns :]
    shared = rest[:, 3 * HW :]
    edge_grad = jnp.concatenate(
        [
            shared[:, :D], shared[:, D + FREQ : D + FREQ + 2 * CH], shared[:, D : D + FREQ],
            rest[:, : 3 * HW],
        ],
        1,
    ).T
    bias_grad = (
        shared[:, D + FREQ + 2 * CH : D + FREQ + 2 * CH + 5 * (HB + 1)].T.reshape(HB + 1, 5 * r1)
    )
    squares = jnp.sum(wide * wide) + jnp.sum(tall * tall)
    late = exchange(jnp.stack([loss_local, squares]), dp_count, nz, 6)
    loss_sum = jnp.sum(late[:, 0])
    grad_norm = jnp.sqrt(jnp.sum(late[:, 1]))
    factor = CLIP_NORM / jnp.maximum(grad_norm, CLIP_NORM)
    new = [
        adamw(block_weights, first_blocks, second_blocks, block_grad, factor, LEARN_RATE),
        adamw(block_gains, first_gains, second_gains, gain_grad, factor, GAIN_RATE),
        adamw(entry_table, first_entry, second_entry, entry_grad, factor, LEARN_RATE),
        adamw(head_weights, first_head, second_head, head_grad, factor, LEARN_RATE),
        adamw(head_biases, first_biases, second_biases, bias_grad, factor, LEARN_RATE),
        adamw(head_edges, first_edges, second_edges, edge_grad, factor, LEARN_RATE),
    ]
    return tuple(new[i][k] for k in range(3) for i in range(6)) + (loss_sum, weight_total, grad_norm)


def solution(mesh):
    rows = [P(AXES, None, None), P(AXES, None), P(AXES), P(AXES, None), P(AXES, None), P(AXES, None)]
    state = [
        P(None, AXES, None), P(None, None, AXES), P(None, AXES),
        P(None, AXES, None), P(None, AXES), P(None, AXES),
    ]
    return jax.shard_map(
        functools.partial(on_device, dict(mesh.shape)),
        mesh=mesh,
        in_specs=tuple(rows + state * 3),
        out_specs=tuple(state * 3 + [P(), P(), P()]),
        check_vma=False,
    )
```

```python
import functools
import math

import jax
import jax.numpy as jnp
from jax import lax
from jax.experimental import pallas as pl
from jax.experimental.pallas import tpu as pltpu
from jax.sharding import PartitionSpec as P

D = 768
HEADS = 12
HD = 64
FF = 3072
HW = 1024
CH = 16
FREQ = 256
LAT = 256
BUF = 64
HB = 2
COPIES = 4
TSTEPS = 1000
ADAM_STEP = 5
SEQ = 320

BETA_ONE = 0.5
BETA_TWO = 0.5
LEARN_RATE = 0.03
GAIN_RATE = 0.3
DECAY_RATE = 0.02
ADAM_EPS = 1e-08
CLIP_NORM = 0.002
NORM_EPS = 1e-06
AXES = ("dp", "fsdp")
MESH_IDS = pl.DeviceIdType.MESH


REDUCE_LAGS = (0, 1, 3, 5, 7)
REDUCE_DEPTH = 3


def reduce_program(nz, row_count, width, jobs, extra_count, refs, between=None):
    job_count = len(jobs)
    picked = lambda ref, index: ref if index is None else ref.at[index]
    x_refs = [picked(ref, job[2]) for ref, job in zip(refs[:job_count], jobs)]
    y_refs = [picked(ref, job[3]) for ref, job in zip(refs[job_count : 2 * job_count], jobs)]
    position = 2 * job_count
    extra_ref = None
    if extra_count:
        extra_ref = refs[position]
        position += 1
    out_ref = refs[position]
    (
        x_buf, y_buf, whole, land_core, first, land_first, second, land_second,
        last, last_low, land_last, extra_sem,
        load_sem, core_send, core_recv, first_send, first_recv, second_send, second_recv,
        last_send, last_recv, credit,
    ) = refs[position + 1 :]
    dp, z = lax.axis_index("dp"), lax.axis_index("fsdp")
    core, xb, yb = lax.rem(dp, 2), lax.rem(dp // 2, 2), dp // 4
    group = row_count // 8
    part = group // nz
    starts, total = [], 0
    for _, columns, _, _ in jobs:
        starts.append(total)
        total += columns // width
    computed = total
    total += extra_count

    core_peer = (dp + 1 - 2 * core, z)
    x_step, y_step = 2 - 4 * xb, 4 - 8 * yb
    z_peers = [(dp, lax.rem(z + s, nz)) for s in range(1, nz)]
    barrier = pltpu.get_barrier_semaphore()
    for peer in [core_peer, (dp + x_step, z), (dp + y_step, z)] + z_peers:
        pl.semaphore_signal(barrier, inc=1, device_id=peer, device_id_type=MESH_IDS)
    pl.semaphore_wait(barrier, 2 + nz)

    def loads(x_ref, y_ref, column, slot):
        return (
            pltpu.make_async_copy(x_ref, x_buf.at[slot], load_sem.at[0, slot]),
            pltpu.make_async_copy(
                y_ref.at[:, pl.ds(pl.multiple_of(column, 128), width)], y_buf.at[slot], load_sem.at[1, slot]
            ),
        )

    def prefetch(g):
        for number, (_, columns, _, _) in enumerate(jobs):
            start, stop = starts[number], starts[number] + columns // width

            @pl.when((g >= start) & (g < stop))
            def _():
                for copy in loads(x_refs[number], y_refs[number], (g - start) * width, lax.rem(g, 2)):
                    copy.start()

    def core_copy(g):
        return pltpu.make_async_remote_copy(
            src_ref=whole.at[lax.rem(g, 2), 1 - core],
            dst_ref=land_core.at[lax.rem(g, 4)],
            send_sem=core_send.at[lax.rem(g, 2)],
            recv_sem=core_recv.at[lax.rem(g, 4)],
            device_id=core_peer,
            device_id_type=MESH_IDS,
        )

    depth = REDUCE_DEPTH

    def first_copy(g):
        p = lax.rem(g, 2)
        mine = (1 - p) * xb + p * yb
        return pltpu.make_async_remote_copy(
            src_ref=first.at[lax.rem(g, depth), 1 - mine],
            dst_ref=land_first.at[g],
            send_sem=first_send.at[lax.rem(g, depth)],
            recv_sem=first_recv.at[g],
            device_id=(dp + (1 - p) * x_step + p * y_step, z),
            device_id_type=MESH_IDS,
        )

    def second_copy(g):
        p = lax.rem(g, 2)
        mine = (1 - p) * yb + p * xb
        return pltpu.make_async_remote_copy(
            src_ref=second.at[lax.rem(g, depth), 1 - mine],
            dst_ref=land_second.at[g],
            send_sem=second_send.at[lax.rem(g, depth)],
            recv_sem=second_recv.at[g],
            device_id=(dp + (1 - p) * y_step + p * x_step, z),
            device_id_type=MESH_IDS,
        )

    def last_copies(g):
        return [
            pltpu.make_async_remote_copy(
                src_ref=last_low.at[lax.rem(g, depth), lax.rem(z + s, nz)],
                dst_ref=land_last.at[g, s - 1],
                send_sem=last_send.at[lax.rem(g, depth), s - 1],
                recv_sem=last_recv.at[g, s - 1],
                device_id=z_peers[s - 1],
                device_id_type=MESH_IDS,
            )
            for s in range(1, nz)
        ]

    low_rows, low_width = last_low.shape[2:]
    folds = width // low_width

    def fold(block):
        return jnp.concatenate([block[:, k * low_width : (k + 1) * low_width] for k in range(folds)], 0)

    def stage_core(g):
        slot = lax.rem(g, 2)

        @pl.when(g >= 2)
        def _():
            core_copy(g - 2).wait_send()

        def put(number, value):
            yx, c = number // 2, number % 2
            whole[slot, c, yx] = value

        @pl.when(g < computed)
        def _():
            for copy in loads(x_refs[0], y_refs[0], 0, slot):
                copy.wait()
            product = lax.dot_general(
                x_buf[slot], y_buf[slot], (((0,), (0,)), ((), ())), preferred_element_type=jnp.float32
            )
            for number in range(8):
                put(number, product[number * group : (number + 1) * group].astype(jnp.bfloat16))

        if extra_count:
            @pl.when(g >= computed)
            def _():
                copies = [
                    pltpu.make_async_copy(
                        extra_ref.at[g - computed, pl.ds(number * group, group), :],
                        whole.at[slot, number % 2, number // 2],
                        extra_sem.at[number],
                    )
                    for number in range(8)
                ]
                for copy in copies:
                    copy.start()
                for copy in copies:
                    copy.wait()

        @pl.when(g >= 4)
        def _():
            pl.semaphore_wait(credit, 1)
        core_copy(g).start()

    def stage_first(g):
        p = lax.rem(g, 2)

        @pl.when(g >= depth)
        def _():
            first_copy(g - depth).wait_send()
        core_copy(g).wait_recv()
        for f in range(2):
            for s in range(2):
                yx = (1 - p) * (2 * s + f) + p * (2 * f + s)
                first[lax.rem(g, depth), f, s] = (
                    whole[lax.rem(g, 2), core, yx].astype(jnp.float32)
                    + land_core[lax.rem(g, 4), yx].astype(jnp.float32)
                ).astype(jnp.bfloat16)

        @pl.when(g < total - 4)
        def _():
            pl.semaphore_signal(credit, inc=1, device_id=core_peer, device_id_type=MESH_IDS)
        first_copy(g).start()

    def stage_second(g):
        p = lax.rem(g, 2)
        mine = (1 - p) * xb + p * yb

        @pl.when(g >= depth)
        def _():
            second_copy(g - depth).wait_send()
        first_copy(g).wait_recv()
        for s in range(2):
            second[lax.rem(g, depth), s] = (
                first[lax.rem(g, depth), mine, s].astype(jnp.float32) + land_first[g, s].astype(jnp.float32)
            ).astype(jnp.bfloat16)
        second_copy(g).start()

    def stage_last(g):
        p = lax.rem(g, 2)
        mine = (1 - p) * yb + p * xb

        @pl.when(g >= depth)
        def _():
            for copy in last_copies(g - depth):
                copy.wait_send()
        second_copy(g).wait_recv()
        summed = second[lax.rem(g, depth), mine].astype(jnp.float32) + land_second[g].astype(jnp.float32)
        for k in range(nz):
            block = fold(summed[k * part : (k + 1) * part])
            last[lax.rem(g, depth), k] = block
            last_low[lax.rem(g, depth), k] = block.astype(jnp.bfloat16)
        for copy in last_copies(g):
            copy.start()

    def stage_out(g):
        for copy in last_copies(g):
            copy.wait_recv()
        value = last[lax.rem(g, depth), z]
        for s in range(1, nz):
            value = value + land_last[g, s - 1].astype(jnp.float32)
        for k in range(folds):
            out_ref[g, :, pl.ds(k * low_width, low_width)] = value[k * part : (k + 1) * part]

    lags = REDUCE_LAGS
    prefetch(0)

    @pl.loop(0, total + lags[-1])
    def _(i):
        for stage, lag in zip((stage_out, stage_last, stage_second, stage_first), lags[:0:-1]):
            @pl.when((i >= lag) & (i < total + lag))
            def _():
                stage(i - lag)

        @pl.when(i + 1 < computed)
        def _():
            prefetch(i + 1)

        @pl.when(i < total)
        def _():
            stage_core(i)

        if between is not None:
            between(i)

    for g in range(max(total - 2, 0), total):
        core_copy(g).wait_send()
    for g in range(max(total - depth, 0), total):
        first_copy(g).wait_send()
        second_copy(g).wait_send()
        for copy in last_copies(g):
            copy.wait_send()


def reduce_kernel(nz, row_count, width, jobs, extra_count, *refs):
    reduce_program(nz, row_count, width, jobs, extra_count, refs)


def reduce_setup(pairs, extras, row_count, width, low_shape, nz):
    bf = jnp.bfloat16
    xs, ys = ([a if isinstance(a, tuple) else (a, None) for a in side] for side in zip(*pairs))
    tokens = xs[0][0].shape[-2]
    group, part = row_count // 8, row_count // 8 // nz
    jobs = [(x.shape[-1], y.shape[-1], i, j) for (x, i), (y, j) in zip(xs, ys)]
    total = sum(job[1] // width for job in jobs) + extras.shape[0]
    low_rows, low_width = low_shape
    dma, reg = pltpu.SemaphoreType.DMA, pltpu.SemaphoreType.REGULAR
    operands = [x for x, _ in xs] + [y for y, _ in ys] + [extras]
    scratch = [
        pltpu.VMEM((2, tokens, row_count), bf),
        pltpu.VMEM((2, tokens, width), bf),
        pltpu.VMEM((2, 2, 4, group, width), bf),
        pltpu.VMEM((4, 4, group, width), bf),
        pltpu.VMEM((REDUCE_DEPTH, 2, 2, group, width), bf),
        pltpu.VMEM((total, 2, group, width), bf),
        pltpu.VMEM((REDUCE_DEPTH, 2, group, width), bf),
        pltpu.VMEM((total, group, width), bf),
        pltpu.VMEM((REDUCE_DEPTH, nz, low_rows, low_width), jnp.float32),
        pltpu.VMEM((REDUCE_DEPTH, nz, low_rows, low_width), bf),
        pltpu.VMEM((total, nz - 1, low_rows, low_width), bf),
        dma((8,)),
        dma((2, 2)), dma((2,)), dma((4,)), dma((REDUCE_DEPTH,)), dma((total,)), dma((REDUCE_DEPTH,)), dma((total,)),
        dma((REDUCE_DEPTH, nz - 1)), dma((total, nz - 1)), reg,
    ]
    return (
        (nz, row_count, width, jobs, extras.shape[0]),
        operands,
        [pl.BlockSpec(memory_space=pl.ANY)] * len(operands),
        jax.ShapeDtypeStruct((total, part, width), jnp.float32),
        scratch,
    )


def reduce_products(pairs, extras, row_count, width, low_shape, nz, collective_id):
    static, operands, specs, shape, scratch = reduce_setup(pairs, extras, row_count, width, low_shape, nz)
    return pl.pallas_call(
        functools.partial(reduce_kernel, *static),
        out_shape=shape,
        in_specs=specs,
        out_specs=pl.BlockSpec(memory_space=pltpu.VMEM),
        scratch_shapes=scratch,
        compiler_params=pltpu.CompilerParams(
            collective_id=collective_id, has_side_effects=True, vmem_limit_bytes=60 * 2**20
        ),
    )(*operands)


def gather_program(nz, chunks, sources, results, sems):
    own_sem, last_send, last_recv, first_send, first_recv, second_send, second_recv, core_send, core_recv = sems
    dp, z = lax.axis_index("dp"), lax.axis_index("fsdp")
    core, xb, yb = lax.rem(dp, 2), lax.rem(dp // 2, 2), dp // 4
    core_peer = (dp + 1 - 2 * core, z)
    x_peer, y_peer = (dp + 2 - 4 * xb, z), (dp + 4 - 8 * yb, z)
    z_peers = [(dp, lax.rem(z + s, nz)) for s in range(1, nz)]
    barrier = pltpu.get_barrier_semaphore()
    for peer in [core_peer, x_peer, y_peer] + z_peers:
        pl.semaphore_signal(barrier, inc=1, device_id=peer, device_id_type=MESH_IDS)
    pl.semaphore_wait(barrier, 2 + nz)

    def remote(source, target, send, recv, peer):
        return pltpu.make_async_remote_copy(
            src_ref=source, dst_ref=target, send_sem=send, recv_sem=recv, device_id=peer, device_id_type=MESH_IDS
        )

    def source_of(k):
        source, index, column, _, _, width = chunks[k]
        ref = sources[source] if index is None else sources[source].at[index]
        return ref.at[:, pl.ds(column, width)]

    def result_of(k):
        _, _, _, result, column, width = chunks[k]
        return results[result].at[:, :, :, :, :, pl.ds(column, width)]

    def own(k):
        return pltpu.make_async_copy(source_of(k), result_of(k).at[yb, xb, core, z], own_sem.at[k])

    def to_z(k, source, target):
        return [
            remote(source, target, last_send.at[k, s], last_recv.at[k, s], z_peers[s]) for s in range(nz - 1)
        ]

    def to_pair(k, late, along_y, source, target):
        send, recv = (second_send, second_recv) if late else (first_send, first_recv)
        return [remote(source, target, send.at[k], recv.at[k], y_peer if along_y else x_peer)]

    def stage(k, number):
        result = result_of(k)
        block = result.at[yb, xb, core, z]
        if number == 0:
            return to_z(k, source_of(k), block)
        if number == 1:
            ref = result.at[yb, xb, core]
            return to_pair(k, False, k % 2, ref, ref)
        ref = result.at[:, xb, core] if k % 2 else result.at[yb, :, core]
        return to_pair(k, True, 1 - k % 2, ref, ref)

    def across(k):
        ref = result_of(k).at[:, :, core]
        return remote(ref, ref, core_send.at[k], core_recv.at[k], core_peer)

    total = len(chunks)

    def pass_on(k, number):
        if number == 0:
            own(k).wait()
        for copy in stage(k, number):
            copy.wait_recv()
        for copy in stage(k, number + 1) if number < 2 else [across(k)]:
            copy.start()

    def step(i):
        for number in (2, 1, 0):
            if 0 <= i - 2 * (number + 1) < total:
                pass_on(i - 2 * (number + 1), number)
        if i < total:
            own(i).start()
            for copy in stage(i, 0):
                copy.start()

    def finish():
        for k in range(total):
            for copy in stage(k, 0) + stage(k, 1) + stage(k, 2) + [across(k)]:
                copy.wait_send()
            across(k).wait_recv()

    return total + 6, step, finish


def gather_sems(total, nz):
    dma = pltpu.SemaphoreType.DMA
    return [dma((total,)), dma((total, nz - 1)), dma((total, nz - 1))] + [dma((total,))] * 6


def gather_kernel(nz, chunks, source_count, *refs):
    sources, refs = refs[:source_count], refs[source_count:]
    result_count = 1 + max(chunk[3] for chunk in chunks)
    steps, step, finish = gather_program(nz, chunks, sources, refs[:result_count], refs[result_count:])
    for i in range(steps):
        step(i)
    finish()


def gather_rows(sources, chunks, shapes, nz, collective_id):
    return pl.pallas_call(
        functools.partial(gather_kernel, nz, chunks, len(sources)),
        out_shape=[jax.ShapeDtypeStruct((2, 2, 2, nz, *shape), jnp.bfloat16) for shape in shapes],
        in_specs=[pl.BlockSpec(memory_space=pl.ANY)] * len(sources),
        out_specs=[pl.BlockSpec(memory_space=pl.ANY)] * len(shapes),
        scratch_shapes=gather_sems(len(chunks), nz),
        compiler_params=pltpu.CompilerParams(
            collective_id=collective_id, has_side_effects=True, vmem_limit_bytes=60 * 2**20
        ),
    )(*sources)


def exchange_kernel(dp_count, nz, in_ref, out_ref, send_sem, recv_sem):
    devices = dp_count * nz
    me = lax.axis_index("dp") * nz + lax.axis_index("fsdp")

    def peer(step):
        there = lax.rem(me + step, devices)
        return (there // nz, lax.rem(there, nz))

    barrier = pltpu.get_barrier_semaphore()

    @pl.loop(1, devices)
    def _(step):
        pl.semaphore_signal(barrier, inc=1, device_id=peer(step), device_id_type=MESH_IDS)

    pl.semaphore_wait(barrier, devices - 1)

    def copy(step):
        return pltpu.make_async_remote_copy(
            src_ref=in_ref,
            dst_ref=out_ref.at[me],
            send_sem=send_sem.at[step - 1],
            recv_sem=recv_sem.at[step - 1],
            device_id=peer(step),
            device_id_type=MESH_IDS,
        )

    @pl.loop(1, devices)
    def _(step):
        copy(step).start()

    out_ref[me] = in_ref[...]

    @pl.loop(1, devices)
    def _(step):
        copy(step).wait()


def exchange(values, dp_count, nz, collective_id):
    devices = dp_count * nz
    tile = jnp.broadcast_to(jnp.pad(values, (0, 128 - values.shape[0])), (8, 128))
    out = pl.pallas_call(
        functools.partial(exchange_kernel, dp_count, nz),
        out_shape=jax.ShapeDtypeStruct((devices, 8, 128), jnp.float32),
        in_specs=[pl.BlockSpec(memory_space=pltpu.VMEM)],
        out_specs=pl.BlockSpec(memory_space=pltpu.VMEM),
        scratch_shapes=[pltpu.SemaphoreType.DMA((devices - 1,)), pltpu.SemaphoreType.DMA((devices - 1,))],
        compiler_params=pltpu.CompilerParams(
            collective_id=collective_id, has_side_effects=True, vmem_limit_bytes=4 * 2**20
        ),
    )(tile)
    return out[:, 0, : values.shape[0]]


def dot_plain(left, right):
    return jnp.dot(left, right, preferred_element_type=jnp.float32)


def dot_left(left, right):
    return lax.dot_general(
        left, right, (((0,), (0,)), ((), ())), preferred_element_type=jnp.float32
    )


def dot_right(left, right):
    return lax.dot_general(
        left, right, (((1,), (1,)), ((), ())), preferred_element_type=jnp.float32
    )


KEPT = (
    ("normed", D, jnp.bfloat16), ("packed", 3 * D, jnp.bfloat16), ("mixed", D, jnp.bfloat16),
    ("second", D, jnp.bfloat16), ("upper", FF, jnp.bfloat16), ("inner", FF, jnp.float32),
    ("norm_one", D, jnp.float32), ("norm_two", D, jnp.float32), ("inv_one", 128, jnp.float32),
    ("inv_two", 128, jnp.float32),
)
KEPT_INDEX = {name: k for k, (name, _, _) in enumerate(KEPT)}
BACK = (("back_packed", 3 * D), ("back_attn", D), ("back_inner", FF), ("back_branch", D))
GELU_SCALE = math.sqrt(2.0 / math.pi)


def in_nn(x, w):
    return jnp.dot(x, w, preferred_element_type=jnp.float32)


def in_nt(x, w):
    return lax.dot_general(x, w, (((1,), (1,)), ((), ())), preferred_element_type=jnp.float32)


def in_tn(x, w):
    return lax.dot_general(x, w, (((0,), (0,)), ((), ())), preferred_element_type=jnp.float32)


def softmax_rows(scores):
    raised = jnp.exp(scores - jnp.max(scores, -1, keepdims=True))
    return raised * (1.0 / jnp.sum(raised, -1, keepdims=True))


def low_half():
    return lax.broadcasted_iota(jnp.int32, (SEQ, 2 * HD), 1) < HD


def forward_pieces(weights, entry, select_ref, mask_ref, hidden, kept, top_ref, gains_ref, need, leave):
    bf = jnp.bfloat16
    pieces = []
    gain = lambda row: gains_ref[row : row + 1, :]

    def start():
        need(entry)
        gains_ref[...] = in_nt(select_ref[2 * SEQ :, :], entry[...])
        hidden[...] = in_nt(select_ref[:SEQ, :], entry[...])
    pieces.append(start)

    def norm(layer, which):
        value = hidden[...]
        centred = value - jnp.mean(value, -1, keepdims=True)
        inv = lax.rsqrt(jnp.mean(centred * centred, -1, keepdims=True) + NORM_EPS)
        n = centred * inv
        names = ("norm_one", "inv_one", "normed") if which == 0 else ("norm_two", "inv_two", "second")
        kept[names[0]][layer] = n
        kept[names[1]][layer] = jnp.broadcast_to(inv, (SEQ, 128))
        kept[names[2]][layer] = (n * gain(2 * layer + which)).astype(bf)
        for name in names:
            leave(layer, name)

    def project(layer):
        norm(layer, 0)
        need(weights[4 * layer])
        kept["packed"][layer] = in_nn(kept["normed"][layer], weights[4 * layer][...]).astype(bf)
        leave(layer, "packed")

    def attend(layer, pair):
        packed = kept["packed"]
        cut = lambda k: packed[layer, :, k * D + pair * 2 * HD : k * D + (pair + 1) * 2 * HD]
        q, k, v = cut(0), cut(1), cut(2)
        low = low_half()
        parts = []
        for side in range(2):
            one = jnp.where(low if side == 0 else ~low, q, jnp.zeros((), bf))
            scores = in_nt(one, k) * HD ** (-0.5)
            if layer == 0:
                scores = jnp.where(mask_ref[...] > 0, scores, -1e30)
            parts.append(in_nn(softmax_rows(scores).astype(bf), v))
        kept["mixed"][layer, :, pair * 2 * HD : (pair + 1) * 2 * HD] = jnp.where(low, parts[0], parts[1]).astype(bf)

    def close(layer):
        leave(layer, "mixed")
        need(weights[4 * layer + 1])
        hidden[...] += in_nn(kept["mixed"][layer], weights[4 * layer + 1][...])
        norm(layer, 1)
        need(weights[4 * layer + 2])

    def up(layer, part, parts):
        columns = slice(part * FF // parts, (part + 1) * FF // parts)
        inner = in_nn(kept["second"][layer], weights[4 * layer + 2][:, columns])
        kept["inner"][layer, :, columns] = inner
        kept["upper"][layer, :, columns] = (
            0.5 * inner * (1.0 + jnp.tanh(GELU_SCALE * (inner + 0.044715 * inner * inner * inner)))
        ).astype(bf)

    def down(layer):
        leave(layer, "inner")
        leave(layer, "upper")
        need(weights[4 * layer + 3])
        hidden[...] += in_nt(kept["upper"][layer], weights[4 * layer + 3][...])

    def between():
        keep = mask_ref[...].reshape(1, SEQ)
        hidden[...] = hidden[...] * keep_column(keep) + in_nt(select_ref[SEQ : 2 * SEQ, :], entry[...])

    def keep_column(keep):
        return jnp.transpose(jnp.broadcast_to(keep, (128, SEQ)))[:, :1]

    for layer in range(2):
        pieces.append(functools.partial(project, layer))
        for pair in range(HEADS // 2):
            pieces.append(functools.partial(attend, layer, pair))
        pieces.append(functools.partial(close, layer))
        for part in range(3):
            pieces.append(functools.partial(up, layer, part, 3))
        pieces.append(functools.partial(down, layer))
        if layer == 0:
            pieces.append(between)

    def finish():
        top_ref[...] = hidden[BUF:, :].astype(bf)
    pieces.append(finish)
    return pieces


def forward_kernel(gather, *refs):
    entry_hbm, weight_hbm, (select_ref, mask_ref), refs = refs[0], refs[1:9], refs[9:11], refs[11:]
    sources, refs = (refs[:1], refs[1:]) if gather else ((), refs)
    kept_hbm, (top_ref, gains_ref), refs = refs[: len(KEPT)], refs[len(KEPT) : len(KEPT) + 2], refs[len(KEPT) + 2 :]
    results = ()
    if gather:
        count = 1 + max(chunk[3] for chunk in gather[1])
        results, refs = refs[:count], refs[count:]
    entry, weights, kept_refs, refs = refs[0], refs[1:9], refs[9 : 9 + len(KEPT)], refs[9 + len(KEPT) :]
    hidden, weight_sem, kept_sem = refs[:3]
    kept = {name: ref for (name, _, _), ref in zip(KEPT, kept_refs)}
    local = [(entry_hbm, entry)] + list(zip(weight_hbm, weights))
    fetches = {id(ref): pltpu.make_async_copy(hbm, ref, weight_sem.at[k]) for k, (hbm, ref) in enumerate(local)}
    for copy in fetches.values():
        copy.start()
    leaving = []

    def leave(layer, name):
        k = KEPT_INDEX[name]
        copy = pltpu.make_async_copy(kept_refs[k].at[layer], kept_hbm[k].at[layer], kept_sem.at[layer, k])
        copy.start()
        leaving.append(copy)

    steps = 0
    if gather:
        steps, step, finish = gather_program(*gather, sources, results, refs[3:])
    pieces = forward_pieces(
        weights, entry, select_ref, mask_ref, hidden, kept, top_ref, gains_ref, lambda ref: fetches[id(ref)].wait(), leave
    )
    for i in range(max(steps, len(pieces))):
        if i < steps:
            step(i)
        if i < len(pieces):
            pieces[i]()
    if gather:
        finish()
    for copy in leaving:
        copy.wait()


def trunk_forward(entry, weights, select, mask, gather=None, sources=(), shapes=(), collective_id=None):
    bf, f32 = jnp.bfloat16, jnp.float32
    vmem, hbm = pl.BlockSpec(memory_space=pltpu.VMEM), pl.BlockSpec(memory_space=pl.ANY)
    kept_shapes = [(2, SEQ, columns) for _, columns, _ in KEPT]
    more = {} if gather is None else {"collective_id": collective_id, "has_side_effects": True}
    outs = pl.pallas_call(
        functools.partial(forward_kernel, gather),
        out_shape=[jax.ShapeDtypeStruct(s, dtype) for s, (_, _, dtype) in zip(kept_shapes, KEPT)]
        + [jax.ShapeDtypeStruct((LAT, D), bf), jax.ShapeDtypeStruct((16, D), f32)]
        + [jax.ShapeDtypeStruct((2, 2, 2, gather[0], *shape), bf) for shape in shapes],
        in_specs=[hbm] * 9 + [vmem] * 2 + [hbm] * len(sources),
        out_specs=[hbm] * len(KEPT) + [vmem] * 2 + [hbm] * len(shapes),
        scratch_shapes=[pltpu.VMEM(w.shape, bf) for w in [entry] + weights]
        + [pltpu.VMEM(s, dtype) for s, (_, _, dtype) in zip(kept_shapes, KEPT)]
        + [pltpu.VMEM((SEQ, D), f32), pltpu.SemaphoreType.DMA((9,)), pltpu.SemaphoreType.DMA((2, len(KEPT)))]
        + ([] if gather is None else gather_sems(len(gather[1]), gather[0])),
        compiler_params=pltpu.CompilerParams(vmem_limit_bytes=60 * 2**20, **more),
    )(entry, *weights, select, mask, *sources)
    count = len(KEPT)
    return outs[count], outs[count + 1], outs[:count], outs[count + 2 :]


BACK_KEPT = ("packed", "inner", "norm_one", "norm_two", "inv_one", "inv_two")


def backward_pieces(refs):
    weight_hbm, (gains_ref, select_ref, mask_ref, top_ref), refs = refs[:8], refs[8:12], refs[12:]
    kept_hbm, refs = refs[: len(BACK_KEPT)], refs[len(BACK_KEPT) :]
    back_hbm, small_ref, refs = refs[: len(BACK)], refs[len(BACK)], refs[len(BACK) + 1 :]
    buffers, kept_refs, refs = refs[:2], refs[2 : 2 + len(BACK_KEPT)], refs[2 + len(BACK_KEPT) :]
    back_refs, (mixed, hidden, middle, decoder, gain_grad, weight_sem, kept_sem, back_sem) = refs[: len(BACK)], refs[len(BACK) :]
    bf = jnp.bfloat16
    back = {name: ref for (name, _), ref in zip(BACK, back_refs)}
    kept = {name: ref for name, ref in zip(BACK_KEPT, kept_refs)}
    places = []
    for layer in (1, 0):
        turn = 1 - layer
        places += [
            (turn, 0, FF, 4 * layer + 3), (1 - turn, 0, FF, 4 * layer + 2),
            (turn, 0, D, 4 * layer + 1), (turn, D, 3 * D, 4 * layer),
        ]
    place_of = {place[3]: k for k, place in enumerate(places)}

    def view(weight):
        buffer, column, columns, _ = places[place_of[weight]]
        return buffers[buffer].at[:, pl.ds(column, columns)]

    def fetch(weight):
        return pltpu.make_async_copy(weight_hbm[weight], view(weight), weight_sem.at[weight])

    def fetch_kept(layer, name):
        k = BACK_KEPT.index(name)
        return pltpu.make_async_copy(kept_hbm[k].at[layer], kept_refs[k], kept_sem.at[k])

    def leave(layer, name):
        k = [n for n, _ in BACK].index(name)
        return pltpu.make_async_copy(back_refs[k], back_hbm[k].at[layer], back_sem.at[k])

    def gain(row):
        return gains_ref[row : row + 1, :]

    def norm_step(upstream, n, inv):
        return inv * (
            upstream - jnp.mean(upstream, -1, keepdims=True) - n * jnp.mean(upstream * n, -1, keepdims=True)
        )

    def begin():
        fetch(7).start()
        fetch_kept(1, "inner").start()
        fetch(6).start()
        for name in ("norm_two", "inv_two", "packed", "norm_one", "inv_one"):
            fetch_kept(1, name).start()
        hidden[...] = top_ref[...]
        gain_grad[...] = jnp.zeros_like(gain_grad)

    def branch(layer):
        if layer == 0:
            leave(1, "back_branch").wait()
        back["back_branch"][...] = hidden[...].astype(bf)
        leave(layer, "back_branch").start()
        fetch(4 * layer + 3).wait()
        fetch_kept(layer, "inner").wait()
        if layer == 0:
            leave(1, "back_inner").wait()

    def widen(layer, part, parts):
        columns = slice(part * FF // parts, (part + 1) * FF // parts)
        up = in_nn(back["back_branch"][...], view(4 * layer + 3)[:, columns])
        x = kept["inner"][:, columns]
        t = jnp.tanh(GELU_SCALE * (x + 0.044715 * x * x * x))
        slope = 0.5 * (1.0 + t) + 0.5 * x * (1.0 - t * t) * (GELU_SCALE * (1.0 + 3.0 * 0.044715 * x * x))
        back["back_inner"][:, columns] = (slope * up).astype(bf)

    def narrow(layer):
        fetch(4 * layer + 1).start()
        fetch(4 * layer).start()
        if layer == 1:
            fetch_kept(0, "inner").start()
        leave(layer, "back_inner").start()
        fetch(4 * layer + 2).wait()
        fetch_kept(layer, "norm_two").wait()
        fetch_kept(layer, "inv_two").wait()
        middle[...] = in_nt(back["back_inner"][...], view(4 * layer + 2)[...])

    def renorm(layer):
        value = middle[...]
        n = kept["norm_two"][...]
        gain_grad[2 * layer + 1 : 2 * layer + 2, :] = jnp.sum(value * n, 0, keepdims=True)
        middle[...] = hidden[...] + norm_step(value * gain(2 * layer + 1), n, kept["inv_two"][:, :1])
        if layer == 0:
            leave(1, "back_attn").wait()
        back["back_attn"][...] = middle[...].astype(bf)
        leave(layer, "back_attn").start()
        if layer == 1:
            fetch(3).start()
            fetch_kept(0, "norm_two").start()
            fetch_kept(0, "inv_two").start()

    def unmix(layer):
        fetch(4 * layer + 1).wait()
        fetch_kept(layer, "packed").wait()
        if layer == 0:
            leave(1, "back_packed").wait()
        mixed[...] = in_nt(back["back_attn"][...], view(4 * layer + 1)[...]).astype(bf)

    def attend(layer, pair):
        low = low_half()
        at = lambda k: slice(k * D + pair * 2 * HD, k * D + (pair + 1) * 2 * HD)
        q, k, v = (kept["packed"][:, at(i)] for i in range(3))
        up = mixed[:, at(0)]
        zero = jnp.zeros((), bf)
        parts = []
        for side in range(2):
            mine = low if side == 0 else ~low
            scores = in_nt(jnp.where(mine, q, zero), k) * HD ** (-0.5)
            if layer == 0:
                scores = jnp.where(mask_ref[...] > 0, scores, -1e30)
            attention = softmax_rows(scores)
            back_attention = in_nt(jnp.where(mine, up, zero), v)
            back_values = in_tn(attention.astype(bf), up)
            back_scores = (
                attention * (back_attention - jnp.sum(back_attention * attention, -1, keepdims=True))
            ).astype(bf)
            parts.append((in_nn(back_scores, k) * HD ** (-0.5), in_tn(back_scores, q) * HD ** (-0.5), back_values))
        for i in range(3):
            back["back_packed"][:, at(i)] = jnp.where(low, parts[0][i], parts[1][i]).astype(bf)

    def close(layer):
        leave(layer, "back_packed").start()
        fetch(4 * layer).wait()
        fetch_kept(layer, "norm_one").wait()
        fetch_kept(layer, "inv_one").wait()
        value = in_nt(back["back_packed"][...], view(4 * layer)[...])
        n = kept["norm_one"][...]
        gain_grad[2 * layer : 2 * layer + 1, :] = jnp.sum(value * n, 0, keepdims=True)
        hidden[...] = middle[...] + norm_step(value * gain(2 * layer), n, kept["inv_one"][:, :1])
        if layer == 1:
            fetch(2).start()
            for name in ("packed", "norm_one", "inv_one"):
                fetch_kept(0, name).start()
            decoder[...] = hidden[...].astype(bf)
            keep = jnp.transpose(jnp.broadcast_to(mask_ref[...], (128, SEQ)))[:, :1]
            hidden[...] = hidden[...] * keep

    def small():
        hidden_low = hidden[...].astype(bf)
        small_ref[...] = (
            in_tn(hidden_low, select_ref[:SEQ, :])
            + in_tn(decoder[...], select_ref[SEQ : 2 * SEQ, :])
            + in_tn(gain_grad[...].astype(bf), select_ref[2 * SEQ :, :])
        ).astype(bf)
        for name, _ in BACK:
            leave(0, name).wait()

    pieces = [begin]
    for layer in (1, 0):
        pieces.append(functools.partial(branch, layer))
        for part in range(3):
            pieces.append(functools.partial(widen, layer, part, 3))
        pieces += [functools.partial(f, layer) for f in (narrow, renorm, unmix)]
        for pair in range(HEADS // 2):
            pieces.append(functools.partial(attend, layer, pair))
        pieces.append(functools.partial(close, layer))
    pieces.append(small)
    return pieces


def backward_kernel(reduction, operand_count, *refs):
    fixed = 12 + len(BACK_KEPT)
    results = len(BACK) + 1
    if reduction is None:
        for piece in backward_pieces(refs):
            piece()
        return
    mine, refs = refs[:fixed], refs[fixed:]
    operands, refs = refs[:operand_count], refs[operand_count:]
    mine, refs = mine + refs[:results], refs[results:]
    summed, refs = refs[0], refs[1:]
    count = 2 + len(BACK_KEPT) + len(BACK) + 8
    pieces = backward_pieces(mine + refs[:count])
    chunks = summed.shape[0]
    start = 0
    per_turn = -(-len(pieces) // (chunks - start))

    def between(i):
        for turn in range(-(-len(pieces) // per_turn)):
            @pl.when(i == start + turn)
            def _():
                for piece in pieces[turn * per_turn : (turn + 1) * per_turn]:
                    piece()

    reduce_program(*reduction, operands + (summed,) + refs[count:], between)


def trunk_backward(gains, weights, select, mask, back_top, kept, reduction=None, collective_id=None):
    bf, f32 = jnp.bfloat16, jnp.float32
    vmem, hbm = pl.BlockSpec(memory_space=pltpu.VMEM), pl.BlockSpec(memory_space=pl.ANY)
    kept_in = [kept[KEPT_INDEX[name]] for name in BACK_KEPT]
    static, operands, specs, shape, scratch = reduction or (None, [], [], None, [])
    more = {} if reduction is None else {"collective_id": collective_id, "has_side_effects": True}
    outs = pl.pallas_call(
        functools.partial(backward_kernel, static, len(operands)),
        out_shape=[jax.ShapeDtypeStruct((2, SEQ, columns), bf) for _, columns in BACK]
        + [jax.ShapeDtypeStruct((D, TRUNK_WIDTH), bf)]
        + ([] if reduction is None else [shape]),
        in_specs=[hbm] * 8 + [vmem] * 4 + [hbm] * len(BACK_KEPT) + specs,
        out_specs=[hbm] * len(BACK) + [vmem] * (1 if reduction is None else 2),
        scratch_shapes=[pltpu.VMEM((D, FF), bf)] * 2
        + [pltpu.VMEM(a.shape[1:], a.dtype) for a in kept_in]
        + [pltpu.VMEM((SEQ, columns), bf) for _, columns in BACK]
        + [
            pltpu.VMEM((SEQ, D), bf), pltpu.VMEM((SEQ, D), f32), pltpu.VMEM((SEQ, D), f32), pltpu.VMEM((SEQ, D), bf),
            pltpu.VMEM((16, D), f32),
            pltpu.SemaphoreType.DMA((8,)), pltpu.SemaphoreType.DMA((len(BACK_KEPT),)),
            pltpu.SemaphoreType.DMA((len(BACK),)),
        ]
        + scratch,
        compiler_params=pltpu.CompilerParams(vmem_limit_bytes=60 * 2**20, **more),
    )(*weights, gains, select, mask, back_top, *kept_in, *operands)
    back = dict(zip([name for name, _ in BACK], outs))
    pairs = []
    for layer in range(2):
        left = lambda name: (kept[KEPT_INDEX[name]], layer)
        right = lambda name: (back[name], layer)
        pairs += [
            (left("normed"), right("back_packed")), (left("mixed"), right("back_attn")),
            (left("second"), right("back_inner")), (right("back_branch"), left("upper")),
        ]
    return pairs, outs[len(BACK)], outs[len(BACK) + 1 :]


ROWS_AT_ONCE = 192
HEAD_WEIGHTS = ((HW, 3 * HW), (HW, HW), (HW, HW)) * HB + (
    (HW, D), (HW, HW), (HW, HW), (HW, HW), (HW, FREQ), (HW, 128), (HW, 128)
)
HEAD_LEFT = (3, 1, 1, 1, 1) * HB + (1, 1, 1, 1, 1, 1, 1, 1)


def sigmoid(x):
    return 0.5 + 0.5 * jnp.tanh(0.5 * x)


def head_kernel(tokens, *refs):
    (embed_ref, noisy_ref, target_ref, grad_col_ref, loss_col_ref, bias_ref, cond_ref), refs = refs[:7], refs[7:]
    count = len(HEAD_WEIGHTS)
    block_hbm, edge_hbm, refs = refs[:HB], refs[HB : HB + 7], refs[HB + 7 :]
    weight_hbm = [
        block.at[:, pl.ds(column, width)]
        for block in block_hbm
        for column, width in ((0, 3 * HW), (3 * HW, HW), (4 * HW, HW))
    ] + list(edge_hbm)
    left_hbm, refs = refs[: len(HEAD_LEFT)], refs[len(HEAD_LEFT) :]
    (pred_ref, back_cond_ref, back_token_ref, bias_grad_ref, loss_ref), refs = refs[:5], refs[5:]
    weights, refs = refs[:count], refs[count:]
    left, refs = refs[: len(HEAD_LEFT)], refs[len(HEAD_LEFT) :]
    (
        time_inner, conditioning, projected, cond_sum, stream, back_silu, t0, t1, t2,
        scale1, normed, inner, gate, branch, inverse, weight_sem, left_sem,
    ) = refs
    cond_t, time_two_t, shift_t, scale_t, time_one_t, in_t, out_t = weights[3 * HB :]
    per_block = 5
    silu_cond, time_hidden, back_time, back_time_inner, back_shift, back_scale, final_low, back_low = left[
        per_block * HB :
    ]
    bf = jnp.bfloat16

    def fetch(k):
        return pltpu.make_async_copy(weight_hbm[k], weights[k], weight_sem.at[k])

    order = [3 * HB, 3 * HB + 4, 3 * HB + 1, 3 * HB + 5]
    for b in range(HB):
        order += [3 * b, 3 * b + 1, 3 * b + 2]
    order += [3 * HB + 2, 3 * HB + 3, 3 * HB + 6]
    for k in order:
        fetch(k).start()

    def nn(x, w):
        return jnp.dot(x, w, preferred_element_type=jnp.float32)

    def nt(x, w):
        return lax.dot_general(x, w, (((1,), (1,)), ((), ())), preferred_element_type=jnp.float32)

    def by_rows(body):
        for i in range(0, tokens, ROWS_AT_ONCE):
            body(slice(i, i + ROWS_AT_ONCE))

    bias_grad_ref[...] = jnp.zeros_like(bias_grad_ref)
    loss_ref[...] = jnp.zeros_like(loss_ref)
    cond_sum[...] = jnp.zeros_like(cond_sum)

    def bias(row):
        return bias_ref[row : row + 1, :]

    def add_bias_grad(row, value):
        bias_grad_ref[row : row + 1, :] += jnp.sum(value.astype(jnp.float32), 0, keepdims=True)

    @pl.loop(0, COPIES)
    def _(c):
        def need(*numbers):
            @pl.when(c == 0)
            def _():
                for k in numbers:
                    fetch(k).wait()

        def leave(k):
            return pltpu.make_async_copy(left[k], left_hbm[k].at[c], left_sem.at[k])

        def room(*numbers):
            @pl.when(c > 0)
            def _():
                for k in numbers:
                    leave(k).wait()

        base = per_block * HB
        room(base, base + 1)
        need(3 * HB)

        @pl.when(c == 0)
        def _():
            projected[...] = nt(cond_ref[...], cond_t[...])

        need(3 * HB + 4, 3 * HB + 1, 3 * HB + 5)
        time_inner[...] = nt(embed_ref[c], time_one_t[...])

        def _(r):
            value = time_inner[r, :] + bias(10)
            time_inner[r, :] = value
            time_hidden[r, :] = (value * sigmoid(value)).astype(bf)
        by_rows(_)
        leave(base + 1).start()
        t0[...] = nt(time_hidden[...], time_two_t[...])
        stream[...] = nt(noisy_ref[c], in_t[...])

        def _(r):
            value = projected[r, :] + (t0[r, :] + bias(11))
            conditioning[r, :] = value
            silu_cond[r, :] = (value * sigmoid(value)).astype(bf)
            stream[r, :] = stream[r, :] + bias(14)
        by_rows(_)
        leave(base).start()

        for b in range(HB):
            w_mod, w_up, w_down = weights[3 * b : 3 * b + 3]
            bm, shaped, back_inner, back_branch, hidden = left[per_block * b : per_block * (b + 1)]
            room(*range(per_block * b, per_block * (b + 1)))
            need(3 * b)
            t0[...] = nn(silu_cond[...], w_mod[:, :HW])
            t1[...] = nn(silu_cond[...], w_mod[:, HW : 2 * HW])
            gate[b] = nn(silu_cond[...], w_mod[:, 2 * HW :])

            def _(r):
                value = stream[r, :]
                centred = value - jnp.mean(value, -1, keepdims=True)
                inv = lax.rsqrt(jnp.mean(centred * centred, -1, keepdims=True) + NORM_EPS)
                n = centred * inv
                s = 1.0 + (t1[r, :] + bias(5 * b + 1))
                inverse[b, r, :] = jnp.broadcast_to(inv, (ROWS_AT_ONCE, 128))
                normed[b, r, :] = n
                scale1[b, r, :] = s
                shaped[r, :] = (n * s + (t0[r, :] + bias(5 * b))).astype(bf)
            by_rows(_)
            leave(per_block * b + 1).start()
            need(3 * b + 1)
            inner[b] = nn(shaped[...], w_up[...])

            def _(r):
                value = inner[b, r, :] + bias(5 * b + 3)
                inner[b, r, :] = value
                hidden[r, :] = (value * sigmoid(value)).astype(bf)
            by_rows(_)
            leave(per_block * b + 4).start()
            need(3 * b + 2)
            branch[b] = nt(hidden[...], w_down[...])

            def _(r):
                value = branch[b, r, :] + bias(5 * b + 4)
                g = gate[b, r, :] + bias(5 * b + 2)
                branch[b, r, :] = value
                gate[b, r, :] = g
                stream[r, :] = stream[r, :] + g * value
            by_rows(_)

        need(3 * HB + 2, 3 * HB + 3, 3 * HB + 6)
        room(*range(base + 2, base + 8))
        t0[...] = nt(silu_cond[...], shift_t[...])
        t1[...] = nt(silu_cond[...], scale_t[...])
        def _(r):
            value = stream[r, :]
            centred = value - jnp.mean(value, -1, keepdims=True)
            inv = lax.rsqrt(jnp.mean(centred * centred, -1, keepdims=True) + NORM_EPS)
            n = centred * inv
            s = 1.0 + (t1[r, :] + bias(13))
            inverse[HB, r, :] = jnp.broadcast_to(inv, (ROWS_AT_ONCE, 128))
            t2[r, :] = n
            t1[r, :] = s
            final_low[r, :] = (n * s + (t0[r, :] + bias(12))).astype(bf)
        by_rows(_)
        leave(base + 6).start()
        difference = nn(final_low[...], out_t[...]) - target_ref[c]
        loss_ref[...] += loss_col_ref[c] * difference * difference
        pred_ref[c] = (grad_col_ref[c] * difference).astype(bf)
        t0[...] = nt(pred_ref[c], out_t[...])

        def _(r):
            back = t0[r, :]
            n = t2[r, :]
            low_shift, low_scale = back.astype(bf), (back * n).astype(bf)
            back_shift[r, :] = low_shift
            back_scale[r, :] = low_scale
            up = back * t1[r, :]
            add_bias_grad(12, low_shift)
            add_bias_grad(13, low_scale)
            stream[r, :] = inverse[HB, r, :1] * (
                up - jnp.mean(up, -1, keepdims=True) - n * jnp.mean(up * n, -1, keepdims=True)
            )
        by_rows(_)
        leave(base + 4).start()
        leave(base + 5).start()
        back_silu[...] = nn(back_shift[...], shift_t[...]) + nn(back_scale[...], scale_t[...])

        for b in reversed(range(HB)):
            w_mod, w_up, w_down = weights[3 * b : 3 * b + 3]
            bm, shaped, back_inner, back_branch, hidden = left[per_block * b : per_block * (b + 1)]

            def _(r):
                back = stream[r, :]
                low = (back * gate[b, r, :]).astype(bf)
                low_gate = (back * branch[b, r, :]).astype(bf)
                back_branch[r, :] = low
                bm[r, 2 * HW :] = low_gate
                add_bias_grad(5 * b + 4, low)
                add_bias_grad(5 * b + 2, low_gate)
            by_rows(_)
            leave(per_block * b + 3).start()
            t0[...] = nn(back_branch[...], w_down[...])

            def _(r):
                value = inner[b, r, :]
                s = sigmoid(value)
                low = (t0[r, :] * (s * (1.0 + value * (1.0 - s)))).astype(bf)
                back_inner[r, :] = low
                add_bias_grad(5 * b + 3, low)
            by_rows(_)
            leave(per_block * b + 2).start()
            t0[...] = nt(back_inner[...], w_up[...])

            def _(r):
                back = t0[r, :]
                n = normed[b, r, :]
                low_shift, low_scale = back.astype(bf), (back * n).astype(bf)
                bm[r, :HW] = low_shift
                bm[r, HW : 2 * HW] = low_scale
                add_bias_grad(5 * b, low_shift)
                add_bias_grad(5 * b + 1, low_scale)
                up = back * scale1[b, r, :]
                stream[r, :] = stream[r, :] + inverse[b, r, :1] * (
                    up - jnp.mean(up, -1, keepdims=True) - n * jnp.mean(up * n, -1, keepdims=True)
                )
            by_rows(_)
            leave(per_block * b).start()
            back_silu[...] += nt(bm[...], w_mod[...])

        def _(r):
            value = conditioning[r, :]
            s = sigmoid(value)
            back = back_silu[r, :] * (s * (1.0 + value * (1.0 - s)))
            low, low_stream = back.astype(bf), stream[r, :].astype(bf)
            cond_sum[r, :] = cond_sum[r, :] + back
            back_time[r, :] = low
            back_low[r, :] = low_stream
            add_bias_grad(11, low)
            add_bias_grad(14, low_stream)
        by_rows(_)
        leave(base + 2).start()
        leave(base + 7).start()
        t0[...] = nn(back_time[...], time_two_t[...])

        def _(r):
            value = time_inner[r, :]
            s = sigmoid(value)
            low = (t0[r, :] * (s * (1.0 + value * (1.0 - s)))).astype(bf)
            back_time_inner[r, :] = low
            add_bias_grad(10, low)
        by_rows(_)
        leave(base + 3).start()

    back_cond_ref[...] = cond_sum[...].astype(bf)
    back_token_ref[...] = nn(back_cond_ref[...], cond_t[...]).astype(bf)
    for k in range(len(HEAD_LEFT)):
        pltpu.make_async_copy(left[k], left_hbm[k].at[COPIES - 1], left_sem.at[k]).wait()


def head_pass(
    blocks, edges, biases, cond_rows, clean_rows, noise_rows, step_rows, weight_rows, weight_total
):
    bf = jnp.bfloat16
    tokens = cond_rows.shape[0]
    half_freq = FREQ // 2
    frequencies = jnp.exp(-math.log(10000.0) * jnp.arange(half_freq, dtype=jnp.float32) / half_freq)
    step_times = step_rows.astype(jnp.float32).T
    angles = step_times[..., None] * frequencies
    time_embed = jnp.concatenate([jnp.cos(angles), jnp.sin(angles)], -1).astype(bf)
    phase_angle = (step_times / TSTEPS + 0.008) / 1.008 * (math.pi / 2)
    keep_part = jnp.cos(phase_angle)[..., None]
    noise_part = jnp.sin(phase_angle)[..., None]
    clean_copies = clean_rows.astype(jnp.float32)[None]
    fresh_noise = noise_rows.astype(jnp.float32).reshape(tokens, COPIES, CH).transpose(1, 0, 2)
    wide = ((0, 0), (0, 0), (0, 128 - CH))
    noisy = jnp.pad((keep_part * clean_copies + noise_part * fresh_noise).astype(bf), wide)
    target = jnp.pad(keep_part * fresh_noise - noise_part * clean_copies, wide)
    by_copy = jnp.broadcast_to(weight_rows.T[..., None], (COPIES, tokens, 128))
    f32 = jnp.float32
    vmem, hbm = pl.BlockSpec(memory_space=pltpu.VMEM), pl.BlockSpec(memory_space=pl.ANY)
    lefts = [(COPIES, tokens, k * HW) for k in HEAD_LEFT]
    units = lambda *lead: pltpu.VMEM((*lead, tokens, HW), f32)
    outs = pl.pallas_call(
        functools.partial(head_kernel, tokens),
        out_shape=[jax.ShapeDtypeStruct(shape, bf) for shape in lefts]
        + [
            jax.ShapeDtypeStruct((COPIES, tokens, 128), bf),
            jax.ShapeDtypeStruct((tokens, HW), bf),
            jax.ShapeDtypeStruct((tokens, D), bf),
            jax.ShapeDtypeStruct((5 * (HB + 1) + 1, HW), f32),
            jax.ShapeDtypeStruct((tokens, 128), f32),
        ],
        in_specs=[vmem] * 7 + [hbm] * (HB + 7),
        out_specs=[hbm] * len(HEAD_LEFT) + [vmem] * 5,
        scratch_shapes=[pltpu.VMEM(shape, bf) for shape in HEAD_WEIGHTS]
        + [pltpu.VMEM((tokens, k * HW), bf) for k in HEAD_LEFT]
        + [units()] * 9
        + [units(HB)] * 5
        + [
            pltpu.VMEM((HB + 1, tokens, 128), f32),
            pltpu.SemaphoreType.DMA((len(HEAD_WEIGHTS),)), pltpu.SemaphoreType.DMA((len(HEAD_LEFT),)),
        ],
        compiler_params=pltpu.CompilerParams(vmem_limit_bytes=60 * 2**20),
    )(
        time_embed, noisy, target, by_copy * (2.0 / (CH * weight_total)), by_copy * (1.0 / CH),
        jnp.pad(biases.reshape(5 * (HB + 1), HW), ((0, 1), (0, 0))), cond_rows,
        *blocks, *edges,
    )
    left = [a.reshape(COPIES * tokens, -1) for a in outs[: len(HEAD_LEFT)]]
    back_pred, back_cond, back_tokens, bias_grad, loss_part = outs[len(HEAD_LEFT) :]
    silu_cond, time_hidden, back_time, back_time_inner, back_shift, back_scale, final_low, back_low = left[5 * HB :]
    pairs = []
    for b in range(HB):
        bm, shaped, back_inner, back_branch, hidden = left[5 * b : 5 * (b + 1)]
        pairs += [(silu_cond, bm), (shaped, back_inner), (back_branch, hidden)]
    pairs += [(back_time, time_hidden), (back_shift, silu_cond), (back_scale, silu_cond)]
    flat = lambda a: a.reshape(COPIES * tokens, -1)
    small = (
        dot_left(back_cond, cond_rows),
        dot_left(back_time_inner, flat(time_embed)),
        dot_left(back_low, flat(noisy))[:, :CH],
        dot_left(final_low, flat(back_pred))[:, :CH],
    )
    bias_grad = bias_grad[: 5 * (HB + 1)].reshape(HB + 1, 5 * HW)
    return (jnp.sum(loss_part), pairs, small, bias_grad, back_tokens)


def adamw(master, first, second, gradient, factor, step_rate):
    clipped = gradient * factor
    first_new = BETA_ONE * first + (1.0 - BETA_ONE) * clipped
    second_new = BETA_TWO * second + (1.0 - BETA_TWO) * clipped * clipped
    mean_hat = first_new / (1.0 - BETA_ONE**ADAM_STEP)
    var_hat = second_new / (1.0 - BETA_TWO**ADAM_STEP)
    updated = master - step_rate * (mean_hat / (jnp.sqrt(var_hat) + ADAM_EPS) + DECAY_RATE * master)
    return (updated, first_new, second_new)


TRUNK_PARTS = (3 * D, D, FF, FF)
HEAD_PARTS = (3 * HW, HW, HW)
EDGE_PARTS = (D, HW, HW, HW, FREQ, 128)
TRUNK_WIDTH = 768
HEAD_WIDTH = 512


def gather_plan(part_sets, limit):
    chunks, shapes = [], []
    for source, index, rows, parts in part_sets:
        column = 0
        for part in parts:
            for k in range(0, part, limit):
                chunks.append((source, index, column + k, len(shapes), k, min(limit, part - k)))
            shapes.append((rows, part))
            column += part
    return chunks, shapes


def plain_gather(sources, chunks, shapes):
    ends = {}
    for source, index, column, result, at, width in chunks:
        start, stop = ends.get(result, (source, index, column, column))[2:]
        ends[result] = (source, index, min(start, column), max(stop, column + width))
    wholes = {}
    results = []
    for number in range(len(shapes)):
        source, index, start, stop = ends[number]
        if (source, index) not in wholes:
            block = sources[source] if index is None else sources[source][index]
            wholes[source, index] = lax.all_gather(block, AXES, axis=0, tiled=True)
        results.append(wholes[source, index][:, start:stop])
    return results


def scatter_sum(values):
    low = lax.psum_scatter(values, "dp", scatter_dimension=0, tiled=True)
    return lax.psum_scatter(low, "fsdp", scatter_dimension=0, tiled=True)


def on_device(
    mesh_shape,
    latents, orders, mask_counts, noise, timesteps, loss_weights,
    block_weights, block_gains, entry_table, head_weights, head_biases, head_edges,
    first_blocks, first_gains, first_entry, first_head, first_biases, first_edges,
    second_blocks, second_gains, second_entry, second_head, second_biases, second_edges,
):
    dp_count, nz = mesh_shape["dp"], mesh_shape["fsdp"]
    devices = dp_count * nz
    me = lax.axis_index("dp") * nz + lax.axis_index("fsdp")
    r0, r1 = D // devices, HW // devices
    direct = dp_count == 8 and nz > 1 and (D // 8) % 16 == 0
    bf = jnp.bfloat16

    low_blocks = block_weights.astype(bf)
    local_total = jnp.sum(mask_counts)
    terms, rest = [local_total.astype(bf)], jnp.sum(loss_weights)
    for _ in range(3):
        terms.append(lax.reduce_precision(rest, 8, 7).astype(bf))
        rest = rest - terms[-1].astype(jnp.float32)
    low_entry = jnp.concatenate(
        [
            entry_table.T.astype(bf), block_gains.reshape(4, r0).T.astype(bf),
            jnp.broadcast_to(jnp.stack(terms), (r0, 4)), jnp.zeros((r0, 104), bf),
        ],
        1,
    )
    low_head = head_weights.astype(bf)
    edge = head_edges.T.astype(bf)
    base = D + 2 * CH
    low_edges = jnp.concatenate(
        [
            edge[:, :D], edge[:, base + FREQ :], edge[:, base : base + FREQ], edge[:, D:base],
            head_biases.reshape((HB + 1) * 5, r1).T.astype(bf), jnp.zeros((r1, 81), bf),
        ],
        1,
    )
    chunks, shapes = gather_plan(
        [(1, None, r0, (TRUNK_WIDTH,)), (0, 0, r0, TRUNK_PARTS), (0, 1, r0, TRUNK_PARTS)], TRUNK_WIDTH
    )
    later = [(0, None, r1, EDGE_PARTS)]
    edge_chunks, edge_shapes = gather_plan(later, HEAD_WIDTH)
    whole = lambda arrays: [a.reshape(devices * a.shape[4], -1) for a in arrays]
    if direct:
        trunk = whole(gather_rows([low_blocks, low_entry], chunks, shapes, nz, 1))
    else:
        trunk = plain_gather([low_blocks, low_entry], chunks, shapes)
        edge_mats = plain_gather([low_edges], edge_chunks, edge_shapes)
    head_blocks = [lax.all_gather(low_head[b], AXES, axis=0, tiled=True) for b in range(HB)]

    early = trunk[0][::r0, 2 * SEQ + CH + 4 : 2 * SEQ + CH + 8].astype(jnp.float32)
    counts = early[:, 0].astype(jnp.int32)
    weight_total = jnp.sum(early[:, 1:])
    count_ends = jnp.cumsum(counts)
    count_starts = count_ends - counts
    offset = jnp.sum(jnp.where(jnp.arange(devices) == me, count_starts, 0))

    order_row = orders[0]
    clean = latents[0]
    ids = jnp.arange(LAT, dtype=jnp.int32)
    masked = jnp.any((order_row[:, None] == ids[None, :]) & (ids < local_total)[:, None], 0)
    key_keep = jnp.concatenate([jnp.ones((BUF,), jnp.float32), 1.0 - masked.astype(jnp.float32)])
    positions = jnp.arange(SEQ, dtype=jnp.int32)
    columns = jnp.arange(TRUNK_WIDTH, dtype=jnp.int32)
    pick_rows = jnp.concatenate([positions, SEQ + positions, 2 * SEQ + CH + jnp.arange(16, dtype=jnp.int32)])
    select = (pick_rows[:, None] == columns[None, :]).astype(bf) + jnp.pad(
        clean, ((BUF, SEQ + 16), (2 * SEQ, TRUNK_WIDTH - 2 * SEQ - CH))
    )
    if direct:
        top_rows, gains, kept, edge_mats = trunk_forward(
            trunk[0], trunk[1:9], select, key_keep[None], (nz, edge_chunks), [low_edges], edge_shapes, 2
        )
        edge_mats = whole(edge_mats)
    else:
        top_rows, gains, kept, _ = trunk_forward(trunk[0], trunk[1:9], select, key_keep[None])

    capacity = (LAT + devices - 1) // devices
    slots = devices * capacity
    slot_ids = jnp.arange(slots, dtype=jnp.int32)
    slot_token = jnp.mod(slot_ids // capacity - offset, devices) + devices * (slot_ids % capacity)
    slot_position = jnp.sum(
        jnp.where(slot_token[:, None] == ids[None, :], order_row[None, :], 0), 1
    )
    pick = (
        (slot_position[:, None] == ids[None, :]) & (slot_token < local_total)[:, None]
    ).astype(bf)
    outgoing = dot_plain(
        pick, jnp.concatenate([top_rows, clean, jnp.zeros((LAT, 112), bf)], 1)
    ).astype(bf)
    incoming = lax.all_to_all(
        outgoing.reshape(devices, capacity, -1), AXES, split_axis=0, concat_axis=0, tiled=True
    ).reshape(slots, -1)
    head_rows = noise.shape[0]
    token_ids = jnp.arange(head_rows, dtype=jnp.int32) * devices + me
    inside = (token_ids[:, None] >= count_starts[None, :]) & (token_ids[:, None] < count_ends[None, :])
    first_token = count_starts + jnp.mod(me - count_starts, devices)
    source_slot = (
        jnp.arange(devices, dtype=jnp.int32)[None, :] * capacity
        + (token_ids[:, None] - first_token[None, :]) // devices
    )
    row_slot = jnp.sum(jnp.where(inside, source_slot, 0), 1)
    place = (row_slot[:, None] == slot_ids[None, :]).astype(bf)
    received = dot_plain(place, incoming).astype(bf)

    misc = edge_mats[5]
    biases = (
        misc[:, 2 * CH : 2 * CH + 5 * (HB + 1)]
        .reshape(devices, r1, HB + 1, 5)
        .transpose(2, 0, 3, 1)
        .reshape(HB + 1, 5 * HW)
        .astype(jnp.float32)
    )
    loss_local, head_pairs, small, bias_grad, back_tokens = head_pass(
        head_blocks,
        edge_mats[:5]
        + [
            jnp.pad(misc[:, :CH], ((0, 0), (0, 128 - CH))),
            jnp.pad(misc[:, CH : 2 * CH], ((0, 0), (0, 128 - CH))),
        ],
        biases,
        received[:, :D],
        received[:, D : D + CH],
        noise,
        timesteps,
        loss_weights,
        weight_total,
    )
    grad_cond_t, grad_time_one_t, grad_in_t, grad_out_t = small
    bias_t = (
        bias_grad.reshape(HB + 1, devices, 5, r1).transpose(1, 3, 0, 2).reshape(HW, 5 * (HB + 1))
    )
    head_small = jnp.concatenate(
        [grad_cond_t, grad_time_one_t, grad_in_t, grad_out_t, bias_t, jnp.zeros((HW, 465), jnp.float32)], 1
    ).astype(bf)
    returning = dot_left(place, back_tokens.astype(bf)).astype(bf)
    returned = lax.all_to_all(
        returning.reshape(devices, capacity, D), AXES, split_axis=0, concat_axis=0, tiled=True
    ).reshape(slots, D)
    back_top = jnp.concatenate([jnp.zeros((BUF, D), jnp.float32), dot_left(pick, returned)], 0)
    reduction = None
    if direct:
        extras = jnp.stack(
            [head_small[:, k : k + HEAD_WIDTH] for k in range(0, head_small.shape[1], HEAD_WIDTH)]
        )
        reduction = reduce_setup(head_pairs, extras, HW, HEAD_WIDTH, (r1, HEAD_WIDTH), nz)
    trunk_pairs, trunk_small, tall = trunk_backward(
        gains, trunk[1:9], select, key_keep[None], back_top, kept, reduction, 4
    )
    if direct:
        tall = tall[0].transpose(1, 0, 2).reshape(r1, -1)
    else:
        tall = jnp.concatenate(
            [scatter_sum(dot_left(x, y)) for x, y in head_pairs]
            + [scatter_sum(head_small.astype(jnp.float32))],
            1,
        )
    if direct:
        wide = reduce_products(
            trunk_pairs, trunk_small[None], D, TRUNK_WIDTH, (2 * r0, TRUNK_WIDTH // 2), nz, 5
        )
        wide = wide.transpose(1, 0, 2).reshape(r0, -1)
    else:
        wide = jnp.concatenate(
            [scatter_sum(dot_left(x[0][x[1]], y[0][y[1]])) for x, y in trunk_pairs]
            + [scatter_sum(trunk_small.astype(jnp.float32))],
            1,
        )
    block_columns, head_columns = sum(TRUNK_PARTS), sum(HEAD_PARTS)
    block_grad = jnp.stack([wide[:, l * block_columns : (l + 1) * block_columns] for l in range(2)])
    rest = wide[:, 2 * block_columns :]
    entry_grad = rest[:, : 2 * SEQ + CH].T
    gain_grad = rest[:, 2 * SEQ + CH : 2 * SEQ + CH + 4].T.reshape(2, 2, r0)
    head_grad = jnp.stack([tall[:, b * head_columns : (b + 1) * head_columns] for b in range(HB)])
    rest = tall[:, HB * head_columns :]
    shared = rest[:, 3 * HW :]
    edge_grad = jnp.concatenate(
        [
            shared[:, :D], shared[:, D + FREQ : D + FREQ + 2 * CH], shared[:, D : D + FREQ],
            rest[:, : 3 * HW],
        ],
        1,
    ).T
    bias_grad = (
        shared[:, D + FREQ + 2 * CH : D + FREQ + 2 * CH + 5 * (HB + 1)].T.reshape(HB + 1, 5 * r1)
    )
    squares = jnp.sum(wide * wide) + jnp.sum(tall * tall)
    late = exchange(jnp.stack([loss_local, squares]), dp_count, nz, 6)
    loss_sum = jnp.sum(late[:, 0])
    grad_norm = jnp.sqrt(jnp.sum(late[:, 1]))
    factor = CLIP_NORM / jnp.maximum(grad_norm, CLIP_NORM)
    new = [
        adamw(block_weights, first_blocks, second_blocks, block_grad, factor, LEARN_RATE),
        adamw(block_gains, first_gains, second_gains, gain_grad, factor, GAIN_RATE),
        adamw(entry_table, first_entry, second_entry, entry_grad, factor, LEARN_RATE),
        adamw(head_weights, first_head, second_head, head_grad, factor, LEARN_RATE),
        adamw(head_biases, first_biases, second_biases, bias_grad, factor, LEARN_RATE),
        adamw(head_edges, first_edges, second_edges, edge_grad, factor, LEARN_RATE),
    ]
    return tuple(new[i][k] for k in range(3) for i in range(6)) + (loss_sum, weight_total, grad_norm)


def solution(mesh):
    rows = [P(AXES, None, None), P(AXES, None), P(AXES), P(AXES, None), P(AXES, None), P(AXES, None)]
    state = [
        P(None, AXES, None), P(None, None, AXES), P(None, AXES),
        P(None, AXES, None), P(None, AXES), P(None, AXES),
    ]
    return jax.shard_map(
        functools.partial(on_device, dict(mesh.shape)),
        mesh=mesh,
        in_specs=tuple(rows + state * 3),
        out_specs=tuple(state * 3 + [P(), P(), P()]),
        check_vma=False,
    )
```

```python
import functools
import math

import jax
import jax.numpy as jnp
from jax import lax
from jax.experimental import pallas as pl
from jax.experimental.pallas import tpu as pltpu
from jax.sharding import PartitionSpec as P

D = 768
HEADS = 12
HD = 64
FF = 3072
HW = 1024
CH = 16
FREQ = 256
LAT = 256
BUF = 64
HB = 2
COPIES = 4
TSTEPS = 1000
ADAM_STEP = 5
SEQ = 320

BETA_ONE = 0.5
BETA_TWO = 0.5
LEARN_RATE = 0.03
GAIN_RATE = 0.3
DECAY_RATE = 0.02
ADAM_EPS = 1e-08
CLIP_NORM = 0.002
NORM_EPS = 1e-06
AXES = ("dp", "fsdp")
MESH_IDS = pl.DeviceIdType.MESH


REDUCE_LAGS = (0, 1, 3, 5, 7)
REDUCE_DEPTH = 3


def reduce_program(nz, row_count, width, columns_of, x_refs, y_refs, extra_ref, out_ref, scratch, between=None):
    (
        x_buf, y_buf, whole, land_core, first, land_first, second, land_second,
        last, last_low, land_last, extra_sem,
        load_sem, core_send, core_recv, first_send, first_recv, second_send, second_recv,
        last_send, last_recv, credit,
    ) = scratch
    dp, z = lax.axis_index("dp"), lax.axis_index("fsdp")
    core, xb, yb = lax.rem(dp, 2), lax.rem(dp // 2, 2), dp // 4
    group = row_count // 8
    part = group // nz
    starts, total = [], 0
    for columns in columns_of:
        starts.append(total)
        total += columns // width
    computed = total
    total += extra_ref.shape[0]

    core_peer = (dp + 1 - 2 * core, z)
    x_step, y_step = 2 - 4 * xb, 4 - 8 * yb
    z_peers = [(dp, lax.rem(z + s, nz)) for s in range(1, nz)]
    barrier = pltpu.get_barrier_semaphore()
    for peer in [core_peer, (dp + x_step, z), (dp + y_step, z)] + z_peers:
        pl.semaphore_signal(barrier, inc=1, device_id=peer, device_id_type=MESH_IDS)
    pl.semaphore_wait(barrier, 2 + nz)

    def loads(x_ref, y_ref, column, slot):
        return (
            pltpu.make_async_copy(x_ref, x_buf.at[slot], load_sem.at[0, slot]),
            pltpu.make_async_copy(
                y_ref.at[:, pl.ds(pl.multiple_of(column, 128), width)], y_buf.at[slot], load_sem.at[1, slot]
            ),
        )

    def prefetch(g):
        for number, columns in enumerate(columns_of):
            start, stop = starts[number], starts[number] + columns // width

            @pl.when((g >= start) & (g < stop))
            def _():
                for copy in loads(x_refs[number], y_refs[number], (g - start) * width, lax.rem(g, 2)):
                    copy.start()

    def core_copy(g):
        return pltpu.make_async_remote_copy(
            src_ref=whole.at[lax.rem(g, 2), 1 - core],
            dst_ref=land_core.at[lax.rem(g, 4)],
            send_sem=core_send.at[lax.rem(g, 2)],
            recv_sem=core_recv.at[lax.rem(g, 4)],
            device_id=core_peer,
            device_id_type=MESH_IDS,
        )

    depth = REDUCE_DEPTH

    def first_copy(g):
        p = lax.rem(g, 2)
        mine = (1 - p) * xb + p * yb
        return pltpu.make_async_remote_copy(
            src_ref=first.at[lax.rem(g, depth), 1 - mine],
            dst_ref=land_first.at[g],
            send_sem=first_send.at[lax.rem(g, depth)],
            recv_sem=first_recv.at[g],
            device_id=(dp + (1 - p) * x_step + p * y_step, z),
            device_id_type=MESH_IDS,
        )

    def second_copy(g):
        p = lax.rem(g, 2)
        mine = (1 - p) * yb + p * xb
        return pltpu.make_async_remote_copy(
            src_ref=second.at[lax.rem(g, depth), 1 - mine],
            dst_ref=land_second.at[g],
            send_sem=second_send.at[lax.rem(g, depth)],
            recv_sem=second_recv.at[g],
            device_id=(dp + (1 - p) * y_step + p * x_step, z),
            device_id_type=MESH_IDS,
        )

    def last_copies(g):
        return [
            pltpu.make_async_remote_copy(
                src_ref=last_low.at[lax.rem(g, depth), lax.rem(z + s, nz)],
                dst_ref=land_last.at[g, s - 1],
                send_sem=last_send.at[lax.rem(g, depth), s - 1],
                recv_sem=last_recv.at[g, s - 1],
                device_id=z_peers[s - 1],
                device_id_type=MESH_IDS,
            )
            for s in range(1, nz)
        ]

    low_rows, low_width = last_low.shape[2:]
    folds = width // low_width

    def fold(block):
        return jnp.concatenate([block[:, k * low_width : (k + 1) * low_width] for k in range(folds)], 0)

    def stage_core(g):
        slot = lax.rem(g, 2)

        @pl.when(g >= 2)
        def _():
            core_copy(g - 2).wait_send()

        def put(number, value):
            yx, c = number // 2, number % 2
            whole[slot, c, yx] = value

        @pl.when(g < computed)
        def _():
            for copy in loads(x_refs[0], y_refs[0], 0, slot):
                copy.wait()
            product = lax.dot_general(
                x_buf[slot], y_buf[slot], (((0,), (0,)), ((), ())), preferred_element_type=jnp.float32
            )
            for number in range(8):
                put(number, product[number * group : (number + 1) * group].astype(jnp.bfloat16))

        @pl.when(g >= computed)
        def _():
            copies = [
                pltpu.make_async_copy(
                    extra_ref.at[g - computed, pl.ds(number * group, group), :],
                    whole.at[slot, number % 2, number // 2],
                    extra_sem.at[number],
                )
                for number in range(8)
            ]
            for copy in copies:
                copy.start()
            for copy in copies:
                copy.wait()

        @pl.when(g >= 4)
        def _():
            pl.semaphore_wait(credit, 1)
        core_copy(g).start()

    def stage_first(g):
        p = lax.rem(g, 2)

        @pl.when(g >= depth)
        def _():
            first_copy(g - depth).wait_send()
        core_copy(g).wait_recv()
        for f in range(2):
            for s in range(2):
                yx = (1 - p) * (2 * s + f) + p * (2 * f + s)
                first[lax.rem(g, depth), f, s] = (
                    whole[lax.rem(g, 2), core, yx].astype(jnp.float32)
                    + land_core[lax.rem(g, 4), yx].astype(jnp.float32)
                ).astype(jnp.bfloat16)

        @pl.when(g < total - 4)
        def _():
            pl.semaphore_signal(credit, inc=1, device_id=core_peer, device_id_type=MESH_IDS)
        first_copy(g).start()

    def stage_second(g):
        p = lax.rem(g, 2)
        mine = (1 - p) * xb + p * yb

        @pl.when(g >= depth)
        def _():
            second_copy(g - depth).wait_send()
        first_copy(g).wait_recv()
        for s in range(2):
            second[lax.rem(g, depth), s] = (
                first[lax.rem(g, depth), mine, s].astype(jnp.float32) + land_first[g, s].astype(jnp.float32)
            ).astype(jnp.bfloat16)
        second_copy(g).start()

    def stage_last(g):
        p = lax.rem(g, 2)
        mine = (1 - p) * yb + p * xb

        @pl.when(g >= depth)
        def _():
            for copy in last_copies(g - depth):
                copy.wait_send()
        second_copy(g).wait_recv()
        summed = second[lax.rem(g, depth), mine].astype(jnp.float32) + land_second[g].astype(jnp.float32)
        for k in range(nz):
            block = fold(summed[k * part : (k + 1) * part])
            last[lax.rem(g, depth), k] = block
            last_low[lax.rem(g, depth), k] = block.astype(jnp.bfloat16)
        for copy in last_copies(g):
            copy.start()

    def stage_out(g):
        for copy in last_copies(g):
            copy.wait_recv()
        value = last[lax.rem(g, depth), z]
        for s in range(1, nz):
            value = value + land_last[g, s - 1].astype(jnp.float32)
        for k in range(folds):
            out_ref[g, :, pl.ds(k * low_width, low_width)] = value[k * part : (k + 1) * part]

    lags = REDUCE_LAGS
    prefetch(0)

    @pl.loop(0, total + lags[-1])
    def _(i):
        for stage, lag in zip((stage_out, stage_last, stage_second, stage_first), lags[:0:-1]):
            @pl.when((i >= lag) & (i < total + lag))
            def _():
                stage(i - lag)

        @pl.when(i + 1 < computed)
        def _():
            prefetch(i + 1)

        @pl.when(i < total)
        def _():
            stage_core(i)

        if between is not None:
            between(i)

    for g in range(max(total - 2, 0), total):
        core_copy(g).wait_send()
    for g in range(max(total - depth, 0), total):
        first_copy(g).wait_send()
        second_copy(g).wait_send()
        for copy in last_copies(g):
            copy.wait_send()


def reduce_scratch(tokens, row_count, width, total, low_shape, nz):
    bf, group = jnp.bfloat16, row_count // 8
    dma, depth = pltpu.SemaphoreType.DMA, REDUCE_DEPTH
    return [
        pltpu.VMEM((2, tokens, row_count), bf),
        pltpu.VMEM((2, tokens, width), bf),
        pltpu.VMEM((2, 2, 4, group, width), bf),
        pltpu.VMEM((4, 4, group, width), bf),
        pltpu.VMEM((depth, 2, 2, group, width), bf),
        pltpu.VMEM((total, 2, group, width), bf),
        pltpu.VMEM((depth, 2, group, width), bf),
        pltpu.VMEM((total, group, width), bf),
        pltpu.VMEM((depth, nz, *low_shape), jnp.float32),
        pltpu.VMEM((depth, nz, *low_shape), bf),
        pltpu.VMEM((total, nz - 1, *low_shape), bf),
        dma((8,)),
        dma((2, 2)), dma((2,)), dma((4,)), dma((depth,)), dma((total,)), dma((depth,)), dma((total,)),
        dma((depth, nz - 1)), dma((total, nz - 1)), pltpu.SemaphoreType.REGULAR,
    ]


def gather_program(nz, chunks, sources, results, sems):
    own_sem, last_send, last_recv, first_send, first_recv, second_send, second_recv, core_send, core_recv = sems
    dp, z = lax.axis_index("dp"), lax.axis_index("fsdp")
    core, xb, yb = lax.rem(dp, 2), lax.rem(dp // 2, 2), dp // 4
    core_peer = (dp + 1 - 2 * core, z)
    x_peer, y_peer = (dp + 2 - 4 * xb, z), (dp + 4 - 8 * yb, z)
    z_peers = [(dp, lax.rem(z + s, nz)) for s in range(1, nz)]
    barrier = pltpu.get_barrier_semaphore()
    for peer in [core_peer, x_peer, y_peer] + z_peers:
        pl.semaphore_signal(barrier, inc=1, device_id=peer, device_id_type=MESH_IDS)
    pl.semaphore_wait(barrier, 2 + nz)

    def remote(source, target, send, recv, peer):
        return pltpu.make_async_remote_copy(
            src_ref=source, dst_ref=target, send_sem=send, recv_sem=recv, device_id=peer, device_id_type=MESH_IDS
        )

    def source_of(k):
        source, index, column, _, _, width = chunks[k]
        ref = sources[source] if index is None else sources[source].at[index]
        return ref.at[:, pl.ds(column, width)]

    def result_of(k):
        _, _, _, result, column, width = chunks[k]
        return results[result].at[:, :, :, :, :, pl.ds(column, width)]

    def own(k):
        return pltpu.make_async_copy(source_of(k), result_of(k).at[yb, xb, core, z], own_sem.at[k])

    def to_z(k, source, target):
        return [
            remote(source, target, last_send.at[k, s], last_recv.at[k, s], z_peers[s]) for s in range(nz - 1)
        ]

    def to_pair(k, late, along_y, source, target):
        send, recv = (second_send, second_recv) if late else (first_send, first_recv)
        return [remote(source, target, send.at[k], recv.at[k], y_peer if along_y else x_peer)]

    def stage(k, number):
        result = result_of(k)
        block = result.at[yb, xb, core, z]
        if number == 0:
            return to_z(k, source_of(k), block)
        if number == 1:
            ref = result.at[yb, xb, core]
            return to_pair(k, False, k % 2, ref, ref)
        ref = result.at[:, xb, core] if k % 2 else result.at[yb, :, core]
        return to_pair(k, True, 1 - k % 2, ref, ref)

    def across(k):
        ref = result_of(k).at[:, :, core]
        return remote(ref, ref, core_send.at[k], core_recv.at[k], core_peer)

    total = len(chunks)

    def pass_on(k, number):
        if number == 0:
            own(k).wait()
        for copy in stage(k, number):
            copy.wait_recv()
        for copy in stage(k, number + 1) if number < 2 else [across(k)]:
            copy.start()

    def step(i):
        for number in (2, 1, 0):
            if 0 <= i - 2 * (number + 1) < total:
                pass_on(i - 2 * (number + 1), number)
        if i < total:
            own(i).start()
            for copy in stage(i, 0):
                copy.start()

    def finish():
        for k in range(total):
            for copy in stage(k, 0) + stage(k, 1) + stage(k, 2) + [across(k)]:
                copy.wait_send()
            across(k).wait_recv()

    return total + 6, step, finish


def gather_sems(total, nz):
    dma = pltpu.SemaphoreType.DMA
    return [dma((total,)), dma((total, nz - 1)), dma((total, nz - 1))] + [dma((total,))] * 6


def gather_kernel(nz, chunks, source_count, *refs):
    sources, refs = refs[:source_count], refs[source_count:]
    result_count = 1 + max(chunk[3] for chunk in chunks)
    steps, step, finish = gather_program(nz, chunks, sources, refs[:result_count], refs[result_count:])
    for i in range(steps):
        step(i)
    finish()


def gather_rows(sources, chunks, shapes, nz, collective_id):
    return pl.pallas_call(
        functools.partial(gather_kernel, nz, chunks, len(sources)),
        out_shape=[jax.ShapeDtypeStruct((2, 2, 2, nz, *shape), jnp.bfloat16) for shape in shapes],
        in_specs=[pl.BlockSpec(memory_space=pl.ANY)] * len(sources),
        out_specs=[pl.BlockSpec(memory_space=pl.ANY)] * len(shapes),
        scratch_shapes=gather_sems(len(chunks), nz),
        compiler_params=pltpu.CompilerParams(
            collective_id=collective_id, has_side_effects=True, vmem_limit_bytes=60 * 2**20
        ),
    )(*sources)


def exchange_kernel(dp_count, nz, in_ref, out_ref, send_sem, recv_sem):
    devices = dp_count * nz
    me = lax.axis_index("dp") * nz + lax.axis_index("fsdp")

    def peer(step):
        there = lax.rem(me + step, devices)
        return (there // nz, lax.rem(there, nz))

    barrier = pltpu.get_barrier_semaphore()

    @pl.loop(1, devices)
    def _(step):
        pl.semaphore_signal(barrier, inc=1, device_id=peer(step), device_id_type=MESH_IDS)

    pl.semaphore_wait(barrier, devices - 1)

    def copy(step):
        return pltpu.make_async_remote_copy(
            src_ref=in_ref,
            dst_ref=out_ref.at[me],
            send_sem=send_sem.at[step - 1],
            recv_sem=recv_sem.at[step - 1],
            device_id=peer(step),
            device_id_type=MESH_IDS,
        )

    @pl.loop(1, devices)
    def _(step):
        copy(step).start()

    out_ref[me] = in_ref[...]

    @pl.loop(1, devices)
    def _(step):
        copy(step).wait()


def exchange(values, dp_count, nz, collective_id):
    devices = dp_count * nz
    tile = jnp.broadcast_to(jnp.pad(values, (0, 128 - values.shape[0])), (8, 128))
    out = pl.pallas_call(
        functools.partial(exchange_kernel, dp_count, nz),
        out_shape=jax.ShapeDtypeStruct((devices, 8, 128), jnp.float32),
        in_specs=[pl.BlockSpec(memory_space=pltpu.VMEM)],
        out_specs=pl.BlockSpec(memory_space=pltpu.VMEM),
        scratch_shapes=[pltpu.SemaphoreType.DMA((devices - 1,)), pltpu.SemaphoreType.DMA((devices - 1,))],
        compiler_params=pltpu.CompilerParams(
            collective_id=collective_id, has_side_effects=True, vmem_limit_bytes=4 * 2**20
        ),
    )(tile)
    return out[:, 0, : values.shape[0]]


def dot_plain(left, right):
    return jnp.dot(left, right, preferred_element_type=jnp.float32)


def dot_left(left, right):
    return lax.dot_general(
        left, right, (((0,), (0,)), ((), ())), preferred_element_type=jnp.float32
    )


def dot_right(left, right):
    return lax.dot_general(
        left, right, (((1,), (1,)), ((), ())), preferred_element_type=jnp.float32
    )


KEPT = (
    ("normed", D, jnp.bfloat16), ("packed", 3 * D, jnp.bfloat16), ("mixed", D, jnp.bfloat16),
    ("second", D, jnp.bfloat16), ("upper", FF, jnp.bfloat16), ("inner", FF, jnp.float32),
    ("norm_one", D, jnp.float32), ("norm_two", D, jnp.float32), ("inv_one", 128, jnp.float32),
    ("inv_two", 128, jnp.float32),
)
KEPT_INDEX = {name: k for k, (name, _, _) in enumerate(KEPT)}
BACK = (("back_packed", 3 * D), ("back_attn", D), ("back_inner", FF), ("back_branch", D))
GELU_SCALE = math.sqrt(2.0 / math.pi)


def in_nn(x, w):
    return jnp.dot(x, w, preferred_element_type=jnp.float32)


def in_nt(x, w):
    return lax.dot_general(x, w, (((1,), (1,)), ((), ())), preferred_element_type=jnp.float32)


def in_tn(x, w):
    return lax.dot_general(x, w, (((0,), (0,)), ((), ())), preferred_element_type=jnp.float32)


def softmax_rows(scores):
    raised = jnp.exp(scores - jnp.max(scores, -1, keepdims=True))
    return raised * (1.0 / jnp.sum(raised, -1, keepdims=True))


def low_half():
    return lax.broadcasted_iota(jnp.int32, (SEQ, 2 * HD), 1) < HD


def forward_pieces(weights, entry, select_ref, mask_ref, hidden, kept, top_ref, gains_ref, need, leave):
    bf = jnp.bfloat16
    pieces = []
    gain = lambda row: gains_ref[row : row + 1, :]

    def start():
        need(entry)
        gains_ref[...] = in_nt(select_ref[2 * SEQ :, :], entry[...])
        hidden[...] = in_nt(select_ref[:SEQ, :], entry[...])
    pieces.append(start)

    def norm(layer, which):
        value = hidden[...]
        centred = value - jnp.mean(value, -1, keepdims=True)
        inv = lax.rsqrt(jnp.mean(centred * centred, -1, keepdims=True) + NORM_EPS)
        n = centred * inv
        names = ("norm_one", "inv_one", "normed") if which == 0 else ("norm_two", "inv_two", "second")
        kept[names[0]][layer] = n
        kept[names[1]][layer] = jnp.broadcast_to(inv, (SEQ, 128))
        kept[names[2]][layer] = (n * gain(2 * layer + which)).astype(bf)
        for name in names:
            leave(layer, name)

    def project(layer):
        norm(layer, 0)
        need(weights[4 * layer])
        kept["packed"][layer] = in_nn(kept["normed"][layer], weights[4 * layer][...]).astype(bf)
        leave(layer, "packed")

    def attend(layer, pair):
        packed = kept["packed"]
        cut = lambda k: packed[layer, :, k * D + pair * 2 * HD : k * D + (pair + 1) * 2 * HD]
        q, k, v = cut(0), cut(1), cut(2)
        low = low_half()
        parts = []
        for side in range(2):
            one = jnp.where(low if side == 0 else ~low, q, jnp.zeros((), bf))
            scores = in_nt(one, k) * HD ** (-0.5)
            if layer == 0:
                scores = jnp.where(mask_ref[...] > 0, scores, -1e30)
            parts.append(in_nn(softmax_rows(scores).astype(bf), v))
        kept["mixed"][layer, :, pair * 2 * HD : (pair + 1) * 2 * HD] = jnp.where(low, parts[0], parts[1]).astype(bf)

    def close(layer):
        leave(layer, "mixed")
        need(weights[4 * layer + 1])
        hidden[...] += in_nn(kept["mixed"][layer], weights[4 * layer + 1][...])
        norm(layer, 1)
        need(weights[4 * layer + 2])

    def up(layer, part, parts):
        columns = slice(part * FF // parts, (part + 1) * FF // parts)
        inner = in_nn(kept["second"][layer], weights[4 * layer + 2][:, columns])
        kept["inner"][layer, :, columns] = inner
        kept["upper"][layer, :, columns] = (
            0.5 * inner * (1.0 + jnp.tanh(GELU_SCALE * (inner + 0.044715 * inner * inner * inner)))
        ).astype(bf)

    def down(layer):
        leave(layer, "inner")
        leave(layer, "upper")
        need(weights[4 * layer + 3])
        hidden[...] += in_nt(kept["upper"][layer], weights[4 * layer + 3][...])

    def between():
        keep = mask_ref[...].reshape(1, SEQ)
        hidden[...] = hidden[...] * keep_column(keep) + in_nt(select_ref[SEQ : 2 * SEQ, :], entry[...])

    def keep_column(keep):
        return jnp.transpose(jnp.broadcast_to(keep, (128, SEQ)))[:, :1]

    for layer in range(2):
        pieces.append(functools.partial(project, layer))
        for pair in range(HEADS // 2):
            pieces.append(functools.partial(attend, layer, pair))
        pieces.append(functools.partial(close, layer))
        for part in range(3):
            pieces.append(functools.partial(up, layer, part, 3))
        pieces.append(functools.partial(down, layer))
        if layer == 0:
            pieces.append(between)

    def finish():
        top_ref[...] = hidden[BUF:, :].astype(bf)
    pieces.append(finish)
    return pieces


def forward_kernel(*refs):
    entry_hbm, weight_hbm, (select_ref, mask_ref), refs = refs[0], refs[1:9], refs[9:11], refs[11:]
    kept_hbm, (top_ref, gains_ref), refs = refs[: len(KEPT)], refs[len(KEPT) : len(KEPT) + 2], refs[len(KEPT) + 2 :]
    entry, weights, kept_refs, refs = refs[0], refs[1:9], refs[9 : 9 + len(KEPT)], refs[9 + len(KEPT) :]
    hidden, weight_sem, kept_sem = refs
    kept = {name: ref for (name, _, _), ref in zip(KEPT, kept_refs)}
    local = [(entry_hbm, entry)] + list(zip(weight_hbm, weights))
    fetches = {id(ref): pltpu.make_async_copy(hbm, ref, weight_sem.at[k]) for k, (hbm, ref) in enumerate(local)}
    for copy in fetches.values():
        copy.start()
    leaving = []

    def leave(layer, name):
        k = KEPT_INDEX[name]
        copy = pltpu.make_async_copy(kept_refs[k].at[layer], kept_hbm[k].at[layer], kept_sem.at[layer, k])
        copy.start()
        leaving.append(copy)

    pieces = forward_pieces(
        weights, entry, select_ref, mask_ref, hidden, kept, top_ref, gains_ref, lambda ref: fetches[id(ref)].wait(), leave
    )
    for piece in pieces:
        piece()
    for copy in leaving:
        copy.wait()


def trunk_forward(entry, weights, select, mask):
    bf, f32 = jnp.bfloat16, jnp.float32
    vmem, hbm = pl.BlockSpec(memory_space=pltpu.VMEM), pl.BlockSpec(memory_space=pl.ANY)
    kept_shapes = [(2, SEQ, columns) for _, columns, _ in KEPT]
    outs = pl.pallas_call(
        forward_kernel,
        out_shape=[jax.ShapeDtypeStruct(s, dtype) for s, (_, _, dtype) in zip(kept_shapes, KEPT)]
        + [jax.ShapeDtypeStruct((LAT, D), bf), jax.ShapeDtypeStruct((16, D), f32)],
        in_specs=[hbm] * 9 + [vmem] * 2,
        out_specs=[hbm] * len(KEPT) + [vmem] * 2,
        scratch_shapes=[pltpu.VMEM(w.shape, bf) for w in [entry] + weights]
        + [pltpu.VMEM(s, dtype) for s, (_, _, dtype) in zip(kept_shapes, KEPT)]
        + [pltpu.VMEM((SEQ, D), f32), pltpu.SemaphoreType.DMA((9,)), pltpu.SemaphoreType.DMA((2, len(KEPT)))],
        compiler_params=pltpu.CompilerParams(vmem_limit_bytes=60 * 2**20),
    )(entry, *weights, select, mask)
    count = len(KEPT)
    return outs[count], outs[count + 1], outs[:count]


BACK_KEPT = ("packed", "inner", "norm_one", "norm_two", "inv_one", "inv_two")
BACK_NAMES = tuple(name for name, _ in BACK)


def backward_pieces(layer, inputs, outputs, scratch):
    weight_hbm, (gains_ref, select_ref, mask_ref, upstream_ref, gain_before_ref) = inputs[:4], inputs[4:9]
    kept_hbm = inputs[9 : 9 + len(BACK_KEPT)]
    back_hbm, (hidden, gain_grad, small_hbm) = outputs[: len(BACK)], outputs[len(BACK) :]
    buffers, kept_refs, scratch = scratch[:2], scratch[2 : 2 + len(BACK_KEPT)], scratch[2 + len(BACK_KEPT) :]
    back_refs, (mixed, middle, small_stage, weight_sem, kept_sem, back_sem, small_sem) = (
        scratch[: len(BACK)], scratch[len(BACK) :]
    )
    bf = jnp.bfloat16
    back = dict(zip(BACK_NAMES, back_refs))
    kept = dict(zip(BACK_KEPT, kept_refs))
    views = (
        buffers[0].at[:, pl.ds(D, 3 * D)], buffers[0].at[:, pl.ds(0, D)], buffers[1], buffers[0]
    )
    QKV, OUT, UP, DOWN = range(4)

    def fetch(k):
        return pltpu.make_async_copy(weight_hbm[k], views[k], weight_sem.at[k])

    def fetch_kept(name):
        k = BACK_KEPT.index(name)
        return pltpu.make_async_copy(kept_hbm[k].at[layer], kept_refs[k], kept_sem.at[k])

    def leave(name):
        k = BACK_NAMES.index(name)
        return pltpu.make_async_copy(back_refs[k], back_hbm[k], back_sem.at[k])

    def gain(row):
        return gains_ref[row : row + 1, :]

    def norm_step(upstream, n, inv):
        return inv * (
            upstream - jnp.mean(upstream, -1, keepdims=True) - n * jnp.mean(upstream * n, -1, keepdims=True)
        )

    def begin():
        fetch(DOWN).start()
        fetch_kept("inner").start()
        fetch(UP).start()
        for name in ("norm_two", "inv_two", "packed", "norm_one", "inv_one"):
            fetch_kept(name).start()
        upstream = upstream_ref[...]
        if layer == 0:
            upstream = upstream * jnp.transpose(jnp.broadcast_to(mask_ref[...], (128, SEQ)))[:, :1]
        hidden[...] = upstream
        gain_grad[...] = gain_before_ref[...]

    def branch():
        back["back_branch"][...] = hidden[...].astype(bf)
        leave("back_branch").start()
        fetch(DOWN).wait()
        fetch_kept("inner").wait()

    def widen(part, parts):
        columns = slice(part * FF // parts, (part + 1) * FF // parts)
        up = in_nn(back["back_branch"][...], views[DOWN][:, columns])
        x = kept["inner"][:, columns]
        t = jnp.tanh(GELU_SCALE * (x + 0.044715 * x * x * x))
        slope = 0.5 * (1.0 + t) + 0.5 * x * (1.0 - t * t) * (GELU_SCALE * (1.0 + 3.0 * 0.044715 * x * x))
        back["back_inner"][:, columns] = (slope * up).astype(bf)

    def narrow():
        fetch(OUT).start()
        fetch(QKV).start()
        leave("back_inner").start()
        fetch(UP).wait()
        fetch_kept("norm_two").wait()
        fetch_kept("inv_two").wait()
        middle[...] = in_nt(back["back_inner"][...], views[UP][...])

    def renorm():
        value = middle[...]
        n = kept["norm_two"][...]
        gain_grad[2 * layer + 1 : 2 * layer + 2, :] = jnp.sum(value * n, 0, keepdims=True)
        middle[...] = hidden[...] + norm_step(value * gain(2 * layer + 1), n, kept["inv_two"][:, :1])
        back["back_attn"][...] = middle[...].astype(bf)
        leave("back_attn").start()

    def unmix():
        fetch(OUT).wait()
        fetch_kept("packed").wait()
        mixed[...] = in_nt(back["back_attn"][...], views[OUT][...]).astype(bf)

    def attend(pair):
        low = low_half()
        at = lambda k: slice(k * D + pair * 2 * HD, k * D + (pair + 1) * 2 * HD)
        q, k, v = (kept["packed"][:, at(i)] for i in range(3))
        up = mixed[:, at(0)]
        zero = jnp.zeros((), bf)
        parts = []
        for side in range(2):
            mine = low if side == 0 else ~low
            scores = in_nt(jnp.where(mine, q, zero), k) * HD ** (-0.5)
            if layer == 0:
                scores = jnp.where(mask_ref[...] > 0, scores, -1e30)
            attention = softmax_rows(scores)
            back_attention = in_nt(jnp.where(mine, up, zero), v)
            back_values = in_tn(attention.astype(bf), up)
            back_scores = (
                attention * (back_attention - jnp.sum(back_attention * attention, -1, keepdims=True))
            ).astype(bf)
            parts.append((in_nn(back_scores, k) * HD ** (-0.5), in_tn(back_scores, q) * HD ** (-0.5), back_values))
        for i in range(3):
            back["back_packed"][:, at(i)] = jnp.where(low, parts[0][i], parts[1][i]).astype(bf)

    def close():
        leave("back_packed").start()
        fetch(QKV).wait()
        fetch_kept("norm_one").wait()
        fetch_kept("inv_one").wait()
        value = in_nt(back["back_packed"][...], views[QKV][...])
        n = kept["norm_one"][...]
        gain_grad[2 * layer : 2 * layer + 1, :] = jnp.sum(value * n, 0, keepdims=True)
        hidden[...] = middle[...] + norm_step(value * gain(2 * layer), n, kept["inv_one"][:, :1])
        for name in BACK_NAMES:
            leave(name).wait()

    def small():
        small_stage[...] = (
            in_tn(hidden[...].astype(bf), select_ref[:SEQ, :])
            + in_tn(upstream_ref[...].astype(bf), select_ref[SEQ : 2 * SEQ, :])
            + in_tn(gain_grad[...].astype(bf), select_ref[2 * SEQ :, :])
        ).astype(bf)
        copy = pltpu.make_async_copy(small_stage, small_hbm.at[0], small_sem)
        copy.start()
        copy.wait()

    return (
        [begin, branch]
        + [functools.partial(widen, part, 3) for part in range(3)]
        + [narrow, renorm, unmix]
        + [functools.partial(attend, pair) for pair in range(HEADS // 2)]
        + [close]
        + ([small] if layer == 0 else [])
    )


def backward_kernel(layer, reduction, *refs):
    input_count, output_count = 9 + len(BACK_KEPT), len(BACK) + 3
    inputs, refs = refs[:input_count], refs[input_count:]
    if reduction is None:
        for piece in backward_pieces(layer, inputs, refs[:output_count], refs[output_count:]):
            piece()
        return
    nz, row_count, width, jobs, has_extras = reduction
    side_refs = []
    for side in range(2):
        chosen = []
        for job in jobs:
            if job[side] is None:
                chosen.append((None, job[2 + side]))
            else:
                chosen.append((refs[0], job[side][0]))
                refs = refs[1:]
        side_refs.append(chosen)
    extra_ref = None
    if has_extras:
        extra_ref, refs = refs[0], refs[1:]
    outputs, summed, refs = refs[:output_count], refs[output_count], refs[output_count + 1 :]
    scratch_count = 2 + len(BACK_KEPT) + len(BACK) + 7

    def resolve(ref, index):
        if ref is None:
            return outputs[BACK_NAMES.index(index)]
        return ref if index is None else ref.at[index]

    x_refs, y_refs = ([resolve(*pair) for pair in chosen] for chosen in side_refs)
    pieces = backward_pieces(layer, inputs, outputs, refs[:scratch_count])
    each, stride = (1, 2) if layer == 1 else (2, 1)

    def between(i):
        for turn in range(-(-len(pieces) // each)):
            @pl.when(i == turn * stride)
            def _():
                for piece in pieces[turn * each : (turn + 1) * each]:
                    piece()

    reduce_program(
        nz, row_count, width, [job[4] for job in jobs], x_refs, y_refs, outputs[-1] if extra_ref is None else extra_ref,
        summed, refs[scratch_count:], between,
    )


def layer_backward(
    layer, gains, weights, select, mask, upstream, gain_before, kept, pairs=None, extras=None, sizes=None, collective_id=None
):
    bf, f32 = jnp.bfloat16, jnp.float32
    vmem, hbm = pl.BlockSpec(memory_space=pltpu.VMEM), pl.BlockSpec(memory_space=pl.ANY)
    kept_in = [kept[KEPT_INDEX[name]] for name in BACK_KEPT]
    static, operands, more, summed, scratch = None, [], {}, [], []
    if pairs is not None:
        row_count, width, low_shape, nz = sizes
        widths, jobs, sides = dict(BACK), [], ([], [])
        for pair in pairs:
            marks, columns = [], 0
            for side, entry in enumerate(pair):
                if isinstance(entry, str):
                    marks.append((None, entry))
                    columns = widths[entry]
                else:
                    array, index = entry if isinstance(entry, tuple) else (entry, None)
                    sides[side].append(array)
                    marks.append(((index,), None))
                    columns, tokens = array.shape[-1], array.shape[-2]
            jobs.append((marks[0][0], marks[1][0], marks[0][1], marks[1][1], columns))
        total = sum(job[4] // width for job in jobs) + (1 if extras is None else extras.shape[0])
        operands = sides[0] + sides[1] + ([] if extras is None else [extras])
        static = (nz, row_count, width, jobs, extras is not None)
        summed = [jax.ShapeDtypeStruct((total, row_count // 8 // nz, width), f32)]
        scratch = reduce_scratch(tokens, row_count, width, total, low_shape, nz)
        more = {"collective_id": collective_id, "has_side_effects": True}
    dma = pltpu.SemaphoreType.DMA
    outs = pl.pallas_call(
        functools.partial(backward_kernel, layer, static),
        out_shape=[jax.ShapeDtypeStruct((SEQ, columns), bf) for _, columns in BACK]
        + [
            jax.ShapeDtypeStruct((SEQ, D), f32), jax.ShapeDtypeStruct((16, D), f32),
            jax.ShapeDtypeStruct((1, D, TRUNK_WIDTH), bf),
        ]
        + summed,
        in_specs=[hbm] * 4 + [vmem] * 5 + [hbm] * (len(BACK_KEPT) + len(operands)),
        out_specs=[hbm] * len(BACK) + [vmem] * 2 + [hbm] + [vmem] * len(summed),
        scratch_shapes=[pltpu.VMEM((D, FF), bf)] * 2
        + [pltpu.VMEM(a.shape[1:], a.dtype) for a in kept_in]
        + [pltpu.VMEM((SEQ, columns), bf) for _, columns in BACK]
        + [
            pltpu.VMEM((SEQ, D), bf), pltpu.VMEM((SEQ, D), f32),
            pltpu.VMEM((D, TRUNK_WIDTH) if layer == 0 else (16, 128), bf),
            dma((4,)), dma((len(BACK_KEPT),)), dma((len(BACK),)), dma,
        ]
        + scratch,
        compiler_params=pltpu.CompilerParams(vmem_limit_bytes=60 * 2**20, **more),
    )(*weights, gains, select, mask, upstream, gain_before, *kept_in, *operands)
    return dict(zip(BACK_NAMES, outs)), *outs[len(BACK) :]


def layer_pairs(layer, kept, back):
    left = lambda name: (kept[KEPT_INDEX[name]], layer)
    return [
        (left("normed"), back["back_packed"]), (left("mixed"), back["back_attn"]),
        (left("second"), back["back_inner"]), (back["back_branch"], left("upper")),
    ]


ROWS_AT_ONCE = 192
HEAD_WEIGHTS = ((HW, 3 * HW), (HW, HW), (HW, HW)) * HB + (
    (HW, D), (HW, HW), (HW, HW), (HW, HW), (HW, FREQ), (HW, 128), (HW, 128)
)
HEAD_LEFT = (3, 1, 1, 1, 1) * HB + (1, 1, 1, 1, 1, 1, 1, 1)


def sigmoid(x):
    return 0.5 + 0.5 * jnp.tanh(0.5 * x)


def head_kernel(tokens, *refs):
    (embed_ref, noisy_ref, target_ref, grad_col_ref, loss_col_ref, bias_ref, cond_ref), refs = refs[:7], refs[7:]
    count = len(HEAD_WEIGHTS)
    block_hbm, edge_hbm, refs = refs[:HB], refs[HB : HB + 7], refs[HB + 7 :]
    weight_hbm = [
        block.at[:, pl.ds(column, width)]
        for block in block_hbm
        for column, width in ((0, 3 * HW), (3 * HW, HW), (4 * HW, HW))
    ] + list(edge_hbm)
    left_hbm, refs = refs[: len(HEAD_LEFT)], refs[len(HEAD_LEFT) :]
    (pred_ref, back_cond_ref, back_token_ref, bias_grad_ref, loss_ref), refs = refs[:5], refs[5:]
    weights, refs = refs[:count], refs[count:]
    left, refs = refs[: len(HEAD_LEFT)], refs[len(HEAD_LEFT) :]
    (
        time_inner, conditioning, projected, cond_sum, stream, back_silu, t0, t1, t2,
        scale1, normed, inner, gate, branch, inverse, weight_sem, left_sem,
    ) = refs
    cond_t, time_two_t, shift_t, scale_t, time_one_t, in_t, out_t = weights[3 * HB :]
    per_block = 5
    silu_cond, time_hidden, back_time, back_time_inner, back_shift, back_scale, final_low, back_low = left[
        per_block * HB :
    ]
    bf = jnp.bfloat16

    def fetch(k):
        return pltpu.make_async_copy(weight_hbm[k], weights[k], weight_sem.at[k])

    order = [3 * HB, 3 * HB + 4, 3 * HB + 1, 3 * HB + 5]
    for b in range(HB):
        order += [3 * b, 3 * b + 1, 3 * b + 2]
    order += [3 * HB + 2, 3 * HB + 3, 3 * HB + 6]
    for k in order:
        fetch(k).start()

    def nn(x, w):
        return jnp.dot(x, w, preferred_element_type=jnp.float32)

    def nt(x, w):
        return lax.dot_general(x, w, (((1,), (1,)), ((), ())), preferred_element_type=jnp.float32)

    def by_rows(body):
        for i in range(0, tokens, ROWS_AT_ONCE):
            body(slice(i, i + ROWS_AT_ONCE))

    bias_grad_ref[...] = jnp.zeros_like(bias_grad_ref)
    loss_ref[...] = jnp.zeros_like(loss_ref)
    cond_sum[...] = jnp.zeros_like(cond_sum)

    def bias(row):
        return bias_ref[row : row + 1, :]

    def add_bias_grad(row, value):
        bias_grad_ref[row : row + 1, :] += jnp.sum(value.astype(jnp.float32), 0, keepdims=True)

    @pl.loop(0, COPIES)
    def _(c):
        def need(*numbers):
            @pl.when(c == 0)
            def _():
                for k in numbers:
                    fetch(k).wait()

        def leave(k):
            return pltpu.make_async_copy(left[k], left_hbm[k].at[c], left_sem.at[k])

        def room(*numbers):
            @pl.when(c > 0)
            def _():
                for k in numbers:
                    leave(k).wait()

        base = per_block * HB
        room(base, base + 1)
        need(3 * HB)

        @pl.when(c == 0)
        def _():
            projected[...] = nt(cond_ref[...], cond_t[...])

        need(3 * HB + 4, 3 * HB + 1, 3 * HB + 5)
        time_inner[...] = nt(embed_ref[c], time_one_t[...])

        def _(r):
            value = time_inner[r, :] + bias(10)
            time_inner[r, :] = value
            time_hidden[r, :] = (value * sigmoid(value)).astype(bf)
        by_rows(_)
        leave(base + 1).start()
        t0[...] = nt(time_hidden[...], time_two_t[...])
        stream[...] = nt(noisy_ref[c], in_t[...])

        def _(r):
            value = projected[r, :] + (t0[r, :] + bias(11))
            conditioning[r, :] = value
            silu_cond[r, :] = (value * sigmoid(value)).astype(bf)
            stream[r, :] = stream[r, :] + bias(14)
        by_rows(_)
        leave(base).start()

        for b in range(HB):
            w_mod, w_up, w_down = weights[3 * b : 3 * b + 3]
            bm, shaped, back_inner, back_branch, hidden = left[per_block * b : per_block * (b + 1)]
            room(*range(per_block * b, per_block * (b + 1)))
            need(3 * b)
            t0[...] = nn(silu_cond[...], w_mod[:, :HW])
            t1[...] = nn(silu_cond[...], w_mod[:, HW : 2 * HW])
            gate[b] = nn(silu_cond[...], w_mod[:, 2 * HW :])

            def _(r):
                value = stream[r, :]
                centred = value - jnp.mean(value, -1, keepdims=True)
                inv = lax.rsqrt(jnp.mean(centred * centred, -1, keepdims=True) + NORM_EPS)
                n = centred * inv
                s = 1.0 + (t1[r, :] + bias(5 * b + 1))
                inverse[b, r, :] = jnp.broadcast_to(inv, (ROWS_AT_ONCE, 128))
                normed[b, r, :] = n
                scale1[b, r, :] = s
                shaped[r, :] = (n * s + (t0[r, :] + bias(5 * b))).astype(bf)
            by_rows(_)
            leave(per_block * b + 1).start()
            need(3 * b + 1)
            inner[b] = nn(shaped[...], w_up[...])

            def _(r):
                value = inner[b, r, :] + bias(5 * b + 3)
                inner[b, r, :] = value
                hidden[r, :] = (value * sigmoid(value)).astype(bf)
            by_rows(_)
            leave(per_block * b + 4).start()
            need(3 * b + 2)
            branch[b] = nt(hidden[...], w_down[...])

            def _(r):
                value = branch[b, r, :] + bias(5 * b + 4)
                g = gate[b, r, :] + bias(5 * b + 2)
                branch[b, r, :] = value
                gate[b, r, :] = g
                stream[r, :] = stream[r, :] + g * value
            by_rows(_)

        need(3 * HB + 2, 3 * HB + 3, 3 * HB + 6)
        room(*range(base + 2, base + 8))
        t0[...] = nt(silu_cond[...], shift_t[...])
        t1[...] = nt(silu_cond[...], scale_t[...])
        def _(r):
            value = stream[r, :]
            centred = value - jnp.mean(value, -1, keepdims=True)
            inv = lax.rsqrt(jnp.mean(centred * centred, -1, keepdims=True) + NORM_EPS)
            n = centred * inv
            s = 1.0 + (t1[r, :] + bias(13))
            inverse[HB, r, :] = jnp.broadcast_to(inv, (ROWS_AT_ONCE, 128))
            t2[r, :] = n
            t1[r, :] = s
            final_low[r, :] = (n * s + (t0[r, :] + bias(12))).astype(bf)
        by_rows(_)
        leave(base + 6).start()
        difference = nn(final_low[...], out_t[...]) - target_ref[c]
        loss_ref[...] += loss_col_ref[c] * difference * difference
        pred_ref[c] = (grad_col_ref[c] * difference).astype(bf)
        t0[...] = nt(pred_ref[c], out_t[...])

        def _(r):
            back = t0[r, :]
            n = t2[r, :]
            low_shift, low_scale = back.astype(bf), (back * n).astype(bf)
            back_shift[r, :] = low_shift
            back_scale[r, :] = low_scale
            up = back * t1[r, :]
            add_bias_grad(12, low_shift)
            add_bias_grad(13, low_scale)
            stream[r, :] = inverse[HB, r, :1] * (
                up - jnp.mean(up, -1, keepdims=True) - n * jnp.mean(up * n, -1, keepdims=True)
            )
        by_rows(_)
        leave(base + 4).start()
        leave(base + 5).start()
        back_silu[...] = nn(back_shift[...], shift_t[...]) + nn(back_scale[...], scale_t[...])

        for b in reversed(range(HB)):
            w_mod, w_up, w_down = weights[3 * b : 3 * b + 3]
            bm, shaped, back_inner, back_branch, hidden = left[per_block * b : per_block * (b + 1)]

            def _(r):
                back = stream[r, :]
                low = (back * gate[b, r, :]).astype(bf)
                low_gate = (back * branch[b, r, :]).astype(bf)
                back_branch[r, :] = low
                bm[r, 2 * HW :] = low_gate
                add_bias_grad(5 * b + 4, low)
                add_bias_grad(5 * b + 2, low_gate)
            by_rows(_)
            leave(per_block * b + 3).start()
            t0[...] = nn(back_branch[...], w_down[...])

            def _(r):
                value = inner[b, r, :]
                s = sigmoid(value)
                low = (t0[r, :] * (s * (1.0 + value * (1.0 - s)))).astype(bf)
                back_inner[r, :] = low
                add_bias_grad(5 * b + 3, low)
            by_rows(_)
            leave(per_block * b + 2).start()
            t0[...] = nt(back_inner[...], w_up[...])

            def _(r):
                back = t0[r, :]
                n = normed[b, r, :]
                low_shift, low_scale = back.astype(bf), (back * n).astype(bf)
                bm[r, :HW] = low_shift
                bm[r, HW : 2 * HW] = low_scale
                add_bias_grad(5 * b, low_shift)
                add_bias_grad(5 * b + 1, low_scale)
                up = back * scale1[b, r, :]
                stream[r, :] = stream[r, :] + inverse[b, r, :1] * (
                    up - jnp.mean(up, -1, keepdims=True) - n * jnp.mean(up * n, -1, keepdims=True)
                )
            by_rows(_)
            leave(per_block * b).start()
            back_silu[...] += nt(bm[...], w_mod[...])

        def _(r):
            value = conditioning[r, :]
            s = sigmoid(value)
            back = back_silu[r, :] * (s * (1.0 + value * (1.0 - s)))
            low, low_stream = back.astype(bf), stream[r, :].astype(bf)
            cond_sum[r, :] = cond_sum[r, :] + back
            back_time[r, :] = low
            back_low[r, :] = low_stream
            add_bias_grad(11, low)
            add_bias_grad(14, low_stream)
        by_rows(_)
        leave(base + 2).start()
        leave(base + 7).start()
        t0[...] = nn(back_time[...], time_two_t[...])

        def _(r):
            value = time_inner[r, :]
            s = sigmoid(value)
            low = (t0[r, :] * (s * (1.0 + value * (1.0 - s)))).astype(bf)
            back_time_inner[r, :] = low
            add_bias_grad(10, low)
        by_rows(_)
        leave(base + 3).start()

    back_cond_ref[...] = cond_sum[...].astype(bf)
    back_token_ref[...] = nn(back_cond_ref[...], cond_t[...]).astype(bf)
    for k in range(len(HEAD_LEFT)):
        pltpu.make_async_copy(left[k], left_hbm[k].at[COPIES - 1], left_sem.at[k]).wait()


def head_pass(
    blocks, edges, biases, cond_rows, clean_rows, noise_rows, step_rows, weight_rows, weight_total
):
    bf = jnp.bfloat16
    tokens = cond_rows.shape[0]
    half_freq = FREQ // 2
    frequencies = jnp.exp(-math.log(10000.0) * jnp.arange(half_freq, dtype=jnp.float32) / half_freq)
    step_times = step_rows.astype(jnp.float32).T
    angles = step_times[..., None] * frequencies
    time_embed = jnp.concatenate([jnp.cos(angles), jnp.sin(angles)], -1).astype(bf)
    phase_angle = (step_times / TSTEPS + 0.008) / 1.008 * (math.pi / 2)
    keep_part = jnp.cos(phase_angle)[..., None]
    noise_part = jnp.sin(phase_angle)[..., None]
    clean_copies = clean_rows.astype(jnp.float32)[None]
    fresh_noise = noise_rows.astype(jnp.float32).reshape(tokens, COPIES, CH).transpose(1, 0, 2)
    wide = ((0, 0), (0, 0), (0, 128 - CH))
    noisy = jnp.pad((keep_part * clean_copies + noise_part * fresh_noise).astype(bf), wide)
    target = jnp.pad(keep_part * fresh_noise - noise_part * clean_copies, wide)
    by_copy = jnp.broadcast_to(weight_rows.T[..., None], (COPIES, tokens, 128))
    f32 = jnp.float32
    vmem, hbm = pl.BlockSpec(memory_space=pltpu.VMEM), pl.BlockSpec(memory_space=pl.ANY)
    lefts = [(COPIES, tokens, k * HW) for k in HEAD_LEFT]
    units = lambda *lead: pltpu.VMEM((*lead, tokens, HW), f32)
    outs = pl.pallas_call(
        functools.partial(head_kernel, tokens),
        out_shape=[jax.ShapeDtypeStruct(shape, bf) for shape in lefts]
        + [
            jax.ShapeDtypeStruct((COPIES, tokens, 128), bf),
            jax.ShapeDtypeStruct((tokens, HW), bf),
            jax.ShapeDtypeStruct((tokens, D), bf),
            jax.ShapeDtypeStruct((5 * (HB + 1) + 1, HW), f32),
            jax.ShapeDtypeStruct((tokens, 128), f32),
        ],
        in_specs=[vmem] * 7 + [hbm] * (HB + 7),
        out_specs=[hbm] * len(HEAD_LEFT) + [vmem] * 5,
        scratch_shapes=[pltpu.VMEM(shape, bf) for shape in HEAD_WEIGHTS]
        + [pltpu.VMEM((tokens, k * HW), bf) for k in HEAD_LEFT]
        + [units()] * 9
        + [units(HB)] * 5
        + [
            pltpu.VMEM((HB + 1, tokens, 128), f32),
            pltpu.SemaphoreType.DMA((len(HEAD_WEIGHTS),)), pltpu.SemaphoreType.DMA((len(HEAD_LEFT),)),
        ],
        compiler_params=pltpu.CompilerParams(vmem_limit_bytes=60 * 2**20),
    )(
        time_embed, noisy, target, by_copy * (2.0 / (CH * weight_total)), by_copy * (1.0 / CH),
        jnp.pad(biases.reshape(5 * (HB + 1), HW), ((0, 1), (0, 0))), cond_rows,
        *blocks, *edges,
    )
    left = [a.reshape(COPIES * tokens, -1) for a in outs[: len(HEAD_LEFT)]]
    back_pred, back_cond, back_tokens, bias_grad, loss_part = outs[len(HEAD_LEFT) :]
    silu_cond, time_hidden, back_time, back_time_inner, back_shift, back_scale, final_low, back_low = left[5 * HB :]
    pairs = []
    for b in range(HB):
        bm, shaped, back_inner, back_branch, hidden = left[5 * b : 5 * (b + 1)]
        pairs += [(silu_cond, bm), (shaped, back_inner), (back_branch, hidden)]
    pairs += [(back_time, time_hidden), (back_shift, silu_cond), (back_scale, silu_cond)]
    flat = lambda a: a.reshape(COPIES * tokens, -1)
    small = (
        dot_left(back_cond, cond_rows),
        dot_left(back_time_inner, flat(time_embed)),
        dot_left(back_low, flat(noisy))[:, :CH],
        dot_left(final_low, flat(back_pred))[:, :CH],
    )
    bias_grad = bias_grad[: 5 * (HB + 1)].reshape(HB + 1, 5 * HW)
    return (jnp.sum(loss_part), pairs, small, bias_grad, back_tokens)


def adamw(master, first, second, gradient, factor, step_rate):
    clipped = gradient * factor
    first_new = BETA_ONE * first + (1.0 - BETA_ONE) * clipped
    second_new = BETA_TWO * second + (1.0 - BETA_TWO) * clipped * clipped
    mean_hat = first_new / (1.0 - BETA_ONE**ADAM_STEP)
    var_hat = second_new / (1.0 - BETA_TWO**ADAM_STEP)
    updated = master - step_rate * (mean_hat / (jnp.sqrt(var_hat) + ADAM_EPS) + DECAY_RATE * master)
    return (updated, first_new, second_new)


TRUNK_PARTS = (3 * D, D, FF, FF)
HEAD_PARTS = (3 * HW, HW, HW)
EDGE_PARTS = (D, HW, HW, HW, FREQ, 128)
TRUNK_WIDTH = 768
HEAD_WIDTH = 512


def gather_plan(part_sets, limit):
    chunks, shapes = [], []
    for source, index, rows, parts in part_sets:
        column = 0
        for part in parts:
            for k in range(0, part, limit):
                chunks.append((source, index, column + k, len(shapes), k, min(limit, part - k)))
            shapes.append((rows, part))
            column += part
    return chunks, shapes


def plain_gather(sources, chunks, shapes):
    ends = {}
    for source, index, column, result, at, width in chunks:
        start, stop = ends.get(result, (source, index, column, column))[2:]
        ends[result] = (source, index, min(start, column), max(stop, column + width))
    wholes = {}
    results = []
    for number in range(len(shapes)):
        source, index, start, stop = ends[number]
        if (source, index) not in wholes:
            block = sources[source] if index is None else sources[source][index]
            wholes[source, index] = lax.all_gather(block, AXES, axis=0, tiled=True)
        results.append(wholes[source, index][:, start:stop])
    return results


def scatter_sum(values):
    low = lax.psum_scatter(values, "dp", scatter_dimension=0, tiled=True)
    return lax.psum_scatter(low, "fsdp", scatter_dimension=0, tiled=True)


def on_device(
    mesh_shape,
    latents, orders, mask_counts, noise, timesteps, loss_weights,
    block_weights, block_gains, entry_table, head_weights, head_biases, head_edges,
    first_blocks, first_gains, first_entry, first_head, first_biases, first_edges,
    second_blocks, second_gains, second_entry, second_head, second_biases, second_edges,
):
    dp_count, nz = mesh_shape["dp"], mesh_shape["fsdp"]
    devices = dp_count * nz
    me = lax.axis_index("dp") * nz + lax.axis_index("fsdp")
    r0, r1 = D // devices, HW // devices
    direct = dp_count == 8 and nz > 1 and (D // 8) % 16 == 0
    bf = jnp.bfloat16

    low_blocks = block_weights.astype(bf)
    local_total = jnp.sum(mask_counts)
    terms, rest = [local_total.astype(bf)], jnp.sum(loss_weights)
    for _ in range(3):
        terms.append(lax.reduce_precision(rest, 8, 7).astype(bf))
        rest = rest - terms[-1].astype(jnp.float32)
    low_entry = jnp.concatenate(
        [
            entry_table.T.astype(bf), block_gains.reshape(4, r0).T.astype(bf),
            jnp.broadcast_to(jnp.stack(terms), (r0, 4)), jnp.zeros((r0, 104), bf),
        ],
        1,
    )
    low_head = head_weights.astype(bf)
    edge = head_edges.T.astype(bf)
    base = D + 2 * CH
    low_edges = jnp.concatenate(
        [
            edge[:, :D], edge[:, base + FREQ :], edge[:, base : base + FREQ], edge[:, D:base],
            head_biases.reshape((HB + 1) * 5, r1).T.astype(bf), jnp.zeros((r1, 81), bf),
        ],
        1,
    )
    chunks, shapes = gather_plan(
        [(1, None, r0, (TRUNK_WIDTH,)), (0, 0, r0, TRUNK_PARTS), (0, 1, r0, TRUNK_PARTS), (2, None, r1, EDGE_PARTS)],
        TRUNK_WIDTH,
    )
    sources = [low_blocks, low_entry, low_edges]
    if direct:
        gathered = [a.reshape(devices * a.shape[4], -1) for a in gather_rows(sources, chunks, shapes, nz, 1)]
    else:
        gathered = plain_gather(sources, chunks, shapes)
    trunk, edge_mats = gathered[:9], gathered[9:]
    head_blocks = [lax.all_gather(low_head[b], AXES, axis=0, tiled=True) for b in range(HB)]

    early = trunk[0][::r0, 2 * SEQ + CH + 4 : 2 * SEQ + CH + 8].astype(jnp.float32)
    counts = early[:, 0].astype(jnp.int32)
    weight_total = jnp.sum(early[:, 1:])
    count_ends = jnp.cumsum(counts)
    count_starts = count_ends - counts
    offset = jnp.sum(jnp.where(jnp.arange(devices) == me, count_starts, 0))

    order_row = orders[0]
    clean = latents[0]
    ids = jnp.arange(LAT, dtype=jnp.int32)
    masked = jnp.any((order_row[:, None] == ids[None, :]) & (ids < local_total)[:, None], 0)
    key_keep = jnp.concatenate([jnp.ones((BUF,), jnp.float32), 1.0 - masked.astype(jnp.float32)])
    positions = jnp.arange(SEQ, dtype=jnp.int32)
    columns = jnp.arange(TRUNK_WIDTH, dtype=jnp.int32)
    pick_rows = jnp.concatenate([positions, SEQ + positions, 2 * SEQ + CH + jnp.arange(16, dtype=jnp.int32)])
    select = (pick_rows[:, None] == columns[None, :]).astype(bf) + jnp.pad(
        clean, ((BUF, SEQ + 16), (2 * SEQ, TRUNK_WIDTH - 2 * SEQ - CH))
    )
    top_rows, gains, kept = trunk_forward(trunk[0], trunk[1:9], select, key_keep[None])

    capacity = (LAT + devices - 1) // devices
    slots = devices * capacity
    slot_ids = jnp.arange(slots, dtype=jnp.int32)
    slot_token = jnp.mod(slot_ids // capacity - offset, devices) + devices * (slot_ids % capacity)
    slot_position = jnp.sum(
        jnp.where(slot_token[:, None] == ids[None, :], order_row[None, :], 0), 1
    )
    pick = (
        (slot_position[:, None] == ids[None, :]) & (slot_token < local_total)[:, None]
    ).astype(bf)
    outgoing = dot_plain(
        pick, jnp.concatenate([top_rows, clean, jnp.zeros((LAT, 112), bf)], 1)
    ).astype(bf)
    incoming = lax.all_to_all(
        outgoing.reshape(devices, capacity, -1), AXES, split_axis=0, concat_axis=0, tiled=True
    ).reshape(slots, -1)
    head_rows = noise.shape[0]
    token_ids = jnp.arange(head_rows, dtype=jnp.int32) * devices + me
    inside = (token_ids[:, None] >= count_starts[None, :]) & (token_ids[:, None] < count_ends[None, :])
    first_token = count_starts + jnp.mod(me - count_starts, devices)
    source_slot = (
        jnp.arange(devices, dtype=jnp.int32)[None, :] * capacity
        + (token_ids[:, None] - first_token[None, :]) // devices
    )
    row_slot = jnp.sum(jnp.where(inside, source_slot, 0), 1)
    place = (row_slot[:, None] == slot_ids[None, :]).astype(bf)
    received = dot_plain(place, incoming).astype(bf)

    misc = edge_mats[5]
    biases = (
        misc[:, 2 * CH : 2 * CH + 5 * (HB + 1)]
        .reshape(devices, r1, HB + 1, 5)
        .transpose(2, 0, 3, 1)
        .reshape(HB + 1, 5 * HW)
        .astype(jnp.float32)
    )
    loss_local, head_pairs, small, bias_grad, back_tokens = head_pass(
        head_blocks,
        edge_mats[:5]
        + [
            jnp.pad(misc[:, :CH], ((0, 0), (0, 128 - CH))),
            jnp.pad(misc[:, CH : 2 * CH], ((0, 0), (0, 128 - CH))),
        ],
        biases,
        received[:, :D],
        received[:, D : D + CH],
        noise,
        timesteps,
        loss_weights,
        weight_total,
    )
    grad_cond_t, grad_time_one_t, grad_in_t, grad_out_t = small
    bias_t = (
        bias_grad.reshape(HB + 1, devices, 5, r1).transpose(1, 3, 0, 2).reshape(HW, 5 * (HB + 1))
    )
    head_small = jnp.concatenate(
        [grad_cond_t, grad_time_one_t, grad_in_t, grad_out_t, bias_t, jnp.zeros((HW, 465), jnp.float32)], 1
    ).astype(bf)
    returning = dot_left(place, back_tokens.astype(bf)).astype(bf)
    returned = lax.all_to_all(
        returning.reshape(devices, capacity, D), AXES, split_axis=0, concat_axis=0, tiled=True
    ).reshape(slots, D)
    back_top = jnp.concatenate([jnp.zeros((BUF, D), jnp.float32), dot_left(pick, returned)], 0)
    mask = key_keep[None]
    no_gain = jnp.zeros((16, D), jnp.float32)
    if direct:
        extras = jnp.stack(
            [head_small[:, k : k + HEAD_WIDTH] for k in range(0, head_small.shape[1], HEAD_WIDTH)]
        )
        decoder_back, back_decoder, gain_grad, _, tall = layer_backward(
            1, gains, trunk[5:9], select, mask, back_top, no_gain, kept,
            head_pairs, extras, (HW, HEAD_WIDTH, (r1, HEAD_WIDTH), nz), 4,
        )
        tall = tall.transpose(1, 0, 2).reshape(r1, -1)
        own = {name: name for name in BACK_NAMES}
        trunk_pairs = layer_pairs(1, kept, decoder_back) + layer_pairs(0, kept, own)
        *_, wide = layer_backward(
            0, gains, trunk[1:5], select, mask, back_decoder, gain_grad, kept,
            trunk_pairs, None, (D, TRUNK_WIDTH, (2 * r0, TRUNK_WIDTH // 2), nz), 5,
        )
        wide = wide.transpose(1, 0, 2).reshape(r0, -1)
    else:
        tall = jnp.concatenate(
            [scatter_sum(dot_left(x, y)) for x, y in head_pairs]
            + [scatter_sum(head_small.astype(jnp.float32))],
            1,
        )
        decoder_back, back_decoder, gain_grad, _ = layer_backward(
            1, gains, trunk[5:9], select, mask, back_top, no_gain, kept
        )
        encoder_back, _, _, trunk_small = layer_backward(
            0, gains, trunk[1:5], select, mask, back_decoder, gain_grad, kept
        )
        whole = lambda entry: entry[0][entry[1]] if isinstance(entry, tuple) else entry
        wide = jnp.concatenate(
            [
                scatter_sum(dot_left(whole(x), whole(y)))
                for x, y in layer_pairs(1, kept, decoder_back) + layer_pairs(0, kept, encoder_back)
            ]
            + [scatter_sum(trunk_small[0].astype(jnp.float32))],
            1,
        )
    block_columns, head_columns = sum(TRUNK_PARTS), sum(HEAD_PARTS)
    block_grad = jnp.stack([wide[:, l * block_columns : (l + 1) * block_columns] for l in (1, 0)])
    rest = wide[:, 2 * block_columns :]
    entry_grad = rest[:, : 2 * SEQ + CH].T
    gain_grad = rest[:, 2 * SEQ + CH : 2 * SEQ + CH + 4].T.reshape(2, 2, r0)
    head_grad = jnp.stack([tall[:, b * head_columns : (b + 1) * head_columns] for b in range(HB)])
    rest = tall[:, HB * head_columns :]
    shared = rest[:, 3 * HW :]
    edge_grad = jnp.concatenate(
        [
            shared[:, :D], shared[:, D + FREQ : D + FREQ + 2 * CH], shared[:, D : D + FREQ],
            rest[:, : 3 * HW],
        ],
        1,
    ).T
    bias_grad = (
        shared[:, D + FREQ + 2 * CH : D + FREQ + 2 * CH + 5 * (HB + 1)].T.reshape(HB + 1, 5 * r1)
    )
    squares = jnp.sum(wide * wide) + jnp.sum(tall * tall)
    late = exchange(jnp.stack([loss_local, squares]), dp_count, nz, 6)
    loss_sum = jnp.sum(late[:, 0])
    grad_norm = jnp.sqrt(jnp.sum(late[:, 1]))
    factor = CLIP_NORM / jnp.maximum(grad_norm, CLIP_NORM)
    new = [
        adamw(block_weights, first_blocks, second_blocks, block_grad, factor, LEARN_RATE),
        adamw(block_gains, first_gains, second_gains, gain_grad, factor, GAIN_RATE),
        adamw(entry_table, first_entry, second_entry, entry_grad, factor, LEARN_RATE),
        adamw(head_weights, first_head, second_head, head_grad, factor, LEARN_RATE),
        adamw(head_biases, first_biases, second_biases, bias_grad, factor, LEARN_RATE),
        adamw(head_edges, first_edges, second_edges, edge_grad, factor, LEARN_RATE),
    ]
    return tuple(new[i][k] for k in range(3) for i in range(6)) + (loss_sum, weight_total, grad_norm)


def solution(mesh):
    rows = [P(AXES, None, None), P(AXES, None), P(AXES), P(AXES, None), P(AXES, None), P(AXES, None)]
    state = [
        P(None, AXES, None), P(None, None, AXES), P(None, AXES),
        P(None, AXES, None), P(None, AXES), P(None, AXES),
    ]
    return jax.shard_map(
        functools.partial(on_device, dict(mesh.shape)),
        mesh=mesh,
        in_specs=tuple(rows + state * 3),
        out_specs=tuple(state * 3 + [P(), P(), P()]),
        check_vma=False,
    )
```

```python
import functools
import math

import jax
import jax.numpy as jnp
from jax import lax
from jax.experimental import pallas as pl
from jax.experimental.pallas import tpu as pltpu
from jax.sharding import PartitionSpec as P

D = 768
HEADS = 12
HD = 64
FF = 3072
HW = 1024
CH = 16
FREQ = 256
LAT = 256
BUF = 64
HB = 2
COPIES = 4
TSTEPS = 1000
ADAM_STEP = 5
SEQ = 320

BETA_ONE = 0.5
BETA_TWO = 0.5
LEARN_RATE = 0.03
GAIN_RATE = 0.3
DECAY_RATE = 0.02
ADAM_EPS = 1e-08
CLIP_NORM = 0.002
NORM_EPS = 1e-06
AXES = ("dp", "fsdp")
MESH_IDS = pl.DeviceIdType.MESH


REDUCE_LAGS = (0, 1, 3, 5, 7)
REDUCE_DEPTH = 3


def reduce_program(nz, row_count, width, columns_of, x_refs, y_refs, extra_ref, out_ref, scratch, between=None):
    (
        x_buf, y_buf, whole, land_core, first, land_first, second, land_second,
        last, last_low, land_last, extra_sem,
        load_sem, core_send, core_recv, first_send, first_recv, second_send, second_recv,
        last_send, last_recv, credit,
    ) = scratch
    dp, z = lax.axis_index("dp"), lax.axis_index("fsdp")
    core, xb, yb = lax.rem(dp, 2), lax.rem(dp // 2, 2), dp // 4
    group = row_count // 8
    part = group // nz
    starts, total = [], 0
    for columns in columns_of:
        starts.append(total)
        total += columns // width
    computed = total
    total += extra_ref.shape[0]

    core_peer = (dp + 1 - 2 * core, z)
    x_step, y_step = 2 - 4 * xb, 4 - 8 * yb
    z_peers = [(dp, lax.rem(z + s, nz)) for s in range(1, nz)]
    def loads(x_ref, y_ref, column, slot):
        return (
            pltpu.make_async_copy(x_ref, x_buf.at[slot], load_sem.at[0, slot]),
            pltpu.make_async_copy(
                y_ref.at[:, pl.ds(pl.multiple_of(column, 128), width)], y_buf.at[slot], load_sem.at[1, slot]
            ),
        )

    def prefetch(g):
        for number, columns in enumerate(columns_of):
            start, stop = starts[number], starts[number] + columns // width

            @pl.when((g >= start) & (g < stop))
            def _():
                for copy in loads(x_refs[number], y_refs[number], (g - start) * width, lax.rem(g, 2)):
                    copy.start()

    prefetch(0)
    barrier = pltpu.get_barrier_semaphore()
    for peer in [core_peer, (dp + x_step, z), (dp + y_step, z)] + z_peers:
        pl.semaphore_signal(barrier, inc=1, device_id=peer, device_id_type=MESH_IDS)
    pl.semaphore_wait(barrier, 2 + nz)

    def core_copy(g):
        return pltpu.make_async_remote_copy(
            src_ref=whole.at[lax.rem(g, 2), 1 - core],
            dst_ref=land_core.at[lax.rem(g, 4)],
            send_sem=core_send.at[lax.rem(g, 2)],
            recv_sem=core_recv.at[lax.rem(g, 4)],
            device_id=core_peer,
            device_id_type=MESH_IDS,
        )

    depth = REDUCE_DEPTH

    def first_copy(g):
        p = lax.rem(g, 2)
        mine = (1 - p) * xb + p * yb
        return pltpu.make_async_remote_copy(
            src_ref=first.at[lax.rem(g, depth), 1 - mine],
            dst_ref=land_first.at[g],
            send_sem=first_send.at[lax.rem(g, depth)],
            recv_sem=first_recv.at[g],
            device_id=(dp + (1 - p) * x_step + p * y_step, z),
            device_id_type=MESH_IDS,
        )

    def second_copy(g):
        p = lax.rem(g, 2)
        mine = (1 - p) * yb + p * xb
        return pltpu.make_async_remote_copy(
            src_ref=second.at[lax.rem(g, depth), 1 - mine],
            dst_ref=land_second.at[g],
            send_sem=second_send.at[lax.rem(g, depth)],
            recv_sem=second_recv.at[g],
            device_id=(dp + (1 - p) * y_step + p * x_step, z),
            device_id_type=MESH_IDS,
        )

    def last_copies(g):
        return [
            pltpu.make_async_remote_copy(
                src_ref=last_low.at[lax.rem(g, depth), lax.rem(z + s, nz)],
                dst_ref=land_last.at[g, s - 1],
                send_sem=last_send.at[lax.rem(g, depth), s - 1],
                recv_sem=last_recv.at[g, s - 1],
                device_id=z_peers[s - 1],
                device_id_type=MESH_IDS,
            )
            for s in range(1, nz)
        ]

    low_rows, low_width = last_low.shape[2:]
    folds = width // low_width

    def fold(block):
        return jnp.concatenate([block[:, k * low_width : (k + 1) * low_width] for k in range(folds)], 0)

    def stage_core(g):
        slot = lax.rem(g, 2)

        @pl.when(g >= 2)
        def _():
            core_copy(g - 2).wait_send()

        def put(number, value):
            yx, c = number // 2, number % 2
            whole[slot, c, yx] = value

        @pl.when(g < computed)
        def _():
            for copy in loads(x_refs[0], y_refs[0], 0, slot):
                copy.wait()
            product = lax.dot_general(
                x_buf[slot], y_buf[slot], (((0,), (0,)), ((), ())), preferred_element_type=jnp.float32
            )
            for number in range(8):
                put(number, product[number * group : (number + 1) * group].astype(jnp.bfloat16))

        @pl.when(g >= computed)
        def _():
            copies = [
                pltpu.make_async_copy(
                    extra_ref.at[g - computed, pl.ds(number * group, group), :],
                    whole.at[slot, number % 2, number // 2],
                    extra_sem.at[number],
                )
                for number in range(8)
            ]
            for copy in copies:
                copy.start()
            for copy in copies:
                copy.wait()

        @pl.when(g >= 4)
        def _():
            pl.semaphore_wait(credit, 1)
        core_copy(g).start()

    def stage_first(g):
        p = lax.rem(g, 2)

        @pl.when(g >= depth)
        def _():
            first_copy(g - depth).wait_send()
        core_copy(g).wait_recv()
        for f in range(2):
            for s in range(2):
                yx = (1 - p) * (2 * s + f) + p * (2 * f + s)
                first[lax.rem(g, depth), f, s] = (
                    whole[lax.rem(g, 2), core, yx].astype(jnp.float32)
                    + land_core[lax.rem(g, 4), yx].astype(jnp.float32)
                ).astype(jnp.bfloat16)

        @pl.when(g < total - 4)
        def _():
            pl.semaphore_signal(credit, inc=1, device_id=core_peer, device_id_type=MESH_IDS)
        first_copy(g).start()

    def stage_second(g):
        p = lax.rem(g, 2)
        mine = (1 - p) * xb + p * yb

        @pl.when(g >= depth)
        def _():
            second_copy(g - depth).wait_send()
        first_copy(g).wait_recv()
        for s in range(2):
            second[lax.rem(g, depth), s] = (
                first[lax.rem(g, depth), mine, s].astype(jnp.float32) + land_first[g, s].astype(jnp.float32)
            ).astype(jnp.bfloat16)
        second_copy(g).start()

    def stage_last(g):
        p = lax.rem(g, 2)
        mine = (1 - p) * yb + p * xb

        @pl.when(g >= depth)
        def _():
            for copy in last_copies(g - depth):
                copy.wait_send()
        second_copy(g).wait_recv()
        summed = second[lax.rem(g, depth), mine].astype(jnp.float32) + land_second[g].astype(jnp.float32)
        for k in range(nz):
            block = fold(summed[k * part : (k + 1) * part])
            last[lax.rem(g, depth), k] = block
            last_low[lax.rem(g, depth), k] = block.astype(jnp.bfloat16)
        for copy in last_copies(g):
            copy.start()

    def stage_out(g):
        for copy in last_copies(g):
            copy.wait_recv()
        value = last[lax.rem(g, depth), z]
        for s in range(1, nz):
            value = value + land_last[g, s - 1].astype(jnp.float32)
        for k in range(folds):
            out_ref[g, :, pl.ds(k * low_width, low_width)] = value[k * part : (k + 1) * part]

    lags = REDUCE_LAGS
    @pl.loop(0, total + lags[-1])
    def _(i):
        for stage, lag in zip((stage_out, stage_last, stage_second, stage_first), lags[:0:-1]):
            @pl.when((i >= lag) & (i < total + lag))
            def _():
                stage(i - lag)

        @pl.when(i + 1 < computed)
        def _():
            prefetch(i + 1)

        @pl.when(i < total)
        def _():
            stage_core(i)

        if between is not None:
            between(i)

    for g in range(max(total - 2, 0), total):
        core_copy(g).wait_send()
    for g in range(max(total - depth, 0), total):
        first_copy(g).wait_send()
        second_copy(g).wait_send()
        for copy in last_copies(g):
            copy.wait_send()


def reduce_scratch(tokens, row_count, width, total, low_shape, nz):
    bf, group = jnp.bfloat16, row_count // 8
    dma, depth = pltpu.SemaphoreType.DMA, REDUCE_DEPTH
    return [
        pltpu.VMEM((2, tokens, row_count), bf),
        pltpu.VMEM((2, tokens, width), bf),
        pltpu.VMEM((2, 2, 4, group, width), bf),
        pltpu.VMEM((4, 4, group, width), bf),
        pltpu.VMEM((depth, 2, 2, group, width), bf),
        pltpu.VMEM((total, 2, group, width), bf),
        pltpu.VMEM((depth, 2, group, width), bf),
        pltpu.VMEM((total, group, width), bf),
        pltpu.VMEM((depth, nz, *low_shape), jnp.float32),
        pltpu.VMEM((depth, nz, *low_shape), bf),
        pltpu.VMEM((total, nz - 1, *low_shape), bf),
        dma((8,)),
        dma((2, 2)), dma((2,)), dma((4,)), dma((depth,)), dma((total,)), dma((depth,)), dma((total,)),
        dma((depth, nz - 1)), dma((total, nz - 1)), pltpu.SemaphoreType.REGULAR,
    ]


def gather_program(nz, chunks, sources, results, sems):
    own_sem, last_send, last_recv, first_send, first_recv, second_send, second_recv, core_send, core_recv = sems
    dp, z = lax.axis_index("dp"), lax.axis_index("fsdp")
    core, xb, yb = lax.rem(dp, 2), lax.rem(dp // 2, 2), dp // 4
    core_peer = (dp + 1 - 2 * core, z)
    x_peer, y_peer = (dp + 2 - 4 * xb, z), (dp + 4 - 8 * yb, z)
    z_peers = [(dp, lax.rem(z + s, nz)) for s in range(1, nz)]
    barrier = pltpu.get_barrier_semaphore()
    for peer in [core_peer, x_peer, y_peer] + z_peers:
        pl.semaphore_signal(barrier, inc=1, device_id=peer, device_id_type=MESH_IDS)
    pl.semaphore_wait(barrier, 2 + nz)

    def remote(source, target, send, recv, peer):
        return pltpu.make_async_remote_copy(
            src_ref=source, dst_ref=target, send_sem=send, recv_sem=recv, device_id=peer, device_id_type=MESH_IDS
        )

    def source_of(k):
        source, index, column, _, _, width = chunks[k]
        ref = sources[source] if index is None else sources[source].at[index]
        return ref.at[:, pl.ds(column, width)]

    def result_of(k):
        _, _, _, result, column, width = chunks[k]
        return results[result].at[:, :, :, :, :, pl.ds(column, width)]

    def own(k):
        return pltpu.make_async_copy(source_of(k), result_of(k).at[yb, xb, core, z], own_sem.at[k])

    def to_z(k, source, target):
        return [
            remote(source, target, last_send.at[k, s], last_recv.at[k, s], z_peers[s]) for s in range(nz - 1)
        ]

    def to_pair(k, late, along_y, source, target):
        send, recv = (second_send, second_recv) if late else (first_send, first_recv)
        return [remote(source, target, send.at[k], recv.at[k], y_peer if along_y else x_peer)]

    def stage(k, number):
        result = result_of(k)
        block = result.at[yb, xb, core, z]
        if number == 0:
            return to_z(k, source_of(k), block)
        if number == 1:
            ref = result.at[yb, xb, core]
            return to_pair(k, False, k % 2, ref, ref)
        ref = result.at[:, xb, core] if k % 2 else result.at[yb, :, core]
        return to_pair(k, True, 1 - k % 2, ref, ref)

    def across(k):
        ref = result_of(k).at[:, :, core]
        return remote(ref, ref, core_send.at[k], core_recv.at[k], core_peer)

    total = len(chunks)

    def pass_on(k, number):
        if number == 0:
            own(k).wait()
        for copy in stage(k, number):
            copy.wait_recv()
        for copy in stage(k, number + 1) if number < 2 else [across(k)]:
            copy.start()

    def step(i):
        for number in (2, 1, 0):
            if 0 <= i - 2 * (number + 1) < total:
                pass_on(i - 2 * (number + 1), number)
        if i < total:
            own(i).start()
            for copy in stage(i, 0):
                copy.start()

    def finish():
        for k in range(total):
            for copy in stage(k, 0) + stage(k, 1) + stage(k, 2) + [across(k)]:
                copy.wait_send()
            across(k).wait_recv()

    return total + 6, step, finish


def gather_sems(total, nz):
    dma = pltpu.SemaphoreType.DMA
    return [dma((total,)), dma((total, nz - 1)), dma((total, nz - 1))] + [dma((total,))] * 6


def gather_kernel(nz, chunks, source_count, *refs):
    sources, refs = refs[:source_count], refs[source_count:]
    result_count = 1 + max(chunk[3] for chunk in chunks)
    steps, step, finish = gather_program(nz, chunks, sources, refs[:result_count], refs[result_count:])
    for i in range(steps):
        step(i)
    finish()


def gather_rows(sources, chunks, shapes, nz, collective_id):
    return pl.pallas_call(
        functools.partial(gather_kernel, nz, chunks, len(sources)),
        out_shape=[jax.ShapeDtypeStruct((2, 2, 2, nz, *shape), jnp.bfloat16) for shape in shapes],
        in_specs=[pl.BlockSpec(memory_space=pl.ANY)] * len(sources),
        out_specs=[pl.BlockSpec(memory_space=pl.ANY)] * len(shapes),
        scratch_shapes=gather_sems(len(chunks), nz),
        compiler_params=pltpu.CompilerParams(
            collective_id=collective_id, has_side_effects=True, vmem_limit_bytes=60 * 2**20
        ),
    )(*sources)


def exchange_kernel(dp_count, nz, in_ref, out_ref, send_sem, recv_sem):
    devices = dp_count * nz
    me = lax.axis_index("dp") * nz + lax.axis_index("fsdp")

    def peer(step):
        there = lax.rem(me + step, devices)
        return (there // nz, lax.rem(there, nz))

    barrier = pltpu.get_barrier_semaphore()

    @pl.loop(1, devices)
    def _(step):
        pl.semaphore_signal(barrier, inc=1, device_id=peer(step), device_id_type=MESH_IDS)

    pl.semaphore_wait(barrier, devices - 1)

    def copy(step):
        return pltpu.make_async_remote_copy(
            src_ref=in_ref,
            dst_ref=out_ref.at[me],
            send_sem=send_sem.at[step - 1],
            recv_sem=recv_sem.at[step - 1],
            device_id=peer(step),
            device_id_type=MESH_IDS,
        )

    @pl.loop(1, devices)
    def _(step):
        copy(step).start()

    out_ref[me] = in_ref[...]

    @pl.loop(1, devices)
    def _(step):
        copy(step).wait()


def exchange(values, dp_count, nz, collective_id):
    devices = dp_count * nz
    tile = jnp.broadcast_to(jnp.pad(values, (0, 128 - values.shape[0])), (8, 128))
    out = pl.pallas_call(
        functools.partial(exchange_kernel, dp_count, nz),
        out_shape=jax.ShapeDtypeStruct((devices, 8, 128), jnp.float32),
        in_specs=[pl.BlockSpec(memory_space=pltpu.VMEM)],
        out_specs=pl.BlockSpec(memory_space=pltpu.VMEM),
        scratch_shapes=[pltpu.SemaphoreType.DMA((devices - 1,)), pltpu.SemaphoreType.DMA((devices - 1,))],
        compiler_params=pltpu.CompilerParams(
            collective_id=collective_id, has_side_effects=True, vmem_limit_bytes=4 * 2**20
        ),
    )(tile)
    return out[:, 0, : values.shape[0]]


def dot_plain(left, right):
    return jnp.dot(left, right, preferred_element_type=jnp.float32)


def dot_left(left, right):
    return lax.dot_general(
        left, right, (((0,), (0,)), ((), ())), preferred_element_type=jnp.float32
    )


def dot_right(left, right):
    return lax.dot_general(
        left, right, (((1,), (1,)), ((), ())), preferred_element_type=jnp.float32
    )


KEPT = (
    ("normed", D, jnp.bfloat16), ("packed", 3 * D, jnp.bfloat16), ("mixed", D, jnp.bfloat16),
    ("second", D, jnp.bfloat16), ("upper", FF, jnp.bfloat16), ("inner", FF, jnp.float32),
    ("norm_one", D, jnp.float32), ("norm_two", D, jnp.float32), ("inv_one", 128, jnp.float32),
    ("inv_two", 128, jnp.float32),
)
KEPT_INDEX = {name: k for k, (name, _, _) in enumerate(KEPT)}
BACK = (("back_packed", 3 * D), ("back_attn", D), ("back_inner", FF), ("back_branch", D))
GELU_SCALE = math.sqrt(2.0 / math.pi)


def in_nn(x, w):
    return jnp.dot(x, w, preferred_element_type=jnp.float32)


def in_nt(x, w):
    return lax.dot_general(x, w, (((1,), (1,)), ((), ())), preferred_element_type=jnp.float32)


def in_tn(x, w):
    return lax.dot_general(x, w, (((0,), (0,)), ((), ())), preferred_element_type=jnp.float32)


def softmax_rows(scores):
    raised = jnp.exp(scores - jnp.max(scores, -1, keepdims=True))
    return raised * (1.0 / jnp.sum(raised, -1, keepdims=True))


def low_half():
    return lax.broadcasted_iota(jnp.int32, (SEQ, 2 * HD), 1) < HD


def forward_pieces(weights, entry, select_ref, mask_ref, hidden, kept, top_ref, gains_ref, need, leave):
    bf = jnp.bfloat16
    pieces = []
    gain = lambda row: gains_ref[row : row + 1, :]

    def start():
        need(entry)
        gains_ref[...] = in_nt(select_ref[2 * SEQ :, :], entry[...])
        hidden[...] = in_nt(select_ref[:SEQ, :], entry[...])
    pieces.append(start)

    def norm(layer, which):
        value = hidden[...]
        centred = value - jnp.mean(value, -1, keepdims=True)
        inv = lax.rsqrt(jnp.mean(centred * centred, -1, keepdims=True) + NORM_EPS)
        n = centred * inv
        names = ("norm_one", "inv_one", "normed") if which == 0 else ("norm_two", "inv_two", "second")
        kept[names[0]][layer] = n
        kept[names[1]][layer] = jnp.broadcast_to(inv, (SEQ, 128))
        kept[names[2]][layer] = (n * gain(2 * layer + which)).astype(bf)
        for name in names:
            leave(layer, name)

    def project(layer):
        norm(layer, 0)
        need(weights[4 * layer])
        kept["packed"][layer] = in_nn(kept["normed"][layer], weights[4 * layer][...]).astype(bf)
        leave(layer, "packed")

    def attend(layer, pair):
        packed = kept["packed"]
        cut = lambda k: packed[layer, :, k * D + pair * 2 * HD : k * D + (pair + 1) * 2 * HD]
        q, k, v = cut(0), cut(1), cut(2)
        low = low_half()
        parts = []
        for side in range(2):
            one = jnp.where(low if side == 0 else ~low, q, jnp.zeros((), bf))
            scores = in_nt(one, k) * HD ** (-0.5)
            if layer == 0:
                scores = jnp.where(mask_ref[...] > 0, scores, -1e30)
            parts.append(in_nn(softmax_rows(scores).astype(bf), v))
        kept["mixed"][layer, :, pair * 2 * HD : (pair + 1) * 2 * HD] = jnp.where(low, parts[0], parts[1]).astype(bf)

    def close(layer):
        leave(layer, "mixed")
        need(weights[4 * layer + 1])
        hidden[...] += in_nn(kept["mixed"][layer], weights[4 * layer + 1][...])
        norm(layer, 1)
        need(weights[4 * layer + 2])

    def up(layer, part, parts):
        columns = slice(part * FF // parts, (part + 1) * FF // parts)
        inner = in_nn(kept["second"][layer], weights[4 * layer + 2][:, columns])
        kept["inner"][layer, :, columns] = inner
        kept["upper"][layer, :, columns] = (
            0.5 * inner * (1.0 + jnp.tanh(GELU_SCALE * (inner + 0.044715 * inner * inner * inner)))
        ).astype(bf)

    def down(layer):
        leave(layer, "inner")
        leave(layer, "upper")
        need(weights[4 * layer + 3])
        hidden[...] += in_nt(kept["upper"][layer], weights[4 * layer + 3][...])

    def between():
        keep = mask_ref[...].reshape(1, SEQ)
        hidden[...] = hidden[...] * keep_column(keep) + in_nt(select_ref[SEQ : 2 * SEQ, :], entry[...])

    def keep_column(keep):
        return jnp.transpose(jnp.broadcast_to(keep, (128, SEQ)))[:, :1]

    for layer in range(2):
        pieces.append(functools.partial(project, layer))
        for pair in range(HEADS // 2):
            pieces.append(functools.partial(attend, layer, pair))
        pieces.append(functools.partial(close, layer))
        for part in range(3):
            pieces.append(functools.partial(up, layer, part, 3))
        pieces.append(functools.partial(down, layer))
        if layer == 0:
            pieces.append(between)

    def finish():
        top_ref[...] = hidden[BUF:, :].astype(bf)
    pieces.append(finish)
    return pieces


def forward_kernel(*refs):
    entry_hbm, weight_hbm, (select_ref, mask_ref), refs = refs[0], refs[1:9], refs[9:11], refs[11:]
    kept_hbm, (top_ref, gains_ref), refs = refs[: len(KEPT)], refs[len(KEPT) : len(KEPT) + 2], refs[len(KEPT) + 2 :]
    entry, weights, kept_refs, refs = refs[0], refs[1:9], refs[9 : 9 + len(KEPT)], refs[9 + len(KEPT) :]
    hidden, weight_sem, kept_sem = refs
    kept = {name: ref for (name, _, _), ref in zip(KEPT, kept_refs)}
    local = [(entry_hbm, entry)] + list(zip(weight_hbm, weights))
    fetches = {id(ref): pltpu.make_async_copy(hbm, ref, weight_sem.at[k]) for k, (hbm, ref) in enumerate(local)}
    for copy in fetches.values():
        copy.start()
    leaving = []

    def leave(layer, name):
        k = KEPT_INDEX[name]
        copy = pltpu.make_async_copy(kept_refs[k].at[layer], kept_hbm[k].at[layer], kept_sem.at[layer, k])
        copy.start()
        leaving.append(copy)

    pieces = forward_pieces(
        weights, entry, select_ref, mask_ref, hidden, kept, top_ref, gains_ref, lambda ref: fetches[id(ref)].wait(), leave
    )
    for piece in pieces:
        piece()
    for copy in leaving:
        copy.wait()


def trunk_forward(entry, weights, select, mask):
    bf, f32 = jnp.bfloat16, jnp.float32
    vmem, hbm = pl.BlockSpec(memory_space=pltpu.VMEM), pl.BlockSpec(memory_space=pl.ANY)
    kept_shapes = [(2, SEQ, columns) for _, columns, _ in KEPT]
    outs = pl.pallas_call(
        forward_kernel,
        out_shape=[jax.ShapeDtypeStruct(s, dtype) for s, (_, _, dtype) in zip(kept_shapes, KEPT)]
        + [jax.ShapeDtypeStruct((LAT, D), bf), jax.ShapeDtypeStruct((16, D), f32)],
        in_specs=[hbm] * 9 + [vmem] * 2,
        out_specs=[hbm] * len(KEPT) + [vmem] * 2,
        scratch_shapes=[pltpu.VMEM(w.shape, bf) for w in [entry] + weights]
        + [pltpu.VMEM(s, dtype) for s, (_, _, dtype) in zip(kept_shapes, KEPT)]
        + [pltpu.VMEM((SEQ, D), f32), pltpu.SemaphoreType.DMA((9,)), pltpu.SemaphoreType.DMA((2, len(KEPT)))],
        compiler_params=pltpu.CompilerParams(vmem_limit_bytes=60 * 2**20),
    )(entry, *weights, select, mask)
    count = len(KEPT)
    return outs[count], outs[count + 1], outs[:count]


BACK_KEPT = ("packed", "inner", "norm_one", "norm_two", "inv_one", "inv_two")
BACK_NAMES = tuple(name for name, _ in BACK)


def backward_pieces(layer, inputs, outputs, scratch):
    weight_hbm, (gains_ref, select_ref, mask_ref, upstream_ref, gain_before_ref) = inputs[:4], inputs[4:9]
    kept_hbm = inputs[9 : 9 + len(BACK_KEPT)]
    back_hbm, (hidden, gain_grad, small_hbm) = outputs[: len(BACK)], outputs[len(BACK) :]
    buffers, kept_refs, scratch = scratch[:2], scratch[2 : 2 + len(BACK_KEPT)], scratch[2 + len(BACK_KEPT) :]
    back_refs, (mixed, middle, small_stage, weight_sem, kept_sem, back_sem, small_sem) = (
        scratch[: len(BACK)], scratch[len(BACK) :]
    )
    bf = jnp.bfloat16
    back = dict(zip(BACK_NAMES, back_refs))
    kept = dict(zip(BACK_KEPT, kept_refs))
    views = (
        buffers[0].at[:, pl.ds(D, 3 * D)], buffers[0].at[:, pl.ds(0, D)], buffers[1], buffers[0]
    )
    QKV, OUT, UP, DOWN = range(4)

    def fetch(k):
        return pltpu.make_async_copy(weight_hbm[k], views[k], weight_sem.at[k])

    def fetch_kept(name):
        k = BACK_KEPT.index(name)
        return pltpu.make_async_copy(kept_hbm[k].at[layer], kept_refs[k], kept_sem.at[k])

    def leave(name):
        k = BACK_NAMES.index(name)
        return pltpu.make_async_copy(back_refs[k], back_hbm[k], back_sem.at[k])

    def gain(row):
        return gains_ref[row : row + 1, :]

    def norm_step(upstream, n, inv):
        return inv * (
            upstream - jnp.mean(upstream, -1, keepdims=True) - n * jnp.mean(upstream * n, -1, keepdims=True)
        )

    def begin():
        fetch(DOWN).start()
        fetch_kept("inner").start()
        fetch(UP).start()
        for name in ("norm_two", "inv_two", "packed", "norm_one", "inv_one"):
            fetch_kept(name).start()
        upstream = upstream_ref[...]
        if layer == 0:
            upstream = upstream * jnp.transpose(jnp.broadcast_to(mask_ref[...], (128, SEQ)))[:, :1]
        hidden[...] = upstream
        gain_grad[...] = gain_before_ref[...]

    def branch():
        back["back_branch"][...] = hidden[...].astype(bf)
        leave("back_branch").start()
        fetch(DOWN).wait()
        fetch_kept("inner").wait()

    def widen(part, parts):
        columns = slice(part * FF // parts, (part + 1) * FF // parts)
        up = in_nn(back["back_branch"][...], views[DOWN][:, columns])
        x = kept["inner"][:, columns]
        t = jnp.tanh(GELU_SCALE * (x + 0.044715 * x * x * x))
        slope = 0.5 * (1.0 + t) + 0.5 * x * (1.0 - t * t) * (GELU_SCALE * (1.0 + 3.0 * 0.044715 * x * x))
        back["back_inner"][:, columns] = (slope * up).astype(bf)

    def narrow():
        fetch(OUT).start()
        fetch(QKV).start()
        leave("back_inner").start()
        fetch(UP).wait()
        fetch_kept("norm_two").wait()
        fetch_kept("inv_two").wait()
        middle[...] = in_nt(back["back_inner"][...], views[UP][...])

    def renorm():
        value = middle[...]
        n = kept["norm_two"][...]
        gain_grad[2 * layer + 1 : 2 * layer + 2, :] = jnp.sum(value * n, 0, keepdims=True)
        middle[...] = hidden[...] + norm_step(value * gain(2 * layer + 1), n, kept["inv_two"][:, :1])
        back["back_attn"][...] = middle[...].astype(bf)
        leave("back_attn").start()

    def unmix():
        fetch(OUT).wait()
        fetch_kept("packed").wait()
        mixed[...] = in_nt(back["back_attn"][...], views[OUT][...]).astype(bf)

    def attend(pair):
        low = low_half()
        at = lambda k: slice(k * D + pair * 2 * HD, k * D + (pair + 1) * 2 * HD)
        q, k, v = (kept["packed"][:, at(i)] for i in range(3))
        up = mixed[:, at(0)]
        zero = jnp.zeros((), bf)
        parts = []
        for side in range(2):
            mine = low if side == 0 else ~low
            scores = in_nt(jnp.where(mine, q, zero), k) * HD ** (-0.5)
            if layer == 0:
                scores = jnp.where(mask_ref[...] > 0, scores, -1e30)
            attention = softmax_rows(scores)
            back_attention = in_nt(jnp.where(mine, up, zero), v)
            back_values = in_tn(attention.astype(bf), up)
            back_scores = (
                attention * (back_attention - jnp.sum(back_attention * attention, -1, keepdims=True))
            ).astype(bf)
            parts.append((in_nn(back_scores, k) * HD ** (-0.5), in_tn(back_scores, q) * HD ** (-0.5), back_values))
        for i in range(3):
            back["back_packed"][:, at(i)] = jnp.where(low, parts[0][i], parts[1][i]).astype(bf)

    def close():
        leave("back_packed").start()
        fetch(QKV).wait()
        fetch_kept("norm_one").wait()
        fetch_kept("inv_one").wait()
        value = in_nt(back["back_packed"][...], views[QKV][...])
        n = kept["norm_one"][...]
        gain_grad[2 * layer : 2 * layer + 1, :] = jnp.sum(value * n, 0, keepdims=True)
        hidden[...] = middle[...] + norm_step(value * gain(2 * layer), n, kept["inv_one"][:, :1])
        for name in BACK_NAMES:
            leave(name).wait()

    def small():
        small_stage[...] = (
            in_tn(hidden[...].astype(bf), select_ref[:SEQ, :])
            + in_tn(upstream_ref[...].astype(bf), select_ref[SEQ : 2 * SEQ, :])
            + in_tn(gain_grad[...].astype(bf), select_ref[2 * SEQ :, :])
        ).astype(bf)
        copy = pltpu.make_async_copy(small_stage, small_hbm.at[0], small_sem)
        copy.start()
        copy.wait()

    return (
        [begin, branch]
        + [functools.partial(widen, part, 3) for part in range(3)]
        + [narrow, renorm, unmix]
        + [functools.partial(attend, pair) for pair in range(HEADS // 2)]
        + [close]
        + ([small] if layer == 0 else [])
    )


def backward_kernel(layer, reduction, *refs):
    input_count, output_count = 9 + len(BACK_KEPT), len(BACK) + 3
    inputs, refs = refs[:input_count], refs[input_count:]
    if reduction is None:
        for piece in backward_pieces(layer, inputs, refs[:output_count], refs[output_count:]):
            piece()
        return
    nz, row_count, width, jobs, has_extras = reduction
    side_refs = []
    for side in range(2):
        chosen = []
        for job in jobs:
            if job[side] is None:
                chosen.append((None, job[2 + side]))
            else:
                chosen.append((refs[0], job[side][0]))
                refs = refs[1:]
        side_refs.append(chosen)
    extra_ref = None
    if has_extras:
        extra_ref, refs = refs[0], refs[1:]
    outputs, summed, refs = refs[:output_count], refs[output_count], refs[output_count + 1 :]
    scratch_count = 2 + len(BACK_KEPT) + len(BACK) + 7

    def resolve(ref, index):
        if ref is None:
            return outputs[BACK_NAMES.index(index)]
        return ref if index is None else ref.at[index]

    x_refs, y_refs = ([resolve(*pair) for pair in chosen] for chosen in side_refs)
    pieces = backward_pieces(layer, inputs, outputs, refs[:scratch_count])
    each, stride = (1, 2) if layer == 1 else (2, 1)

    def between(i):
        for turn in range(-(-len(pieces) // each)):
            @pl.when(i == turn * stride)
            def _():
                for piece in pieces[turn * each : (turn + 1) * each]:
                    piece()

    reduce_program(
        nz, row_count, width, [job[4] for job in jobs], x_refs, y_refs, outputs[-1] if extra_ref is None else extra_ref,
        summed, refs[scratch_count:], between,
    )


def layer_backward(
    layer, gains, weights, select, mask, upstream, gain_before, kept, pairs=None, extras=None, sizes=None, collective_id=None
):
    bf, f32 = jnp.bfloat16, jnp.float32
    vmem, hbm = pl.BlockSpec(memory_space=pltpu.VMEM), pl.BlockSpec(memory_space=pl.ANY)
    kept_in = [kept[KEPT_INDEX[name]] for name in BACK_KEPT]
    static, operands, more, summed, scratch = None, [], {}, [], []
    if pairs is not None:
        row_count, width, low_shape, nz = sizes
        widths, jobs, sides = dict(BACK), [], ([], [])
        for pair in pairs:
            marks, columns = [], 0
            for side, entry in enumerate(pair):
                if isinstance(entry, str):
                    marks.append((None, entry))
                    columns = widths[entry]
                else:
                    array, index = entry if isinstance(entry, tuple) else (entry, None)
                    sides[side].append(array)
                    marks.append(((index,), None))
                    columns, tokens = array.shape[-1], array.shape[-2]
            jobs.append((marks[0][0], marks[1][0], marks[0][1], marks[1][1], columns))
        total = sum(job[4] // width for job in jobs) + (1 if extras is None else extras.shape[0])
        operands = sides[0] + sides[1] + ([] if extras is None else [extras])
        static = (nz, row_count, width, jobs, extras is not None)
        summed = [jax.ShapeDtypeStruct((total, row_count // 8 // nz, width), f32)]
        scratch = reduce_scratch(tokens, row_count, width, total, low_shape, nz)
        more = {"collective_id": collective_id, "has_side_effects": True}
    dma = pltpu.SemaphoreType.DMA
    outs = pl.pallas_call(
        functools.partial(backward_kernel, layer, static),
        out_shape=[jax.ShapeDtypeStruct((SEQ, columns), bf) for _, columns in BACK]
        + [
            jax.ShapeDtypeStruct((SEQ, D), f32), jax.ShapeDtypeStruct((16, D), f32),
            jax.ShapeDtypeStruct((1, D, TRUNK_WIDTH), bf),
        ]
        + summed,
        in_specs=[hbm] * 4 + [vmem] * 5 + [hbm] * (len(BACK_KEPT) + len(operands)),
        out_specs=[hbm] * len(BACK) + [vmem] * 2 + [hbm] + [vmem] * len(summed),
        scratch_shapes=[pltpu.VMEM((D, FF), bf)] * 2
        + [pltpu.VMEM(a.shape[1:], a.dtype) for a in kept_in]
        + [pltpu.VMEM((SEQ, columns), bf) for _, columns in BACK]
        + [
            pltpu.VMEM((SEQ, D), bf), pltpu.VMEM((SEQ, D), f32),
            pltpu.VMEM((D, TRUNK_WIDTH) if layer == 0 else (16, 128), bf),
            dma((4,)), dma((len(BACK_KEPT),)), dma((len(BACK),)), dma,
        ]
        + scratch,
        compiler_params=pltpu.CompilerParams(vmem_limit_bytes=60 * 2**20, **more),
    )(*weights, gains, select, mask, upstream, gain_before, *kept_in, *operands)
    return dict(zip(BACK_NAMES, outs)), *outs[len(BACK) :]


def layer_pairs(layer, kept, back):
    left = lambda name: (kept[KEPT_INDEX[name]], layer)
    return [
        (left("normed"), back["back_packed"]), (left("mixed"), back["back_attn"]),
        (left("second"), back["back_inner"]), (back["back_branch"], left("upper")),
    ]


ROWS_AT_ONCE = 192
HEAD_WEIGHTS = ((HW, 3 * HW), (HW, HW), (HW, HW)) * HB + (
    (HW, D), (HW, HW), (HW, HW), (HW, HW), (HW, FREQ), (HW, 128), (HW, 128)
)
HEAD_LEFT = (3, 1, 1, 1, 1) * HB + (1, 1, 1, 1, 1, 1, 1, 1)


def sigmoid(x):
    return 0.5 + 0.5 * jnp.tanh(0.5 * x)


def head_kernel(tokens, *refs):
    (embed_ref, noisy_ref, target_ref, loss_col_ref, bias_ref, cond_ref), refs = refs[:6], refs[6:]
    count = len(HEAD_WEIGHTS)
    block_hbm, edge_hbm, refs = refs[:HB], refs[HB : HB + 7], refs[HB + 7 :]
    weight_hbm = [
        block.at[:, pl.ds(column, width)]
        for block in block_hbm
        for column, width in ((0, 3 * HW), (3 * HW, HW), (4 * HW, HW))
    ] + list(edge_hbm)
    left_hbm, refs = refs[: len(HEAD_LEFT)], refs[len(HEAD_LEFT) :]
    (pred_ref, back_cond_ref, back_token_ref, bias_grad_ref, loss_ref), refs = refs[:5], refs[5:]
    weights, refs = refs[:count], refs[count:]
    left, refs = refs[: len(HEAD_LEFT)], refs[len(HEAD_LEFT) :]
    (
        time_inner, conditioning, projected, cond_sum, stream, back_silu, t0, t1,
        scale1, normed, inner, gate, branch, inverse, weight_sem, left_sem,
    ) = refs
    cond_t, time_two_t, shift_t, scale_t, time_one_t, in_t, out_t = weights[3 * HB :]
    per_block = 5
    silu_cond, time_hidden, back_time, back_time_inner, back_shift, back_scale, final_low, back_low = left[
        per_block * HB :
    ]
    bf = jnp.bfloat16

    def fetch(k):
        return pltpu.make_async_copy(weight_hbm[k], weights[k], weight_sem.at[k])

    order = [3 * HB, 3 * HB + 4, 3 * HB + 1, 3 * HB + 5]
    for b in range(HB):
        order += [3 * b, 3 * b + 1, 3 * b + 2]
    order += [3 * HB + 2, 3 * HB + 3, 3 * HB + 6]
    for k in order:
        fetch(k).start()

    def nn(x, w):
        return jnp.dot(x, w, preferred_element_type=jnp.float32)

    def nt(x, w):
        return lax.dot_general(x, w, (((1,), (1,)), ((), ())), preferred_element_type=jnp.float32)

    def by_rows(body):
        for i in range(0, tokens, ROWS_AT_ONCE):
            body(slice(i, i + ROWS_AT_ONCE))

    bias_grad_ref[...] = jnp.zeros_like(bias_grad_ref)
    loss_ref[...] = jnp.zeros_like(loss_ref)
    cond_sum[...] = jnp.zeros_like(cond_sum)

    def bias(row):
        return bias_ref[row : row + 1, :]

    def add_bias_grad(row, value):
        bias_grad_ref[row : row + 1, :] += jnp.sum(value.astype(jnp.float32), 0, keepdims=True)

    base = per_block * HB
    doubled = [per_block * b for b in range(HB)] + [base + 2, base + 3]

    def leave(k, c, half):
        source = left[k].at[pl.ds(half * tokens, tokens), :] if k in doubled else left[k]
        return pltpu.make_async_copy(source, left_hbm[k].at[c], left_sem.at[k, half if k in doubled else 0])

    def one_copy(pair, half):
        c = 2 * pair + half
        own = slice(half * tokens, (half + 1) * tokens)

        def need(*numbers):
            if half == 0:
                @pl.when(pair == 0)
                def _():
                    for k in numbers:
                        fetch(k).wait()

        def send(k):
            leave(k, c, half).start()

        def room(*numbers):
            for k in numbers:
                if half == 1 and k not in doubled:
                    leave(k, c, half).wait()
                else:
                    @pl.when(pair > 0)
                    def _():
                        leave(k, c, half).wait()

        room(base, base + 1)
        need(3 * HB)

        if half == 0:
            @pl.when(pair == 0)
            def _():
                projected[...] = nt(cond_ref[...], cond_t[...])

        need(3 * HB + 4, 3 * HB + 1, 3 * HB + 5)
        t1[...] = nt(embed_ref[c], time_one_t[...])

        def _(r):
            value = t1[r, :] + bias(10)
            time_inner[own, :] = value
            time_hidden[r, :] = (value * sigmoid(value)).astype(bf)
        by_rows(_)
        send(base + 1)
        t0[...] = nt(time_hidden[...], time_two_t[...])
        stream[...] = nt(noisy_ref[c], in_t[...])

        def _(r):
            value = projected[r, :] + (t0[r, :] + bias(11))
            conditioning[own, :] = value
            silu_cond[r, :] = (value * sigmoid(value)).astype(bf)
            stream[r, :] = stream[r, :] + bias(14)
        by_rows(_)
        send(base)

        for b in range(HB):
            w_mod, w_up, w_down = weights[3 * b : 3 * b + 3]
            bm, shaped, back_inner, back_branch, hidden = left[per_block * b : per_block * (b + 1)]
            room(*range(per_block * b, per_block * (b + 1)))
            need(3 * b)
            t0[...] = nn(silu_cond[...], w_mod[:, :HW])
            t1[...] = nn(silu_cond[...], w_mod[:, HW : 2 * HW])

            def _(r):
                value = stream[r, :]
                centred = value - jnp.mean(value, -1, keepdims=True)
                inv = lax.rsqrt(jnp.mean(centred * centred, -1, keepdims=True) + NORM_EPS)
                n = centred * inv
                s = 1.0 + (t1[r, :] + bias(5 * b + 1))
                inverse[b, r, :] = jnp.broadcast_to(inv, (ROWS_AT_ONCE, 128))
                normed[b, r, :] = n
                scale1[b, r, :] = s
                shaped[r, :] = (n * s + (t0[r, :] + bias(5 * b))).astype(bf)
            by_rows(_)
            send(per_block * b + 1)
            need(3 * b + 1)
            inner[b] = nn(shaped[...], w_up[...])

            def _(r):
                value = inner[b, r, :] + bias(5 * b + 3)
                inner[b, r, :] = value
                hidden[r, :] = (value * sigmoid(value)).astype(bf)
            by_rows(_)
            send(per_block * b + 4)
            need(3 * b + 2)
            t0[...] = nn(silu_cond[...], w_mod[:, 2 * HW :])
            t1[...] = nt(hidden[...], w_down[...])

            def _(r):
                value = t1[r, :] + bias(5 * b + 4)
                g = t0[r, :] + bias(5 * b + 2)
                branch[b, r, :] = value.astype(bf)
                gate[b, r, :] = g.astype(bf)
                stream[r, :] = stream[r, :] + g * value
            by_rows(_)

        need(3 * HB + 2, 3 * HB + 3, 3 * HB + 6)
        room(*range(base + 4, base + 8))
        t0[...] = nt(silu_cond[...], shift_t[...])
        t1[...] = nt(silu_cond[...], scale_t[...])
        def _(r):
            value = stream[r, :]
            centred = value - jnp.mean(value, -1, keepdims=True)
            inv = lax.rsqrt(jnp.mean(centred * centred, -1, keepdims=True) + NORM_EPS)
            n = centred * inv
            s = 1.0 + (t1[r, :] + bias(13))
            inverse[HB, r, :] = jnp.broadcast_to(inv, (ROWS_AT_ONCE, 128))
            back_silu[own, :] = n
            t1[r, :] = s
            final_low[r, :] = (n * s + (t0[r, :] + bias(12))).astype(bf)
        by_rows(_)
        send(base + 6)
        difference = nn(final_low[...], out_t[...]) - target_ref[c]
        loss_ref[...] += loss_col_ref[c] * difference * difference
        pred_ref[c] = (loss_col_ref[c] * bias_ref[15:16, :128] * difference).astype(bf)
        t0[...] = nt(pred_ref[c], out_t[...])

        def _(r):
            back = t0[r, :]
            n = back_silu[own, :]
            low_shift, low_scale = back.astype(bf), (back * n).astype(bf)
            back_shift[r, :] = low_shift
            back_scale[r, :] = low_scale
            up = back * t1[r, :]
            add_bias_grad(12, low_shift)
            add_bias_grad(13, low_scale)
            stream[r, :] = inverse[HB, r, :1] * (
                up - jnp.mean(up, -1, keepdims=True) - n * jnp.mean(up * n, -1, keepdims=True)
            )
        by_rows(_)
        send(base + 4)
        send(base + 5)
        back_silu[own, :] = nn(back_shift[...], shift_t[...]) + nn(back_scale[...], scale_t[...])

        for b in reversed(range(HB)):
            w_mod, w_up, w_down = weights[3 * b : 3 * b + 3]
            bm, shaped, back_inner, back_branch, hidden = left[per_block * b : per_block * (b + 1)]

            def _(r):
                back = stream[r, :]
                low = (back * gate[b, r, :].astype(jnp.float32)).astype(bf)
                low_gate = (back * branch[b, r, :].astype(jnp.float32)).astype(bf)
                back_branch[r, :] = low
                bm[own, 2 * HW :] = low_gate
                add_bias_grad(5 * b + 4, low)
                add_bias_grad(5 * b + 2, low_gate)
            by_rows(_)
            send(per_block * b + 3)
            t0[...] = nn(back_branch[...], w_down[...])

            def _(r):
                value = inner[b, r, :]
                s = sigmoid(value)
                low = (t0[r, :] * (s * (1.0 + value * (1.0 - s)))).astype(bf)
                back_inner[r, :] = low
                add_bias_grad(5 * b + 3, low)
            by_rows(_)
            send(per_block * b + 2)
            t0[...] = nt(back_inner[...], w_up[...])

            def _(r):
                back = t0[r, :]
                n = normed[b, r, :]
                low_shift, low_scale = back.astype(bf), (back * n).astype(bf)
                bm[own, :HW] = low_shift
                bm[own, HW : 2 * HW] = low_scale
                add_bias_grad(5 * b, low_shift)
                add_bias_grad(5 * b + 1, low_scale)
                up = back * scale1[b, r, :]
                stream[r, :] = stream[r, :] + inverse[b, r, :1] * (
                    up - jnp.mean(up, -1, keepdims=True) - n * jnp.mean(up * n, -1, keepdims=True)
                )
            by_rows(_)
            send(per_block * b)

        def _(r):
            low_stream = stream[r, :].astype(bf)
            back_low[r, :] = low_stream
            add_bias_grad(14, low_stream)
        by_rows(_)
        send(base + 7)

    @pl.loop(0, COPIES // 2)
    def _(pair):
        for half in range(2):
            one_copy(pair, half)
        for b in range(HB):
            for n in range(0, HW, 256):
                back_silu[:, n : n + 256] += nt(left[per_block * b][...], weights[3 * b][n : n + 256, :])
        for half in range(2):
            @pl.when(pair > 0)
            def _():
                leave(base + 2, 2 * pair + half, half).wait()
                leave(base + 3, 2 * pair + half, half).wait()

        for first in range(0, 2 * tokens, 32):
            own, sum_rows = slice(first, first + 32), slice(first % tokens, first % tokens + 32)
            value = conditioning[own, :]
            s = sigmoid(value)
            back = back_silu[own, :] * (s * (1.0 + value * (1.0 - s)))
            low = back.astype(bf)
            cond_sum[sum_rows, :] = cond_sum[sum_rows, :] + back
            back_time[own, :] = low
            add_bias_grad(11, low)
        for n in range(0, HW, 256):
            back_silu[:, n : n + 256] = nn(back_time[...], time_two_t[:, n : n + 256])
        for first in range(0, 2 * tokens, 32):
            own = slice(first, first + 32)
            value = time_inner[own, :]
            s = sigmoid(value)
            low = (back_silu[own, :] * (s * (1.0 + value * (1.0 - s)))).astype(bf)
            back_time_inner[own, :] = low
            add_bias_grad(10, low)
        for half in range(2):
            leave(base + 2, 2 * pair + half, half).start()
            leave(base + 3, 2 * pair + half, half).start()

    back_cond_ref[...] = cond_sum[...].astype(bf)
    back_token_ref[...] = nn(back_cond_ref[...], cond_t[...]).astype(bf)
    for k in range(len(HEAD_LEFT)):
        for half in (0, 1) if k in doubled else (1,):
            leave(k, COPIES - 2 + half, half).wait()


def head_pass(
    blocks, edges, biases, cond_rows, clean_rows, noise_rows, step_rows, weight_rows, weight_total
):
    bf = jnp.bfloat16
    tokens = cond_rows.shape[0]
    half_freq = FREQ // 2
    frequencies = jnp.exp(-math.log(10000.0) * jnp.arange(half_freq, dtype=jnp.float32) / half_freq)
    step_times = step_rows.astype(jnp.float32).T
    angles = step_times[..., None] * frequencies
    time_embed = jnp.concatenate([jnp.cos(angles), jnp.sin(angles)], -1).astype(bf)
    phase_angle = (step_times / TSTEPS + 0.008) / 1.008 * (math.pi / 2)
    keep_part = jnp.cos(phase_angle)[..., None]
    noise_part = jnp.sin(phase_angle)[..., None]
    clean_copies = clean_rows.astype(jnp.float32)[None]
    fresh_noise = noise_rows.astype(jnp.float32).reshape(tokens, COPIES, CH).transpose(1, 0, 2)
    wide = ((0, 0), (0, 0), (0, 128 - CH))
    noisy = jnp.pad((keep_part * clean_copies + noise_part * fresh_noise).astype(bf), wide)
    target = jnp.pad(keep_part * fresh_noise - noise_part * clean_copies, wide)
    by_copy = jnp.broadcast_to(weight_rows.T[..., None], (COPIES, tokens, 128))
    f32 = jnp.float32
    vmem, hbm = pl.BlockSpec(memory_space=pltpu.VMEM), pl.BlockSpec(memory_space=pl.ANY)
    lefts = [(COPIES, tokens, k * HW) for k in HEAD_LEFT]
    units = lambda *lead: pltpu.VMEM((*lead, tokens, HW), f32)
    outs = pl.pallas_call(
        functools.partial(head_kernel, tokens),
        out_shape=[jax.ShapeDtypeStruct(shape, bf) for shape in lefts]
        + [
            jax.ShapeDtypeStruct((COPIES, tokens, 128), bf),
            jax.ShapeDtypeStruct((tokens, HW), bf),
            jax.ShapeDtypeStruct((tokens, D), bf),
            jax.ShapeDtypeStruct((5 * (HB + 1) + 1, HW), f32),
            jax.ShapeDtypeStruct((tokens, 128), f32),
        ],
        in_specs=[vmem] * 6 + [hbm] * (HB + 7),
        out_specs=[hbm] * len(HEAD_LEFT) + [vmem] * 5,
        scratch_shapes=[pltpu.VMEM(shape, bf) for shape in HEAD_WEIGHTS]
        + [
            pltpu.VMEM((2 * tokens if k in (0, 5, 5 * HB + 2, 5 * HB + 3) else tokens, units_of * HW), bf)
            for k, units_of in enumerate(HEAD_LEFT)
        ]
        + [pltpu.VMEM((2 * tokens, HW), f32)] * 2
        + [units()] * 3
        + [pltpu.VMEM((2 * tokens, HW), f32)]
        + [units()] * 2
        + [units(HB)] * 3
        + [pltpu.VMEM((HB, tokens, HW), bf)] * 2
        + [
            pltpu.VMEM((HB + 1, tokens, 128), f32),
            pltpu.SemaphoreType.DMA((len(HEAD_WEIGHTS),)), pltpu.SemaphoreType.DMA((len(HEAD_LEFT), 2)),
        ],
        compiler_params=pltpu.CompilerParams(vmem_limit_bytes=63_400_000),
    )(
        time_embed, noisy, target, by_copy * (1.0 / CH),
        jnp.concatenate([biases.reshape(5 * (HB + 1), HW), jnp.full((1, HW), 2.0 / weight_total)], 0), cond_rows,
        *blocks, *edges,
    )
    left = [a.reshape(COPIES * tokens, -1) for a in outs[: len(HEAD_LEFT)]]
    back_pred, back_cond, back_tokens, bias_grad, loss_part = outs[len(HEAD_LEFT) :]
    silu_cond, time_hidden, back_time, back_time_inner, back_shift, back_scale, final_low, back_low = left[5 * HB :]
    pairs = []
    for b in range(HB):
        bm, shaped, back_inner, back_branch, hidden = left[5 * b : 5 * (b + 1)]
        pairs += [(silu_cond, bm), (shaped, back_inner), (back_branch, hidden)]
    pairs += [(back_time, time_hidden), (back_shift, silu_cond), (back_scale, silu_cond)]
    flat = lambda a: a.reshape(COPIES * tokens, -1)
    small = (
        dot_left(back_cond, cond_rows),
        dot_left(back_time_inner, flat(time_embed)),
        dot_left(back_low, flat(noisy))[:, :CH],
        dot_left(final_low, flat(back_pred))[:, :CH],
    )
    bias_grad = bias_grad[: 5 * (HB + 1)].reshape(HB + 1, 5 * HW)
    return (jnp.sum(loss_part), pairs, small, bias_grad, back_tokens)


def adamw(master, first, second, gradient, factor, step_rate):
    clipped = gradient * factor
    first_new = BETA_ONE * first + (1.0 - BETA_ONE) * clipped
    second_new = BETA_TWO * second + (1.0 - BETA_TWO) * clipped * clipped
    mean_hat = first_new / (1.0 - BETA_ONE**ADAM_STEP)
    var_hat = second_new / (1.0 - BETA_TWO**ADAM_STEP)
    updated = master - step_rate * (mean_hat / (jnp.sqrt(var_hat) + ADAM_EPS) + DECAY_RATE * master)
    return (updated, first_new, second_new)


TRUNK_PARTS = (3 * D, D, FF, FF)
HEAD_PARTS = (3 * HW, HW, HW)
EDGE_PARTS = (D, HW, HW, HW, FREQ, 128)
TRUNK_WIDTH = 768
HEAD_WIDTH = 512


def gather_plan(part_sets, limit):
    chunks, shapes = [], []
    for source, index, rows, parts in part_sets:
        column = 0
        for part in parts:
            for k in range(0, part, limit):
                chunks.append((source, index, column + k, len(shapes), k, min(limit, part - k)))
            shapes.append((rows, part))
            column += part
    return chunks, shapes


def plain_gather(sources, chunks, shapes):
    ends = {}
    for source, index, column, result, at, width in chunks:
        start, stop = ends.get(result, (source, index, column, column))[2:]
        ends[result] = (source, index, min(start, column), max(stop, column + width))
    wholes = {}
    results = []
    for number in range(len(shapes)):
        source, index, start, stop = ends[number]
        if (source, index) not in wholes:
            block = sources[source] if index is None else sources[source][index]
            wholes[source, index] = lax.all_gather(block, AXES, axis=0, tiled=True)
        results.append(wholes[source, index][:, start:stop])
    return results


def scatter_sum(values):
    low = lax.psum_scatter(values, "dp", scatter_dimension=0, tiled=True)
    return lax.psum_scatter(low, "fsdp", scatter_dimension=0, tiled=True)


def on_device(
    mesh_shape,
    latents, orders, mask_counts, noise, timesteps, loss_weights,
    block_weights, block_gains, entry_table, head_weights, head_biases, head_edges,
    first_blocks, first_gains, first_entry, first_head, first_biases, first_edges,
    second_blocks, second_gains, second_entry, second_head, second_biases, second_edges,
):
    dp_count, nz = mesh_shape["dp"], mesh_shape["fsdp"]
    devices = dp_count * nz
    me = lax.axis_index("dp") * nz + lax.axis_index("fsdp")
    r0, r1 = D // devices, HW // devices
    direct = dp_count == 8 and nz > 1 and (D // 8) % 16 == 0
    bf = jnp.bfloat16

    low_blocks = block_weights.astype(bf)
    local_total = jnp.sum(mask_counts)
    terms, rest = [local_total.astype(bf)], jnp.sum(loss_weights)
    for _ in range(3):
        terms.append(lax.reduce_precision(rest, 8, 7).astype(bf))
        rest = rest - terms[-1].astype(jnp.float32)
    low_entry = jnp.concatenate(
        [
            entry_table.T.astype(bf), block_gains.reshape(4, r0).T.astype(bf),
            jnp.broadcast_to(jnp.stack(terms), (r0, 4)), jnp.zeros((r0, 104), bf),
        ],
        1,
    )
    low_head = head_weights.astype(bf)
    edge = head_edges.T.astype(bf)
    base = D + 2 * CH
    low_edges = jnp.concatenate(
        [
            edge[:, :D], edge[:, base + FREQ :], edge[:, base : base + FREQ], edge[:, D:base],
            head_biases.reshape((HB + 1) * 5, r1).T.astype(bf), jnp.zeros((r1, 81), bf),
        ],
        1,
    )
    chunks, shapes = gather_plan(
        [(1, None, r0, (TRUNK_WIDTH,)), (0, 0, r0, TRUNK_PARTS), (0, 1, r0, TRUNK_PARTS), (2, None, r1, EDGE_PARTS)],
        TRUNK_WIDTH,
    )
    sources = [low_blocks, low_entry, low_edges]
    if direct:
        gathered = [a.reshape(devices * a.shape[4], -1) for a in gather_rows(sources, chunks, shapes, nz, 1)]
    else:
        gathered = plain_gather(sources, chunks, shapes)
    trunk, edge_mats = gathered[:9], gathered[9:]
    head_blocks = [lax.all_gather(low_head[b], AXES, axis=0, tiled=True) for b in range(HB)]

    early = trunk[0][::r0, 2 * SEQ + CH + 4 : 2 * SEQ + CH + 8].astype(jnp.float32)
    counts = early[:, 0].astype(jnp.int32)
    weight_total = jnp.sum(early[:, 1:])
    count_ends = jnp.cumsum(counts)
    count_starts = count_ends - counts
    offset = jnp.sum(jnp.where(jnp.arange(devices) == me, count_starts, 0))

    order_row = orders[0]
    clean = latents[0]
    ids = jnp.arange(LAT, dtype=jnp.int32)
    masked = jnp.any((order_row[:, None] == ids[None, :]) & (ids < local_total)[:, None], 0)
    key_keep = jnp.concatenate([jnp.ones((BUF,), jnp.float32), 1.0 - masked.astype(jnp.float32)])
    positions = jnp.arange(SEQ, dtype=jnp.int32)
    columns = jnp.arange(TRUNK_WIDTH, dtype=jnp.int32)
    pick_rows = jnp.concatenate([positions, SEQ + positions, 2 * SEQ + CH + jnp.arange(16, dtype=jnp.int32)])
    select = (pick_rows[:, None] == columns[None, :]).astype(bf) + jnp.pad(
        clean, ((BUF, SEQ + 16), (2 * SEQ, TRUNK_WIDTH - 2 * SEQ - CH))
    )
    top_rows, gains, kept = trunk_forward(trunk[0], trunk[1:9], select, key_keep[None])

    capacity = (LAT + devices - 1) // devices
    slots = devices * capacity
    slot_ids = jnp.arange(slots, dtype=jnp.int32)
    slot_token = jnp.mod(slot_ids // capacity - offset, devices) + devices * (slot_ids % capacity)
    slot_position = jnp.sum(
        jnp.where(slot_token[:, None] == ids[None, :], order_row[None, :], 0), 1
    )
    pick = (
        (slot_position[:, None] == ids[None, :]) & (slot_token < local_total)[:, None]
    ).astype(bf)
    outgoing = dot_plain(
        pick, jnp.concatenate([top_rows, clean, jnp.zeros((LAT, 112), bf)], 1)
    ).astype(bf)
    incoming = lax.all_to_all(
        outgoing.reshape(devices, capacity, -1), AXES, split_axis=0, concat_axis=0, tiled=True
    ).reshape(slots, -1)
    head_rows = noise.shape[0]
    token_ids = jnp.arange(head_rows, dtype=jnp.int32) * devices + me
    inside = (token_ids[:, None] >= count_starts[None, :]) & (token_ids[:, None] < count_ends[None, :])
    first_token = count_starts + jnp.mod(me - count_starts, devices)
    source_slot = (
        jnp.arange(devices, dtype=jnp.int32)[None, :] * capacity
        + (token_ids[:, None] - first_token[None, :]) // devices
    )
    row_slot = jnp.sum(jnp.where(inside, source_slot, 0), 1)
    place = (row_slot[:, None] == slot_ids[None, :]).astype(bf)
    received = dot_plain(place, incoming).astype(bf)

    misc = edge_mats[5]
    biases = (
        misc[:, 2 * CH : 2 * CH + 5 * (HB + 1)]
        .reshape(devices, r1, HB + 1, 5)
        .transpose(2, 0, 3, 1)
        .reshape(HB + 1, 5 * HW)
        .astype(jnp.float32)
    )
    loss_local, head_pairs, small, bias_grad, back_tokens = head_pass(
        head_blocks,
        edge_mats[:5]
        + [
            jnp.pad(misc[:, :CH], ((0, 0), (0, 128 - CH))),
            jnp.pad(misc[:, CH : 2 * CH], ((0, 0), (0, 128 - CH))),
        ],
        biases,
        received[:, :D],
        received[:, D : D + CH],
        noise,
        timesteps,
        loss_weights,
        weight_total,
    )
    grad_cond_t, grad_time_one_t, grad_in_t, grad_out_t = small
    bias_t = (
        bias_grad.reshape(HB + 1, devices, 5, r1).transpose(1, 3, 0, 2).reshape(HW, 5 * (HB + 1))
    )
    head_small = jnp.concatenate(
        [grad_cond_t, grad_time_one_t, grad_in_t, grad_out_t, bias_t, jnp.zeros((HW, 465), jnp.float32)], 1
    ).astype(bf)
    returning = dot_left(place, back_tokens.astype(bf)).astype(bf)
    returned = lax.all_to_all(
        returning.reshape(devices, capacity, D), AXES, split_axis=0, concat_axis=0, tiled=True
    ).reshape(slots, D)
    back_top = jnp.concatenate([jnp.zeros((BUF, D), jnp.float32), dot_left(pick, returned)], 0)
    mask = key_keep[None]
    no_gain = jnp.zeros((16, D), jnp.float32)
    if direct:
        extras = jnp.stack(
            [head_small[:, k : k + HEAD_WIDTH] for k in range(0, head_small.shape[1], HEAD_WIDTH)]
        )
        decoder_back, back_decoder, gain_grad, _, tall = layer_backward(
            1, gains, trunk[5:9], select, mask, back_top, no_gain, kept,
            head_pairs, extras, (HW, HEAD_WIDTH, (r1, HEAD_WIDTH), nz), 4,
        )
        tall = tall.transpose(1, 0, 2).reshape(r1, -1)
        own = {name: name for name in BACK_NAMES}
        trunk_pairs = layer_pairs(1, kept, decoder_back) + layer_pairs(0, kept, own)
        *_, wide = layer_backward(
            0, gains, trunk[1:5], select, mask, back_decoder, gain_grad, kept,
            trunk_pairs, None, (D, TRUNK_WIDTH, (2 * r0, TRUNK_WIDTH // 2), nz), 5,
        )
        wide = wide.transpose(1, 0, 2).reshape(r0, -1)
    else:
        tall = jnp.concatenate(
            [scatter_sum(dot_left(x, y)) for x, y in head_pairs]
            + [scatter_sum(head_small.astype(jnp.float32))],
            1,
        )
        decoder_back, back_decoder, gain_grad, _ = layer_backward(
            1, gains, trunk[5:9], select, mask, back_top, no_gain, kept
        )
        encoder_back, _, _, trunk_small = layer_backward(
            0, gains, trunk[1:5], select, mask, back_decoder, gain_grad, kept
        )
        whole = lambda entry: entry[0][entry[1]] if isinstance(entry, tuple) else entry
        wide = jnp.concatenate(
            [
                scatter_sum(dot_left(whole(x), whole(y)))
                for x, y in layer_pairs(1, kept, decoder_back) + layer_pairs(0, kept, encoder_back)
            ]
            + [scatter_sum(trunk_small[0].astype(jnp.float32))],
            1,
        )
    block_columns, head_columns = sum(TRUNK_PARTS), sum(HEAD_PARTS)
    block_grad = jnp.stack([wide[:, l * block_columns : (l + 1) * block_columns] for l in (1, 0)])
    rest = wide[:, 2 * block_columns :]
    entry_grad = rest[:, : 2 * SEQ + CH].T
    gain_grad = rest[:, 2 * SEQ + CH : 2 * SEQ + CH + 4].T.reshape(2, 2, r0)
    head_grad = jnp.stack([tall[:, b * head_columns : (b + 1) * head_columns] for b in range(HB)])
    rest = tall[:, HB * head_columns :]
    shared = rest[:, 3 * HW :]
    edge_grad = jnp.concatenate(
        [
            shared[:, :D], shared[:, D + FREQ : D + FREQ + 2 * CH], shared[:, D : D + FREQ],
            rest[:, : 3 * HW],
        ],
        1,
    ).T
    bias_grad = (
        shared[:, D + FREQ + 2 * CH : D + FREQ + 2 * CH + 5 * (HB + 1)].T.reshape(HB + 1, 5 * r1)
    )
    squares = jnp.sum(wide * wide) + jnp.sum(tall * tall)
    late = exchange(jnp.stack([loss_local, squares]), dp_count, nz, 6)
    loss_sum = jnp.sum(late[:, 0])
    grad_norm = jnp.sqrt(jnp.sum(late[:, 1]))
    factor = CLIP_NORM / jnp.maximum(grad_norm, CLIP_NORM)
    new = [
        adamw(block_weights, first_blocks, second_blocks, block_grad, factor, LEARN_RATE),
        adamw(block_gains, first_gains, second_gains, gain_grad, factor, GAIN_RATE),
        adamw(entry_table, first_entry, second_entry, entry_grad, factor, LEARN_RATE),
        adamw(head_weights, first_head, second_head, head_grad, factor, LEARN_RATE),
        adamw(head_biases, first_biases, second_biases, bias_grad, factor, LEARN_RATE),
        adamw(head_edges, first_edges, second_edges, edge_grad, factor, LEARN_RATE),
    ]
    return tuple(new[i][k] for k in range(3) for i in range(6)) + (loss_sum, weight_total, grad_norm)


def solution(mesh):
    rows = [P(AXES, None, None), P(AXES, None), P(AXES), P(AXES, None), P(AXES, None), P(AXES, None)]
    state = [
        P(None, AXES, None), P(None, None, AXES), P(None, AXES),
        P(None, AXES, None), P(None, AXES), P(None, AXES),
    ]
    return jax.shard_map(
        functools.partial(on_device, dict(mesh.shape)),
        mesh=mesh,
        in_specs=tuple(rows + state * 3),
        out_specs=tuple(state * 3 + [P(), P(), P()]),
        check_vma=False,
    )
```
